32 devices in a mesh: pipe: 2 (over core), dp: 4 (over z), mp: 4 (over y, x).
Axes of the slice: x: 2, y: 2, z: 4, core: 2. Of those that a mesh axis runs over, the one named last changes fastest.
Arguments:
- inputs: bfloat16 [8, 576, 1024], P('dp', 'mp'), may hold values from -6 to 6
- cotangent: bfloat16 [8, 576, 1024], P('dp', 'mp'), may hold values from -6 to 6
- highres: bfloat16 [8, 48, 48, 1536], P('dp', 'pipe', None, 'mp')
- resolution: int32 [8], P('dp'), may hold values from 768 to 1536, as said below
- assign: int32 [4, 2], P('dp'), may hold values from 0 to 1, each once within a row
- norm_gain: float32 [2, 2, 1024], P('pipe'), may hold values from 0.5 to 1.5
- norm_bias: float32 [2, 2, 1024], P('pipe'), may hold values from -2 to 2
- qkv_weight: bfloat16 [2, 1024, 3, 1024], P('pipe', None, None, 'mp'), may hold values from -0.1875 to 0.1875
- out_weight: bfloat16 [2, 1024, 1024], P('pipe', 'mp'), may hold values from -0.375 to 0.375
- up_weight: bfloat16 [2, 1024, 4096], P('pipe', None, 'mp'), may hold values from -0.1875 to 0.1875
- down_weight: bfloat16 [2, 4096, 1024], P('pipe', 'mp'), may hold values from -0.09375 to 0.09375
- conv_weight: bfloat16 [2, 1536, 1024], P('pipe', 'mp'), may hold values from -0.15625 to 0.15625
- depth_weight: float32 [2, 9, 1024], P('pipe'), may hold values from -2 to 2
- depth_bias: float32 [2, 1024], P('pipe'), may hold values from -3 to 3
- gate_in: bfloat16 [2, 256, 1024], P('pipe', 'mp'), may hold values from -0.1875 to 0.1875
- gate_out: bfloat16 [2, 256, 1024], P('pipe', 'mp'), may hold values from -0.375 to 0.375
Outputs:
- layer_out: bfloat16 [2, 8, 576, 1024], P('pipe', 'dp', 'mp')
- input_grad: bfloat16 [2, 8, 576, 1024], P('pipe', 'dp', 'mp')
- norm_gain_grad: float32 [2, 2, 1024], P('pipe')
- norm_bias_grad: float32 [2, 2, 1024], P('pipe')
- qkv_grad: float32 [2, 1024, 3, 1024], P('pipe', 'dp', None, 'mp')
- out_grad: float32 [2, 1024, 1024], P('pipe', 'mp', 'dp')
- up_grad: float32 [2, 1024, 4096], P('pipe', 'dp', 'mp')
- down_grad: float32 [2, 4096, 1024], P('pipe', 'mp', 'dp')
- conv_grad: float32 [2, 1536, 1024], P('pipe', 'mp', 'dp')
- depth_weight_grad: float32 [2, 9, 1024], P('pipe')
- depth_bias_grad: float32 [2, 1024], P('pipe')
- gate_in_grad: float32 [2, 256, 1024], P('pipe', 'mp')
- gate_out_grad: float32 [2, 256, 1024], P('pipe', 'mp')
The draws below stay inside these ranges and needn't reach their ends.
Inputs may be any that keep to these rules, and one draw needn't show every extreme that they name: Each image's resolution is 768, 1024 or 1536, and its feature map fills the first resolution * 24 // 768 cells of each side. `assign`: each row is an ordering of its index's 2 images.
All inputs are finite; a program needn't handle non-finite values.
Results may differ from the reference program's by a relative error of at most 0.018.
Values may be sent and summed in bfloat16 or wider, within the bound.
A program may use at most 320 MiB of HBM per device.

```python
import jax
import jax.numpy as jnp
from jax import lax

D = 1024
HEADS = 16
FF = 4096
CH = 1536
GH = 256
GRID = 24
MICRO = 2
HDIM = 64
TOKS = 576
SIDE = 48
IMAGES = 8
N_DP = 4


def draw_highres(key, part):
    key_noise, key_shift = jax.random.split(jax.random.fold_in(key, 11))
    noise = jax.random.normal(key_noise, (IMAGES, SIDE, SIDE, CH), jnp.float32)
    shift = 1.5 * jax.random.normal(key_shift, (IMAGES, 1, 1, CH), jnp.float32)
    return (noise + shift).astype(jnp.bfloat16)


def draw_resolution(key, part):
    picks = jax.random.randint(jax.random.fold_in(key, 23), (IMAGES,), 0, 3)
    picks = picks.at[0].set(2).at[1].set(0)
    return jnp.where(picks == 0, 768, jnp.where(picks == 1, 1024, 1536)).astype(jnp.int32)


def block_scale(stream_key, extent, cuts, low, top_value):
    factor_of, own = 1.0, jax.random.fold_in(stream_key, 6)
    for dim, shards_of in cuts:
        steps = jnp.exp(jax.random.uniform(jax.random.fold_in(own, dim), (shards_of,), jnp.float32, low / len(cuts), top_value / len(cuts)))
        factor_of = factor_of * jnp.repeat(steps, extent[dim] // shards_of).reshape([-1 if axis == dim else 1 for axis in range(len(extent))])
    return factor_of


def bell_draw(stream_key, dims, deviation, reach, pieces=(), kind=jnp.bfloat16):
    factor_of = block_scale(stream_key, dims, pieces, -0.22, 0.18) if pieces else 1.0
    entries = jax.random.normal(stream_key, dims, jnp.float32) * deviation * factor_of
    return jnp.minimum(jnp.maximum(entries, -reach), reach).astype(kind)


def setup_inputs(seed: int = 0) -> dict:
    splits = jax.random.split(jax.random.key(seed), 17)
    inputs = bell_draw(splits[0], (IMAGES, TOKS, D), 1.0, 6.0, ((0, 4), (1, 4)))
    cotangent = bell_draw(splits[1], (IMAGES, TOKS, D), 1.0, 6.0, ((0, 4), (1, 4)))
    highres = draw_highres(jax.random.fold_in(splits[16], 71), 0)
    resolution = draw_resolution(jax.random.fold_in(splits[16], 71), 0)
    assign = jax.vmap(lambda own: jax.random.permutation(own, MICRO))(jax.random.split(splits[4], N_DP)).reshape((N_DP, MICRO)).astype(jnp.int32)
    norm_gain = jnp.clip(1.0 + 0.1 * jax.random.normal(splits[5], (2, 2, D), jnp.float32), 0.5, 1.5)
    norm_bias = bell_draw(splits[6], (2, 2, D), 0.3, 2.0, ((0, 2),), jnp.float32)
    qkv_weight = bell_draw(splits[7], (2, D, 3, D), D ** -0.5, 0.1875, ((0, 2), (3, 4)))
    out_weight = bell_draw(splits[8], (2, D, D), (D // 4) ** -0.5, 0.375, ((0, 2), (1, 4)))
    up_weight = bell_draw(splits[9], (2, D, FF), D ** -0.5, 0.1875, ((0, 2), (2, 4)))
    down_weight = bell_draw(splits[10], (2, FF, D), FF ** -0.5, 0.09375, ((0, 2), (1, 4)))
    conv_weight = bell_draw(splits[11], (2, CH, D), CH ** -0.5, 0.15625, ((0, 2), (1, 4)))
    depth_weight = bell_draw(splits[12], (2, 9, D), 9 ** -0.5, 2.0, ((0, 2),), jnp.float32)
    depth_bias = bell_draw(splits[13], (2, D), 0.5, 3.0, ((0, 2),), jnp.float32)
    gate_in = bell_draw(splits[14], (2, GH, D), D ** -0.5, 0.1875, ((0, 2), (1, 4)))
    gate_out = bell_draw(splits[15], (2, GH, D), GH ** -0.5, 0.375, ((0, 2), (1, 4)))
    return {"inputs": inputs, "cotangent": cotangent, "highres": highres, "resolution": resolution, "assign": assign, "norm_gain": norm_gain, "norm_bias": norm_bias, "qkv_weight": qkv_weight, "out_weight": out_weight, "up_weight": up_weight, "down_weight": down_weight, "conv_weight": conv_weight, "depth_weight": depth_weight, "depth_bias": depth_bias, "gate_in": gate_in, "gate_out": gate_out}


norm_eps = 1e-06
precise = lax.Precision.HIGHEST

@jax.custom_vjp
def low(v):
    return lax.optimization_barrier(v.astype(jnp.bfloat16)).astype(jnp.float32)

@jax.custom_vjp
def low_back(v):
    return v

def low_keep(v):
    return (low(v), None)

def low_pass(kept, grad):
    return (grad,)

def back_keep(v):
    return (v, None)

def back_low(kept, grad):
    return (low(grad),)
low.defvjp(low_keep, low_pass)
low_back.defvjp(back_keep, back_low)

def norm_rows(values, gain, shift):
    center = values - lax.optimization_barrier(jnp.mean(values, axis=-1, keepdims=True))
    spread = lax.optimization_barrier(jnp.mean(center * center, axis=-1, keepdims=True))
    return center * lax.rsqrt(spread + norm_eps) * gain + shift

def depthwise(field, kernel):
    grid_map = field.reshape(GRID, GRID, field.shape[1])
    padded = jnp.pad(grid_map, ((1, 1), (1, 1), (0, 0)))
    total = jnp.zeros_like(grid_map)
    for offset in range(9):
        row_shift = offset // 3
        col_shift = offset % 3
        total = total + kernel[offset] * padded[row_shift:row_shift + GRID, col_shift:col_shift + GRID]
    return total.reshape(field.shape)

def pool_matrix(side):
    rows_index = jnp.arange(GRID, dtype=jnp.int32)[:, None]
    cols_index = jnp.arange(SIDE, dtype=jnp.int32)[None, :]
    lower = rows_index * side // GRID
    upper = ((rows_index + 1) * side + GRID - 1) // GRID
    inside = (cols_index >= lower) & (cols_index < upper)
    width = (upper - lower).astype(jnp.float32)
    return jnp.where(inside, 1.0 / width, 0.0).astype(jnp.float32)

def pool_image(feature, pixels):
    matrix = pool_matrix(pixels * GRID // 768)
    first = jnp.einsum('ia,abc->ibc', matrix, feature, precision=precise)
    second = jnp.einsum('jb,ibc->ijc', matrix, first, precision=precise)
    return second.reshape(GRID * GRID, feature.shape[2])

def gate_local(weight_in, weight_out, mean_vec):
    inner = jnp.dot(weight_in, mean_vec, precision=precise)
    return jnp.dot(jax.nn.gelu(inner, approximate=False), weight_out, precision=precise)

def attend_image(qkv_rows):
    split = qkv_rows.reshape(TOKS, 3, HEADS, HDIM)
    query, key, value = (split[:, 0], split[:, 1], split[:, 2])
    scores = low_back(jnp.einsum('qhd,khd->hqk', query, key, precision=precise) * HDIM ** (-0.5))
    probs = low(jax.nn.softmax(scores, axis=-1))
    mixed = jnp.einsum('hqk,khd->qhd', probs, value, precision=precise)
    return mixed.reshape(TOKS, D)

def layer(weights, which, values, pooled):
    gain, shift, weight_qkv, weight_out, weight_up, weight_down, weight_conv, kernel, kernel_bias, weight_gate_in, weight_gate_out = [w[which] for w in weights]
    first = low(norm_rows(values, gain[0], shift[0]))
    qkv = low_back(low(jnp.einsum('btd,dcf->btcf', first, weight_qkv, precision=precise)))
    mixed = lax.map(jax.checkpoint(attend_image), qkv.reshape(qkv.shape[0], TOKS, 3 * D))
    mixed = low_back(low(mixed))
    attn_out = low_back(jnp.einsum('btf,fd->btd', mixed, weight_out, precision=precise))
    after = values + attn_out
    second = low(norm_rows(after, gain[1], shift[1]))
    hidden_pre = low_back(jnp.einsum('btd,df->btf', second, weight_up, precision=precise))
    hidden = low(jax.nn.gelu(hidden_pre, approximate=False))
    mlp_out = jnp.einsum('btf,fd->btd', hidden, weight_down, precision=precise)
    conv = low_back(jnp.einsum('btc,cd->btd', pooled, weight_conv, precision=precise))
    adapter = jax.vmap(depthwise, in_axes=(0, None))(conv, kernel) + kernel_bias
    mean_vec = lax.optimization_barrier(jnp.mean(adapter, axis=(0, 1)))
    gate = jnp.tanh(gate_local(weight_gate_in, weight_gate_out, mean_vec))
    return after + mlp_out + gate * adapter

def reference(inputs, cotangent, highres, resolution, assign, norm_gain, norm_bias, qkv_weight, out_weight, up_weight, down_weight, conv_weight, depth_weight, depth_bias, gate_in, gate_out):
    pooled = lax.map(lambda arrays: pool_image(arrays[0].astype(jnp.float32), arrays[1]), (highres, resolution))
    pooled = low(pooled)
    weights = tuple((w.astype(jnp.float32) for w in (norm_gain, norm_bias, qkv_weight, out_weight, up_weight, down_weight, conv_weight, depth_weight, depth_bias, gate_in, gate_out)))
    zero_in = jnp.zeros(inputs.shape, jnp.float32)
    checked = jax.checkpoint(layer, static_argnums=(1,))

    def whole(weights, first_in, second_in):
        final_all = jnp.zeros(first_in.shape, jnp.float32)
        middle_all = jnp.zeros(first_in.shape, jnp.float32)
        for micro_index in range(MICRO):
            picks = (jnp.arange(N_DP, dtype=jnp.int32) * MICRO + assign[:, micro_index]).astype(jnp.int32)
            images_pool = pooled[picks]
            middle = checked(weights, 0, first_in[picks], images_pool)
            rounded = low(middle)
            sent = low_back(rounded + second_in[picks])
            final = checked(weights, 1, sent, images_pool)
            final_all = final_all.at[picks].set(final)
            middle_all = middle_all.at[picks].set(rounded)
        return (final_all, middle_all)
    final_all, pull, middle_all = jax.vjp(whole, weights, inputs.astype(jnp.float32), zero_in, has_aux=True)
    grads, grad_first, grad_second = pull(cotangent.astype(jnp.float32))
    layer_out = jnp.stack([middle_all, final_all]).astype(jnp.bfloat16)
    input_grad = jnp.stack([grad_first, grad_second]).astype(jnp.bfloat16)
    return (layer_out, input_grad, grads[0], grads[1], grads[2], grads[3], grads[4], grads[5], grads[6], grads[7], grads[8], grads[9], grads[10])
```

```python
import functools

import jax
import jax.numpy as jnp
from jax import lax
from jax.experimental import pallas as pl
from jax.experimental.pallas import tpu as pltpu
from jax.sharding import PartitionSpec as P

GRID = 24
HEAD = 64
EPS = 1e-06
TILE = 256
VMEM_BYTES = 60 * 1024 * 1024
MESH = pl.DeviceIdType.MESH
F32 = jnp.float32
BF16 = jnp.bfloat16
SWAP = [(0, 1), (1, 0)]


def mm(a, b, ca=1, cb=0):
    return lax.dot_general(a, b, (((ca,), (cb,)), ((), ())), preferred_element_type=F32)


def tile_of(index, width=TILE):
    return pl.ds(pl.multiple_of(index * width, width), width)


def place():
    me = lax.axis_index("mp")
    col, line = lax.rem(me, 2), lax.div(me, 2)
    return me, line * 2 + 1 - col, (1 - line) * 2 + col, (1 - line) * 2 + 1 - col


def greet(peers):
    barrier = pltpu.get_barrier_semaphore()
    for peer in peers:
        pl.semaphore_signal(barrier, inc=1, device_id=peer, device_id_type=MESH)
    pl.semaphore_wait(barrier, len(peers))


def push(src, dst, send, recv, slot, peer):
    copy = pltpu.make_async_remote_copy(
        src_ref=src,
        dst_ref=dst,
        send_sem=send.at[slot],
        recv_sem=recv.at[slot],
        device_id=peer,
        device_id_type=MESH,
    )
    copy.start()
    return copy


class Gather:
    def __init__(self, buf, send, recv, spot, rows):
        me, xn, yn, dn = spot
        self.buf, self.send, self.recv, self.spot, self.rows = buf, send, recv, spot, rows
        own = buf.at[rows(me)]
        self.near = [
            push(own, own, send, recv, 0, {"mp": xn}),
            push(own, own, send, recv, 1, {"mp": yn}),
        ]

    def forward(self):
        me, xn, yn, dn = self.spot
        half = self.buf.shape[1] // 2
        self.near[0].wait_recv()
        left = self.buf.at[self.rows(xn), pl.ds(0, half)]
        first = push(left, left, self.send, self.recv, 2, {"mp": yn})
        self.near[1].wait_recv()
        right = self.buf.at[self.rows(yn), pl.ds(half, half)]
        self.far = [first, push(right, right, self.send, self.recv, 3, {"mp": xn})]

    def finish(self):
        for copy in self.far:
            copy.wait_recv()

    def drain(self):
        for copy in self.near + self.far:
            copy.wait_send()


class Scatter:
    def __init__(self, bufs, send, recv, spot):
        self.px, self.py, self.pd, self.via, self.rx, self.ry = bufs
        self.send, self.recv, self.spot = send, recv, spot
        width = self.px.shape[1]
        self.low, self.high = pl.ds(0, width // 2), pl.ds(width // 2, width // 2)

    def far(self):
        me, xn, yn, dn = self.spot
        self.far_copies = [
            push(self.pd.at[:, self.low], self.via.at[0], self.send, self.recv, 0, {"mp": xn}),
            push(self.pd.at[:, self.high], self.via.at[1], self.send, self.recv, 1, {"mp": yn}),
        ]

    def near_x(self):
        self.x_copy = push(
            self.px.at[:, self.low], self.rx.at[:, self.low], self.send, self.recv, 2, {"mp": self.spot[1]}
        )

    def near_y(self):
        self.y_copy = push(
            self.py.at[:, self.high], self.ry.at[:, self.high], self.send, self.recv, 3, {"mp": self.spot[2]}
        )

    def relay(self):
        me, xn, yn, dn = self.spot
        self.far_copies[0].wait_recv()
        self.py[:, self.low] = (self.py[:, self.low].astype(F32) + self.via[0].astype(F32)).astype(BF16)
        first = push(self.py.at[:, self.low], self.ry.at[:, self.low], self.send, self.recv, 4, {"mp": yn})
        self.far_copies[1].wait_recv()
        self.px[:, self.high] = (self.px[:, self.high].astype(F32) + self.via[1].astype(F32)).astype(BF16)
        second = push(self.px.at[:, self.high], self.rx.at[:, self.high], self.send, self.recv, 5, {"mp": xn})
        self.last_copies = [first, second]

    def total(self, own):
        for copy in [self.x_copy, self.y_copy] + self.last_copies:
            copy.wait_recv()
        return own + self.rx[...].astype(F32) + self.ry[...].astype(F32)

    def drain(self):
        for copy in self.far_copies + [self.x_copy, self.y_copy] + self.last_copies:
            copy.wait_send()


def scatter_scratch(rows, width):
    return [
        pltpu.VMEM((rows, width), BF16),
        pltpu.VMEM((rows, width), BF16),
        pltpu.VMEM((rows, width), BF16),
        pltpu.VMEM((2, rows, width // 2), BF16),
        pltpu.VMEM((rows, width), BF16),
        pltpu.VMEM((rows, width), BF16),
    ]


def norm_rows(values, gain, shift):
    center = values - jnp.mean(values, axis=-1, keepdims=True)
    spread = jnp.mean(center * center, axis=-1, keepdims=True)
    return center * lax.rsqrt(spread + EPS) * gain + shift


def norm_back(values, gain, grad):
    center = values - jnp.mean(values, axis=-1, keepdims=True)
    scale = lax.rsqrt(jnp.mean(center * center, axis=-1, keepdims=True) + EPS)
    unit = center * scale
    scaled = grad * gain
    mean_one = jnp.mean(scaled, axis=-1, keepdims=True)
    mean_two = jnp.mean(scaled * unit, axis=-1, keepdims=True)
    back = scale * (scaled - mean_one - unit * mean_two)
    return back, jnp.sum(grad * unit, axis=0, keepdims=True), jnp.sum(grad, axis=0, keepdims=True)


def gelu_parts(values):
    below = 0.5 * (1.0 + lax.erf(values * 0.7071067811865476))
    bell = jnp.exp(-0.5 * values * values) * 0.3989422804014327
    return values * below, below + values * bell


def load_layer(layer, own, got, held, sems):
    mine = lax.axis_index("pipe") == layer
    for i in range(len(held)):

        @pl.when(mine)
        def _():
            pltpu.make_async_copy(own[i], held[i], sems.at[i]).start()

        @pl.when(jnp.logical_not(mine))
        def _():
            pltpu.make_async_copy(got[i], held[i], sems.at[i]).start()

    return [pltpu.make_async_copy(own[i], held[i], sems.at[i]) for i in range(len(held))]


def forward_kernel(layer, *refs):
    x_ref, nrm, depth_hbm = refs[:3]
    own_w, got_w = refs[3:7], refs[7:11]
    out_ref, after_ref = refs[11:13]
    saved_hbm = refs[13:20]
    first, qkv, probs, mixed, second, hidden, slope = refs[20:27]
    depth, wq, wo, wu, wd, own = refs[27:33]
    bufs_one, bufs_two = refs[33:39], refs[39:45]
    load_sem, save_sem, ag_send, ag_recv, rs_send, rs_recv = refs[45:]

    size = x_ref.shape[0]
    width = x_ref.shape[1]
    tokens = first.shape[0]
    share = mixed.shape[1]
    spot = place()
    me, xn, yn, dn = spot

    def rows(i):
        return pl.ds(pl.multiple_of(i * size, 16), size)

    loads = load_layer(layer, own_w, got_w, (wq, wo, wu, wd), load_sem)
    depth_load = pltpu.make_async_copy(depth_hbm.at[layer], depth, load_sem.at[4])
    depth_load.start()
    saves = []

    def save(index, ref):
        copy = pltpu.make_async_copy(ref, saved_hbm[index], save_sem.at[index])
        copy.start()
        saves.append(copy)

    greet([{"mp": xn}, {"mp": yn}, {"mp": dn}])

    x = x_ref[...].astype(F32)
    first[rows(me), :] = norm_rows(x, nrm[0:1, :], nrm[1:2, :]).astype(BF16)
    gather = Gather(first, ag_send.at[0], ag_recv.at[0], spot, rows)
    loads[0].wait()

    def project(i):
        @pl.loop(0, qkv.shape[1] // TILE)
        def _(t):
            qkv[rows(i), tile_of(t)] = mm(first[rows(i), :], wq[:, tile_of(t)]).astype(BF16)

    project(me)
    gather.forward()
    project(xn)
    project(yn)
    gather.finish()
    project(dn)
    gather.drain()
    save(0, first)
    save(1, qkv)

    @pl.loop(0, tokens // size)
    def _(t):
        parts = []
        for h in range(share // HEAD):
            query = qkv[rows(t), h * HEAD : (h + 1) * HEAD]
            key = qkv[:, share + h * HEAD : share + (h + 1) * HEAD]
            value = qkv[:, 2 * share + h * HEAD : 2 * share + (h + 1) * HEAD]
            scores = mm(query, key, 1, 1) * (HEAD**-0.5)
            raised = jnp.exp(scores - jnp.max(scores, axis=-1, keepdims=True))
            weights = (raised / jnp.sum(raised, axis=-1, keepdims=True)).astype(BF16)
            probs[h, rows(t), :] = weights
            parts.append(mm(weights, value))
        mixed[rows(t), :] = jnp.concatenate(parts, axis=1).astype(BF16)

    save(2, probs)
    save(3, mixed)
    loads[1].wait()

    def out_part(i, dest):
        @pl.loop(0, width // TILE)
        def _(t):
            dest[:, tile_of(t)] = mm(mixed[rows(i), :], wo[:, tile_of(t)]).astype(dest.dtype)

    scatter = Scatter(bufs_one, rs_send.at[0], rs_recv.at[0], spot)
    out_part(dn, scatter.pd)
    scatter.far()
    out_part(xn, scatter.px)
    scatter.near_x()
    out_part(yn, scatter.py)
    scatter.near_y()
    out_part(me, own)
    scatter.relay()
    after = x + scatter.total(own[...])
    after_ref[...] = after
    second[rows(me), :] = norm_rows(after, nrm[2:3, :], nrm[3:4, :]).astype(BF16)
    gather = Gather(second, ag_send.at[1], ag_recv.at[1], spot, rows)
    scatter.drain()
    loads[2].wait()
    loads[3].wait()
    depth_load.wait()

    def feed(i, dest):
        @pl.loop(0, hidden.shape[1] // TILE)
        def _(t):
            value, grad = gelu_parts(mm(second[rows(i), :], wu[:, tile_of(t)]))
            hidden[rows(i), tile_of(t)] = value.astype(BF16)
            slope[rows(i), tile_of(t)] = grad.astype(BF16)

        @pl.loop(0, width // TILE)
        def _(t):
            part = mm(hidden[rows(i), :], wd[:, tile_of(t)])
            part = part + nrm[4:5, tile_of(t)] * depth[rows(i), tile_of(t)].astype(F32)
            dest[:, tile_of(t)] = part.astype(dest.dtype)

    scatter = Scatter(bufs_two, rs_send.at[1], rs_recv.at[1], spot)
    feed(me, own)
    gather.forward()
    feed(xn, scatter.px)
    scatter.near_x()
    feed(yn, scatter.py)
    scatter.near_y()
    gather.finish()
    save(4, second)
    feed(dn, scatter.pd)
    scatter.far()
    save(5, hidden)
    save(6, slope)
    scatter.relay()
    out_ref[...] = (after_ref[...] + scatter.total(own[...]) + nrm[5:6, :]).astype(BF16)
    gather.drain()
    scatter.drain()
    for copy in saves:
        copy.wait()


def forward_layer(layer, ident, x, nrm, depth, own, got):
    size, width = x.shape
    tokens = depth.shape[1]
    share, ff = own[1].shape[0], own[2].shape[1]
    heads = share // HEAD
    vmem, anywhere = pl.BlockSpec(memory_space=pltpu.VMEM), pl.BlockSpec(memory_space=pl.ANY)
    saved = [
        ((tokens, width), BF16),
        ((tokens, 3 * share), BF16),
        ((heads, tokens, tokens), BF16),
        ((tokens, share), BF16),
        ((tokens, width), BF16),
        ((tokens, ff), BF16),
        ((tokens, ff), BF16),
    ]
    flops = 2 * tokens * width * (4 * share + 2 * ff) + 4 * heads * tokens * tokens * HEAD
    outs = pl.pallas_call(
        functools.partial(forward_kernel, layer),
        out_shape=[jax.ShapeDtypeStruct((size, width), BF16), jax.ShapeDtypeStruct((size, width), F32)]
        + [jax.ShapeDtypeStruct(*s) for s in saved],
        in_specs=[vmem, vmem] + [anywhere] * 9,
        out_specs=[vmem, vmem] + [anywhere] * 7,
        scratch_shapes=[pltpu.VMEM(*s) for s in saved]
        + [
            pltpu.VMEM((tokens, width), BF16),
            pltpu.VMEM(own[0].shape, BF16),
            pltpu.VMEM(own[1].shape, BF16),
            pltpu.VMEM(own[2].shape, BF16),
            pltpu.VMEM(own[3].shape, BF16),
            pltpu.VMEM((size, width), F32),
        ]
        + scatter_scratch(size, width)
        + scatter_scratch(size, width)
        + [
            pltpu.SemaphoreType.DMA((5,)),
            pltpu.SemaphoreType.DMA((7,)),
            pltpu.SemaphoreType.DMA((2, 4)),
            pltpu.SemaphoreType.DMA((2, 4)),
            pltpu.SemaphoreType.DMA((2, 6)),
            pltpu.SemaphoreType.DMA((2, 6)),
        ],
        compiler_params=pltpu.CompilerParams(
            collective_id=ident, has_side_effects=True, vmem_limit_bytes=VMEM_BYTES
        ),
        cost_estimate=pl.CostEstimate(flops=flops * 4, bytes_accessed=30_000_000, transcendentals=0),
        name="layer_forward",
    )(x, nrm, depth, *own, *got)
    return outs[0], outs[1], outs[2:]


def backward_kernel(layer, *refs):
    dy_ref, x_ref, after_ref, nrm = refs[:4]
    saved_hbm, depth_hbm = refs[4:11], refs[11]
    own_w, got_w = refs[12:16], refs[16:20]
    dx_ref, small_ref, dyf_hbm, grads_hbm = refs[20:24]
    first, qkv, probs, mixed, second, hidden, slope = refs[24:31]
    depth, wq, wo, wu, wd, own = refs[31:37]
    bufs_one, bufs_two = refs[37:43], refs[43:49]
    dyf, dhp, daf, dqkv, key_acc, value_acc, dafter, grads = refs[49:57]
    load_sem, saved_sem, save_sem, ag_send, ag_recv, rs_send, rs_recv = refs[57:]

    size, width = dy_ref.shape
    tokens = first.shape[0]
    share, ff = mixed.shape[1], hidden.shape[1]
    shards = grads.shape[0]
    part_cols = width // shards
    spot = place()
    me, xn, yn, dn = spot

    def rows(i):
        return pl.ds(pl.multiple_of(i * size, 16), size)

    loads = load_layer(layer, own_w, got_w, (wq, wo, wu, wd), load_sem)
    held = (first, qkv, probs, mixed, second, hidden, slope)
    saved = [pltpu.make_async_copy(saved_hbm[i], held[i], saved_sem.at[i]) for i in range(7)]
    for i in (6, 5, 4, 3, 2, 1, 0):
        saved[i].start()
    depth_load = pltpu.make_async_copy(depth_hbm.at[layer], depth, load_sem.at[4])
    depth_load.start()
    saves = []

    def save(index, src, dst):
        copy = pltpu.make_async_copy(src, dst, save_sem.at[index])
        copy.start()
        saves.append(copy)

    greet([{"mp": xn}, {"mp": yn}, {"mp": dn}])

    dyf[rows(me), :] = dy_ref[...]
    gather = Gather(dyf, ag_send.at[0], ag_recv.at[0], spot, rows)
    scatter = Scatter(bufs_one, rs_send.at[0], rs_recv.at[0], spot)
    small_ref[...] = jnp.zeros_like(small_ref)
    small_ref[5:6, :] = jnp.sum(dy_ref[...].astype(F32), axis=0, keepdims=True)
    key_acc[...] = jnp.zeros_like(key_acc)
    value_acc[...] = jnp.zeros_like(value_acc)
    loads[2].wait()
    loads[3].wait()
    saved[6].wait()

    def feed_back(i, dest):
        @pl.loop(0, ff // TILE)
        def _(t):
            back = mm(dyf[rows(i), :], wd[tile_of(t), :], 1, 1)
            dhp[rows(i), tile_of(t)] = (back * slope[rows(i), tile_of(t)].astype(F32)).astype(BF16)

        @pl.loop(0, width // TILE)
        def _(t):
            dest[:, tile_of(t)] = mm(dhp[rows(i), :], wu[tile_of(t), :], 1, 1).astype(dest.dtype)

    feed_back(me, own)
    gather.forward()
    feed_back(xn, scatter.px)
    scatter.near_x()
    feed_back(yn, scatter.py)
    scatter.near_y()
    gather.finish()
    feed_back(dn, scatter.pd)
    scatter.far()
    save(0, dyf, dyf_hbm)
    saved[5].wait()
    base_out, base_up, base_down = 3 * share, 3 * share + share, 3 * share + share + ff

    @pl.loop(0, ff // TILE)
    def _(t):
        grad = mm(hidden[:, tile_of(t)], dyf[...], 0, 0).astype(BF16)
        for s in range(shards):
            grads[s, pl.ds(pl.multiple_of(base_down + t * TILE, TILE), TILE), :] = grad[
                :, s * part_cols : (s + 1) * part_cols
            ]

    scatter.relay()
    saved[4].wait()

    @pl.loop(0, shards)
    def _(s):
        grad = mm(second[:, tile_of(s, part_cols)], dhp[...], 0, 0).astype(BF16)
        for t in range(ff // part_cols):
            grads[s, base_up + t * part_cols : base_up + (t + 1) * part_cols, :] = grad[
                :, t * part_cols : (t + 1) * part_cols
            ]

    depth_load.wait()
    for i in range(tokens // size):
        block = slice(i * size, (i + 1) * size)
        small_ref[4:5, :] += jnp.sum(
            dyf[block, :].astype(F32) * depth[block, :].astype(F32), axis=0, keepdims=True
        )
    back, gain_grad, bias_grad = norm_back(after_ref[...], nrm[2:3, :], scatter.total(own[...]))
    small_ref[2:3, :] = gain_grad
    small_ref[3:4, :] = bias_grad
    dafter[...] = dy_ref[...].astype(F32) + back
    daf[rows(me), :] = dafter[...].astype(BF16)
    gather.drain()
    scatter.drain()

    gather = Gather(daf, ag_send.at[1], ag_recv.at[1], spot, rows)
    scatter = Scatter(bufs_two, rs_send.at[1], rs_recv.at[1], spot)
    loads[1].wait()
    saved[1].wait()
    saved[2].wait()

    def attend_back(i):
        grad_mixed = mm(daf[rows(i), :], wo[...], 1, 1).astype(BF16)
        parts = []
        for h in range(share // HEAD):
            lanes = slice(h * HEAD, (h + 1) * HEAD)
            query = qkv[rows(i), lanes]
            key = qkv[:, share + h * HEAD : share + (h + 1) * HEAD]
            value = qkv[:, 2 * share + h * HEAD : 2 * share + (h + 1) * HEAD]
            weights = probs[h, rows(i), :]
            grad_probs = mm(grad_mixed[:, lanes], value, 1, 1)
            exact = weights.astype(F32)
            delta = jnp.sum(exact * grad_probs, axis=-1, keepdims=True)
            grad_scores = (exact * (grad_probs - delta)).astype(BF16)
            parts.append(mm(grad_scores, key))
            key_acc[lanes, :tokens] += mm(query, grad_scores, 0, 0)
            value_acc[lanes, :tokens] += mm(grad_mixed[:, lanes], weights, 0, 0)
        dqkv[rows(i), :share] = (jnp.concatenate(parts, axis=1) * (HEAD**-0.5)).astype(BF16)

    attend_back(me)
    gather.forward()
    attend_back(xn)
    attend_back(yn)
    gather.finish()
    attend_back(dn)
    dqkv[:, share : 2 * share] = (key_acc[...].T[:tokens] * (HEAD**-0.5)).astype(BF16)
    dqkv[:, 2 * share :] = value_acc[...].T[:tokens].astype(BF16)
    loads[0].wait()

    def first_back(i, dest):
        @pl.loop(0, width // TILE)
        def _(t):
            dest[:, tile_of(t)] = mm(dqkv[rows(i), :], wq[tile_of(t), :], 1, 1).astype(dest.dtype)

    first_back(dn, scatter.pd)
    scatter.far()
    first_back(xn, scatter.px)
    scatter.near_x()
    first_back(yn, scatter.py)
    scatter.near_y()
    first_back(me, own)
    saved[3].wait()
    grad = mm(mixed[...], daf[...], 0, 0).astype(BF16)
    for s in range(shards):
        grads[s, base_out : base_out + share, :] = grad[:, s * part_cols : (s + 1) * part_cols]
    scatter.relay()
    saved[0].wait()

    @pl.loop(0, shards)
    def _(s):
        grad = mm(first[:, tile_of(s, part_cols)], dqkv[...], 0, 0).astype(BF16)
        for t in range(3 * share // part_cols):
            grads[s, t * part_cols : (t + 1) * part_cols, :] = grad[:, t * part_cols : (t + 1) * part_cols]

    save(1, grads, grads_hbm)
    back, gain_grad, bias_grad = norm_back(
        x_ref[...].astype(F32), nrm[0:1, :], scatter.total(own[...])
    )
    small_ref[0:1, :] = gain_grad
    small_ref[1:2, :] = bias_grad
    dx_ref[...] = (dafter[...] + back).astype(BF16)
    gather.drain()
    scatter.drain()
    for copy in saves:
        copy.wait()


def backward_layer(layer, ident, shards, dy, x, after, nrm, saved, depth, own, got):
    size, width = dy.shape
    tokens = depth.shape[1]
    share, ff = own[1].shape[0], own[2].shape[1]
    heads = share // HEAD
    vmem, anywhere = pl.BlockSpec(memory_space=pltpu.VMEM), pl.BlockSpec(memory_space=pl.ANY)
    held = [pltpu.VMEM(s.shape, s.dtype) for s in saved]
    grads_shape = (shards, 4 * share + 2 * ff, width // shards)
    lanes = -(-tokens // 128) * 128
    flops = 4 * tokens * width * (4 * share + 2 * ff) + 8 * heads * tokens * tokens * HEAD
    return pl.pallas_call(
        functools.partial(backward_kernel, layer),
        out_shape=[
            jax.ShapeDtypeStruct((size, width), BF16),
            jax.ShapeDtypeStruct((8, width), F32),
            jax.ShapeDtypeStruct((tokens, width), BF16),
            jax.ShapeDtypeStruct(grads_shape, BF16),
        ],
        in_specs=[vmem] * 4 + [anywhere] * 16,
        out_specs=[vmem, vmem, anywhere, anywhere],
        scratch_shapes=held
        + [
            pltpu.VMEM((tokens, width), BF16),
            pltpu.VMEM(own[0].shape, BF16),
            pltpu.VMEM(own[1].shape, BF16),
            pltpu.VMEM(own[2].shape, BF16),
            pltpu.VMEM(own[3].shape, BF16),
            pltpu.VMEM((size, width), F32),
        ]
        + scatter_scratch(size, width)
        + scatter_scratch(size, width)
        + [
            pltpu.VMEM((tokens, width), BF16),
            pltpu.VMEM((tokens, ff), BF16),
            pltpu.VMEM((tokens, width), BF16),
            pltpu.VMEM((tokens, 3 * share), BF16),
            pltpu.VMEM((share, lanes), F32),
            pltpu.VMEM((share, lanes), F32),
            pltpu.VMEM((size, width), F32),
            pltpu.VMEM(grads_shape, BF16),
            pltpu.SemaphoreType.DMA((5,)),
            pltpu.SemaphoreType.DMA((7,)),
            pltpu.SemaphoreType.DMA((2,)),
            pltpu.SemaphoreType.DMA((2, 4)),
            pltpu.SemaphoreType.DMA((2, 4)),
            pltpu.SemaphoreType.DMA((2, 6)),
            pltpu.SemaphoreType.DMA((2, 6)),
        ],
        compiler_params=pltpu.CompilerParams(
            collective_id=ident, has_side_effects=True, vmem_limit_bytes=VMEM_BYTES
        ),
        cost_estimate=pl.CostEstimate(flops=flops * 3, bytes_accessed=40_000_000, transcendentals=0),
        name="layer_backward",
    )(dy, x, after, nrm, *saved, depth, *own, *got)


def beside(field):
    cells, width = field.shape
    index = lax.broadcasted_iota(jnp.int32, (cells, width), 0)
    col = index - lax.shift_right_logical(index * 2731, 16) * GRID
    before = jnp.where(col >= 1, pltpu.roll(field, 1, 0), 0.0)
    behind = jnp.where(col <= GRID - 2, pltpu.roll(field, cells - 1, 0), 0.0)
    return before, field, behind


def depthwise(field, kernel):
    cells, width = field.shape
    shifted = beside(field)
    lines = [sum(kernel[3 * i + j] * shifted[j] for j in range(3)) for i in range(3)]
    none = jnp.zeros((GRID, width), F32)
    above = jnp.concatenate([none, lines[0][: cells - GRID]], axis=0)
    below = jnp.concatenate([lines[2][GRID:], none], axis=0)
    return above + lines[1] + below


def adapter_kernel(pooled_ref, weight_ref, depth_ref, conv_out, depth_out, sum_out):
    conv = mm(pooled_ref[...], weight_ref[0])
    conv_out[0] = conv.astype(BF16)
    mapped = depthwise(conv, [depth_ref[0, k : k + 1, :] for k in range(9)])
    depth_out[0] = mapped.astype(BF16)
    sum_out[0] = jnp.broadcast_to(jnp.sum(mapped, axis=0, keepdims=True), sum_out.shape[1:])


def adapter_forward(pooled, weights, depth_w):
    tokens, channels = pooled.shape
    width = weights.shape[2]
    return pl.pallas_call(
        adapter_kernel,
        grid=(2, width // TILE),
        out_shape=[
            jax.ShapeDtypeStruct((2, tokens, width), BF16),
            jax.ShapeDtypeStruct((2, tokens, width), BF16),
            jax.ShapeDtypeStruct((2, 8, width), F32),
        ],
        in_specs=[
            pl.BlockSpec((tokens, channels), lambda l, t: (0, 0)),
            pl.BlockSpec((1, channels, TILE), lambda l, t: (l, 0, t)),
            pl.BlockSpec((1, 16, TILE), lambda l, t: (l, 0, t)),
        ],
        out_specs=[
            pl.BlockSpec((1, tokens, TILE), lambda l, t: (l, 0, t)),
            pl.BlockSpec((1, tokens, TILE), lambda l, t: (l, 0, t)),
            pl.BlockSpec((1, 8, TILE), lambda l, t: (l, 0, t)),
        ],
        compiler_params=pltpu.CompilerParams(vmem_limit_bytes=VMEM_BYTES),
        name="adapter_forward",
    )(pooled, weights, depth_w)


def adapter_back_kernel(groups, pooled_ref, dy0, dy1, conv_ref, depth_ref, gate_ref, conv_grad, depth_grad):
    cells = conv_ref.shape[1]
    for layer, dy_ref in enumerate((dy0, dy1)):
        grad = gate_ref[layer : layer + 1, :] * dy_ref[...].astype(F32) + gate_ref[2 + layer : 3 + layer, :]
        shifted = beside(conv_ref[layer].astype(F32))
        sums = []
        for i in range(3):
            for j in range(3):
                if i == 0:
                    terms = shifted[j][: cells - GRID] * grad[GRID:]
                elif i == 1:
                    terms = shifted[j] * grad
                else:
                    terms = shifted[j][GRID:] * grad[: cells - GRID]
                sums.append(jnp.sum(terms, axis=0, keepdims=True))
        sums.append(jnp.sum(grad, axis=0, keepdims=True) * (1.0 / groups))
        sums.append(jnp.zeros((6, grad.shape[1]), F32))
        depth_grad[layer] = jnp.concatenate(sums, axis=0)
        back = depthwise(grad, [depth_ref[layer, 8 - k : 9 - k, :] for k in range(9)])
        conv_grad[layer, 0] = mm(pooled_ref[...], back.astype(BF16), 0, 0).astype(BF16)


def adapter_backward(groups, shards, pooled, dy0, dy1, conv, depth_w, gates):
    tokens, channels = pooled.shape
    width = dy0.shape[1]
    tile = width // shards
    return pl.pallas_call(
        functools.partial(adapter_back_kernel, groups),
        grid=(shards,),
        out_shape=[
            jax.ShapeDtypeStruct((2, shards, channels, tile), BF16),
            jax.ShapeDtypeStruct((2, 16, width), F32),
        ],
        in_specs=[
            pl.BlockSpec((tokens, channels), lambda t: (0, 0)),
            pl.BlockSpec((tokens, tile), lambda t: (0, t)),
            pl.BlockSpec((tokens, tile), lambda t: (0, t)),
            pl.BlockSpec((2, tokens, tile), lambda t: (0, 0, t)),
            pl.BlockSpec((2, 16, tile), lambda t: (0, 0, t)),
            pl.BlockSpec((8, tile), lambda t: (0, t)),
        ],
        out_specs=[
            pl.BlockSpec((2, 1, channels, tile), lambda t: (0, t, 0, 0)),
            pl.BlockSpec((2, 16, tile), lambda t: (0, 0, t)),
        ],
        compiler_params=pltpu.CompilerParams(vmem_limit_bytes=VMEM_BYTES),
        name="adapter_backward",
    )(pooled, dy0, dy1, conv, depth_w, gates)


def others(axis, count):
    me = lax.axis_index(axis)
    return [{axis: lax.rem(me + j, count)} for j in range(1, count)]


def add_up(value, slots, send, recv, axis, count):
    copies = [push(value, slots.at[j], send, recv, j, peer) for j, peer in enumerate(others(axis, count))]
    for copy in copies:
        copy.wait_recv()
    total = value[...]
    for j in range(count - 1):
        total = total + slots[j]
    for copy in copies:
        copy.wait_send()
    return total


def gate_rows(weight_in, weight_out, layer, mean):
    inner = jnp.sum(weight_in[layer].astype(F32) * mean, axis=1, keepdims=True)
    return inner, gelu_parts(inner), weight_out[layer].astype(F32)


def gate_kernel(
    groups, copies, patches, sums_ref, extra, weight_in, weight_out, out_ref, value, slot_a, slot_b, slot_c, send, recv
):
    greet(others("mp", groups) + others("dp", copies))
    value[0] = jnp.concatenate(
        [sums_ref[0, 0:1, :], sums_ref[1, 0:1, :], jnp.zeros((6, out_ref.shape[1]), F32)], axis=0
    )
    value[1] = add_up(value.at[0], slot_a, send.at[0], recv.at[0], "mp", groups)
    mean = add_up(value.at[1], slot_b, send.at[1], recv.at[1], "dp", copies) * (1.0 / patches) + extra[0:8, :]
    parts = []
    for layer in range(2):
        inner, (level, slope), out = gate_rows(weight_in, weight_out, layer, mean[layer : layer + 1])
        parts.append(jnp.sum(level * out, axis=0, keepdims=True))
    value[2] = jnp.concatenate(parts + [jnp.zeros((6, out_ref.shape[1]), F32)], axis=0)
    gate = jnp.tanh(add_up(value.at[2], slot_c, send.at[2], recv.at[2], "mp", groups))
    out_ref[...] = jnp.concatenate([gate[0:2], mean[0:2], gate[2:6]], axis=0)


def gate_back_kernel(
    groups, copies, patches, small0, small1, extra, gates, weight_in, weight_out,
    out_ref, grad_in, grad_out, value, slot_a, slot_b, slot_c, send, recv,
):
    greet(others("mp", groups) + others("dp", copies))
    none = jnp.zeros((6, out_ref.shape[1]), F32)
    value[0] = jnp.concatenate(
        [small[4:5, :] + extra[l : l + 1, :] * small[5:6, :] for l, small in enumerate((small0, small1))] + [none],
        axis=0,
    )
    value[1] = add_up(value.at[0], slot_a, send.at[0], recv.at[0], "mp", groups)
    gate_grad = add_up(value.at[1], slot_b, send.at[1], recv.at[1], "dp", copies)
    parts = []
    for layer in range(2):
        gate = gates[layer : layer + 1, :]
        mean = gates[2 + layer : 3 + layer, :]
        pre = gate_grad[layer : layer + 1] * (1.0 - gate * gate)
        inner, (level, slope), out = gate_rows(weight_in, weight_out, layer, mean)
        back = jnp.sum(out * pre, axis=1, keepdims=True) * slope
        grad_out[layer] = level * pre
        grad_in[layer] = back * mean
        parts.append(jnp.sum(weight_in[layer].astype(F32) * back, axis=0, keepdims=True))
    value[2] = jnp.concatenate(parts + [none], axis=0)
    total = add_up(value.at[2], slot_c, send.at[2], recv.at[2], "mp", groups)
    out_ref[...] = jnp.concatenate([gates[0:2, :], total[0:2] * (1.0 / patches), none[0:4]], axis=0)


def last_kernel(groups, copies, value_ref, out_ref, value, slot_p, slot_a, slot_b, send_p, recv_p, send, recv):
    me = lax.axis_index("pipe")
    greet([{"pipe": 1 - me}] + others("mp", groups) + others("dp", copies))
    copy = push(value_ref.at[1 - me], slot_p, send_p, recv_p, 0, {"pipe": 1 - me})
    copy.wait_recv()
    value[0] = value_ref[me] + slot_p[...]
    value[1] = add_up(value.at[0], slot_a, send.at[0], recv.at[0], "mp", groups)
    out_ref[...] = add_up(value.at[1], slot_b, send.at[1], recv.at[1], "dp", copies)
    copy.wait_send()


def sum_scratch(groups, copies, rows, width, stages):
    most = max(groups, copies) - 1
    return [
        pltpu.VMEM((3, rows, width), F32),
        *[pltpu.VMEM((count - 1, rows, width), F32) for count in (groups, copies, groups)[:stages]],
        pltpu.SemaphoreType.DMA((3, most)),
        pltpu.SemaphoreType.DMA((3, most)),
    ]


def talk(ident):
    return pltpu.CompilerParams(collective_id=ident, has_side_effects=True, vmem_limit_bytes=VMEM_BYTES)


def pool_weights(side, count, offset):
    rows_index = jnp.arange(GRID, dtype=jnp.int32)[:, None]
    cols_index = jnp.arange(count, dtype=jnp.int32)[None, :] + offset
    lower = rows_index * side // GRID
    upper = ((rows_index + 1) * side + GRID - 1) // GRID
    inside = (cols_index >= lower) & (cols_index < upper)
    return jnp.where(inside, 1.0 / (upper - lower).astype(F32), 0.0)


def pool_partial(feature, pixels, row_start):
    side = pixels * GRID // 768
    row_matrix = pool_weights(side, feature.shape[0], row_start)
    col_matrix = pool_weights(side, feature.shape[1], 0)
    first = jnp.einsum("ia,abc->ibc", row_matrix.astype(BF16), feature, preferred_element_type=F32)
    second = jnp.einsum("jb,ibc->ijc", col_matrix, first, precision=lax.Precision.HIGHEST)
    return second.reshape(GRID * GRID, feature.shape[2])


def per_device(
    inputs, cotangent, highres, resolution, assign, norm_gain, norm_bias, qkv_weight, out_weight, up_weight,
    down_weight, conv_weight, depth_weight, depth_bias, gate_in, gate_out,
):
    section = lax.axis_index("pipe")
    groups, copies = lax.axis_size("mp"), lax.axis_size("dp")
    first_half = section == 0
    order = assign[0]
    slot, other_slot = order[section], order[1 - section]

    def swap(block):
        return lax.ppermute(block, "pipe", SWAP)

    def both(own):
        got = swap(own)
        return jnp.stack([jnp.where(first_half, own, got), jnp.where(first_half, got, own)])

    def pick(array, index):
        return lax.dynamic_index_in_dim(array, index, 0, keepdims=False)

    width = inputs.shape[2]
    share = out_weight.shape[1]
    own = (qkv_weight[0].reshape(width, 3 * share), out_weight[0], up_weight[0], down_weight[0])
    got = tuple(swap(w) for w in own)
    half_in = gate_in.shape[1]
    low = both(jnp.concatenate([conv_weight[0], gate_in[0], gate_out[0]], axis=0))
    channels = conv_weight.shape[1]
    conv_w, gate_in_w, gate_out_w = low[:, :channels], low[:, channels : channels + half_in], low[:, channels + half_in :]
    wide = both(
        jnp.concatenate(
            [depth_weight[0], depth_bias, norm_gain[0], norm_bias[0], jnp.zeros((2, width), F32)], axis=0
        )
    )
    depth_w, bias = wide, wide[:, 9]
    gains, shifts = wide[:, 10:12], wide[:, 12:14]

    row_start = section * highres.shape[1]
    parts = jax.vmap(pool_partial, in_axes=(0, 0, None))(highres, resolution, row_start).astype(BF16)
    pooled = pick(parts, slot) + swap(pick(parts, other_slot))
    tokens = pooled.shape[0]
    patches = copies * tokens

    conv, depth, sums = adapter_forward(pooled, conv_w, depth_w)
    extra = jnp.pad(bias, ((0, 6), (0, 0)))
    vmem = pl.BlockSpec(memory_space=pltpu.VMEM)
    gates = pl.pallas_call(
        functools.partial(gate_kernel, groups, copies, patches),
        out_shape=jax.ShapeDtypeStruct((8, width), F32),
        in_specs=[vmem] * 4,
        out_specs=vmem,
        scratch_shapes=sum_scratch(groups, copies, 8, width, 3),
        compiler_params=talk(4),
        name="gate_forward",
    )(sums, extra, gate_in_w, gate_out_w)

    def norms(layer):
        return jnp.concatenate(
            [
                jnp.stack([gains[layer, 0], shifts[layer, 0], gains[layer, 1], shifts[layer, 1]]),
                gates[layer : layer + 1],
                gates[layer : layer + 1] * bias[layer : layer + 1],
                jnp.zeros((2, width), F32),
            ]
        )

    norm_packs = (norms(0), norms(1))
    x0 = pick(inputs, slot)
    out0, after0, saved0 = forward_layer(0, 0, x0, norm_packs[0], depth, own, got)
    out1, after1, saved1 = forward_layer(1, 1, out0, norm_packs[1], depth, own, got)
    dy = pick(cotangent, slot)

    cols = width // copies
    ff = up_weight.shape[2]
    blocks = width // TILE
    ends = [3 * share, 4 * share, 4 * share + ff]

    def halves(grads):
        if copies != blocks:
            return grads
        count = grads.shape[1] // 2
        kept = lax.dynamic_slice_in_dim(grads, section * count, count, 1)
        sent = lax.dynamic_slice_in_dim(grads, (1 - section) * count, count, 1)
        summed = (kept.astype(F32) + swap(sent).astype(F32)).astype(BF16)
        return lax.psum_scatter(summed, "dp", scatter_dimension=0, tiled=True)[0]

    dx1, small1, dy_full1, grads1 = backward_layer(
        1, 2, blocks, dy, out0, after1, norm_packs[1], saved1, depth, own, got
    )
    part1 = halves(grads1)
    dx0, small0, dy_full0, grads0 = backward_layer(
        0, 3, blocks, dx1, x0, after0, norm_packs[0], saved0, depth, own, got
    )
    part0 = halves(grads0)

    back_gates, grad_in, grad_out = pl.pallas_call(
        functools.partial(gate_back_kernel, groups, copies, patches),
        out_shape=[
            jax.ShapeDtypeStruct((8, width), F32),
            jax.ShapeDtypeStruct((2, half_in, width), F32),
            jax.ShapeDtypeStruct((2, half_in, width), F32),
        ],
        in_specs=[vmem] * 6,
        out_specs=[vmem] * 3,
        scratch_shapes=sum_scratch(groups, copies, 8, width, 3),
        compiler_params=talk(5),
        name="gate_backward",
    )(small0, small1, extra, gates, gate_in_w, gate_out_w)
    conv_grads, depth_grads = adapter_backward(
        groups, blocks, pooled, dy_full0, dy_full1, conv, depth_w, back_gates
    )

    def owned(first, second):
        kept = jnp.where(first_half, first, second)
        return kept, swap(jnp.where(first_half, second, first))

    def cores_sum(first, second):
        kept, received = owned(first, second)
        return (kept.astype(F32) + received.astype(F32)).astype(BF16)

    def scattered(blocked, dim):
        return lax.psum_scatter(blocked, "dp", scatter_dimension=dim, tiled=True)

    conv_sum = cores_sum(conv_grads[0], conv_grads[1])
    if copies == blocks:
        conv_sum = scattered(conv_sum, 0)[0].astype(F32)
    else:
        conv_sum = scattered(conv_sum.transpose(1, 0, 2).reshape(channels, width), 1).astype(F32)

    values = jnp.stack(
        [
            jnp.concatenate([small[0:4], depth_grads[l, 0:10], jnp.zeros((2, width), F32)])
            for l, small in enumerate((small0, small1))
        ]
    )
    last = pl.pallas_call(
        functools.partial(last_kernel, groups, copies),
        out_shape=jax.ShapeDtypeStruct((16, width), F32),
        in_specs=[vmem],
        out_specs=vmem,
        scratch_shapes=[
            pltpu.VMEM((2, 16, width), F32),
            pltpu.VMEM((16, width), F32),
            pltpu.VMEM((groups - 1, 16, width), F32),
            pltpu.VMEM((copies - 1, 16, width), F32),
            pltpu.SemaphoreType.DMA((1,)),
            pltpu.SemaphoreType.DMA((1,)),
            pltpu.SemaphoreType.DMA((2, max(groups, copies) - 1)),
            pltpu.SemaphoreType.DMA((2, max(groups, copies) - 1)),
        ],
        compiler_params=talk(6),
        name="last_sums",
    )(values)

    gate_kept, gate_got = owned(
        jnp.stack([grad_in[0], grad_out[0]]), jnp.stack([grad_in[1], grad_out[1]])
    )
    gate_sum = gate_kept + gate_got

    def by_image(kept, received):
        return jnp.where(slot == 0, jnp.stack([kept, received]), jnp.stack([received, kept]))

    layer_out = by_image(*owned(out0, out1))
    input_grad = by_image(*owned(dx0, dx1))
    if copies == blocks:
        kept, received = owned(part0, part1)
        full = jnp.where(
            first_half, jnp.concatenate([kept, received]), jnp.concatenate([received, kept])
        ).astype(F32)
        qkv_grad = full[: ends[0]].reshape(3 * share // cols, cols, cols).transpose(1, 0, 2).reshape(cols, 3, share)
        out_grad = full[ends[0] : ends[1]]
        up_grad = full[ends[1] : ends[2]].reshape(ff // cols, cols, cols).transpose(1, 0, 2).reshape(cols, ff)
        down_grad = full[ends[2] :]
    else:
        whole = cores_sum(part0, part1)

        def by_rows(block):
            tiles = block.reshape(blocks, block.shape[1] // TILE, TILE, TILE)
            return scattered(tiles.transpose(0, 2, 1, 3).reshape(width, block.shape[1]), 0).astype(F32)

        def by_cols(block):
            return scattered(block.transpose(1, 0, 2).reshape(block.shape[1], width), 1).astype(F32)

        qkv_grad = by_rows(whole[:, : ends[0]]).reshape(cols, 3, share)
        out_grad = by_cols(whole[:, ends[0] : ends[1]])
        up_grad = by_rows(whole[:, ends[1] : ends[2]])
        down_grad = by_cols(whole[:, ends[2] :])
    return (
        layer_out[None],
        input_grad[None],
        jnp.stack([last[0], last[2]])[None],
        jnp.stack([last[1], last[3]])[None],
        qkv_grad[None],
        out_grad[None],
        up_grad[None],
        down_grad[None],
        conv_sum[None],
        last[4:13][None],
        last[13][None],
        gate_sum[0][None],
        gate_sum[1][None],
    )


def solution(mesh):
    return jax.shard_map(
        per_device,
        mesh=mesh,
        in_specs=(
            P("dp", "mp", None),
            P("dp", "mp", None),
            P("dp", "pipe", None, "mp"),
            P("dp"),
            P("dp", None),
            P("pipe", None, None),
            P("pipe", None, None),
            P("pipe", None, None, "mp"),
            P("pipe", "mp", None),
            P("pipe", None, "mp"),
            P("pipe", "mp", None),
            P("pipe", "mp", None),
            P("pipe", None, None),
            P("pipe", None),
            P("pipe", "mp", None),
            P("pipe", "mp", None),
        ),
        out_specs=(
            P("pipe", "dp", "mp", None),
            P("pipe", "dp", "mp", None),
            P("pipe", None, None),
            P("pipe", None, None),
            P("pipe", "dp", None, "mp"),
            P("pipe", "mp", "dp"),
            P("pipe", "dp", "mp"),
            P("pipe", "mp", "dp"),
            P("pipe", "mp", "dp"),
            P("pipe", None, None),
            P("pipe", None),
            P("pipe", "mp", None),
            P("pipe", "mp", None),
        ),
        check_vma=False,
    )
```

```python
import functools

import jax
import jax.numpy as jnp
from jax import lax
from jax.experimental import pallas as pl
from jax.experimental.pallas import tpu as pltpu
from jax.sharding import PartitionSpec as P

GRID = 24
HEAD = 64
EPS = 1e-06
TILE = 256
VMEM_BYTES = 60 * 1024 * 1024
MESH = pl.DeviceIdType.MESH
F32 = jnp.float32
BF16 = jnp.bfloat16
SWAP = [(0, 1), (1, 0)]


def mm(a, b, ca=1, cb=0):
    return lax.dot_general(a, b, (((ca,), (cb,)), ((), ())), preferred_element_type=F32)


def tile_of(index, width=TILE):
    return pl.ds(pl.multiple_of(index * width, width), width)


def place():
    me = lax.axis_index("mp")
    col, line = lax.rem(me, 2), lax.div(me, 2)
    return me, line * 2 + 1 - col, (1 - line) * 2 + col, (1 - line) * 2 + 1 - col


def greet(peers):
    barrier = pltpu.get_barrier_semaphore()
    for peer in peers:
        pl.semaphore_signal(barrier, inc=1, device_id=peer, device_id_type=MESH)
    pl.semaphore_wait(barrier, len(peers))


def push(src, dst, send, recv, slot, peer):
    copy = pltpu.make_async_remote_copy(
        src_ref=src,
        dst_ref=dst,
        send_sem=send.at[slot],
        recv_sem=recv.at[slot],
        device_id=peer,
        device_id_type=MESH,
    )
    copy.start()
    return copy


class Gather:
    def __init__(self, buf, send, recv, spot, rows):
        me, xn, yn, dn = spot
        self.buf, self.send, self.recv, self.spot, self.rows = buf, send, recv, spot, rows
        own = buf.at[rows(me)]
        self.near = [
            push(own, own, send, recv, 0, {"mp": xn}),
            push(own, own, send, recv, 1, {"mp": yn}),
        ]

    def forward(self):
        me, xn, yn, dn = self.spot
        half = self.buf.shape[1] // 2
        self.near[0].wait_recv()
        left = self.buf.at[self.rows(xn), pl.ds(0, half)]
        first = push(left, left, self.send, self.recv, 2, {"mp": yn})
        self.near[1].wait_recv()
        right = self.buf.at[self.rows(yn), pl.ds(half, half)]
        self.far = [first, push(right, right, self.send, self.recv, 3, {"mp": xn})]

    def finish(self):
        for copy in self.far:
            copy.wait_recv()

    def drain(self):
        for copy in self.near + self.far:
            copy.wait_send()


class Scatter:
    def __init__(self, bufs, send, recv, spot):
        self.px, self.py, self.pd, self.via, self.rx, self.ry = bufs
        self.send, self.recv, self.spot = send, recv, spot
        width = self.px.shape[1]
        self.low, self.high = pl.ds(0, width // 2), pl.ds(width // 2, width // 2)

    def far(self):
        me, xn, yn, dn = self.spot
        self.far_copies = [
            push(self.pd.at[:, self.low], self.via.at[0], self.send, self.recv, 0, {"mp": xn}),
            push(self.pd.at[:, self.high], self.via.at[1], self.send, self.recv, 1, {"mp": yn}),
        ]

    def near_x(self):
        self.x_copy = push(
            self.px.at[:, self.low], self.rx.at[:, self.low], self.send, self.recv, 2, {"mp": self.spot[1]}
        )

    def near_y(self):
        self.y_copy = push(
            self.py.at[:, self.high], self.ry.at[:, self.high], self.send, self.recv, 3, {"mp": self.spot[2]}
        )

    def relay(self):
        me, xn, yn, dn = self.spot
        self.far_copies[0].wait_recv()
        self.py[:, self.low] = (self.py[:, self.low].astype(F32) + self.via[0].astype(F32)).astype(BF16)
        first = push(self.py.at[:, self.low], self.ry.at[:, self.low], self.send, self.recv, 4, {"mp": yn})
        self.far_copies[1].wait_recv()
        self.px[:, self.high] = (self.px[:, self.high].astype(F32) + self.via[1].astype(F32)).astype(BF16)
        second = push(self.px.at[:, self.high], self.rx.at[:, self.high], self.send, self.recv, 5, {"mp": xn})
        self.last_copies = [first, second]

    def total(self, own):
        for copy in [self.x_copy, self.y_copy] + self.last_copies:
            copy.wait_recv()
        return own + self.rx[...].astype(F32) + self.ry[...].astype(F32)

    def drain(self):
        for copy in self.far_copies + [self.x_copy, self.y_copy] + self.last_copies:
            copy.wait_send()


def scatter_scratch(rows, width):
    return [
        pltpu.VMEM((rows, width), BF16),
        pltpu.VMEM((rows, width), BF16),
        pltpu.VMEM((rows, width), BF16),
        pltpu.VMEM((2, rows, width // 2), BF16),
        pltpu.VMEM((rows, width), BF16),
        pltpu.VMEM((rows, width), BF16),
    ]


def norm_rows(values, gain, shift):
    center = values - jnp.mean(values, axis=-1, keepdims=True)
    spread = jnp.mean(center * center, axis=-1, keepdims=True)
    return center * lax.rsqrt(spread + EPS) * gain + shift


def norm_back(values, gain, grad):
    center = values - jnp.mean(values, axis=-1, keepdims=True)
    scale = lax.rsqrt(jnp.mean(center * center, axis=-1, keepdims=True) + EPS)
    unit = center * scale
    scaled = grad * gain
    mean_one = jnp.mean(scaled, axis=-1, keepdims=True)
    mean_two = jnp.mean(scaled * unit, axis=-1, keepdims=True)
    back = scale * (scaled - mean_one - unit * mean_two)
    return back, jnp.sum(grad * unit, axis=0, keepdims=True), jnp.sum(grad, axis=0, keepdims=True)


def gelu_parts(values):
    below = 0.5 * (1.0 + lax.erf(values * 0.7071067811865476))
    bell = jnp.exp(-0.5 * values * values) * 0.3989422804014327
    return values * below, below + values * bell


class Sum:
    def __init__(self, value, slots, send, recv, axis, count):
        self.value, self.slots = value, slots
        self.copies = [push(value, slots.at[j], send, recv, j, peer) for j, peer in enumerate(others(axis, count))]

    def finish(self):
        for copy in self.copies:
            copy.wait_recv()
        total = self.value[...]
        for j in range(len(self.copies)):
            total = total + self.slots[j]
        return total

    def drain(self):
        for copy in self.copies:
            copy.wait_send()


def others(axis, count):
    me = lax.axis_index(axis)
    return [{axis: lax.rem(me + j, count)} for j in range(1, count)]


def sum_scratch(groups, copies, width):
    most = max(groups, copies) - 1
    return [
        pltpu.VMEM((3, 1, width), F32),
        pltpu.VMEM((3, most, 1, width), F32),
        pltpu.SemaphoreType.DMA((3, most)),
        pltpu.SemaphoreType.DMA((3, most)),
    ]


class Loads:
    def __init__(self, layer, own, got, held, sems):
        self.mine = lax.axis_index("pipe") == layer
        self.own, self.got, self.held, self.sems = own, got, held, sems

    def start(self, *which):
        for i in which:

            @pl.when(self.mine)
            def _():
                pltpu.make_async_copy(self.own[i], self.held[i], self.sems.at[i]).start()

            @pl.when(jnp.logical_not(self.mine))
            def _():
                pltpu.make_async_copy(self.got[i], self.held[i], self.sems.at[i]).start()

    def wait(self, *which):
        for i in which:
            pltpu.make_async_copy(self.own[i], self.held[i], self.sems.at[i]).wait()


class Copies:
    def __init__(self, pairs, sems):
        self.copies = [pltpu.make_async_copy(src, dst, sems.at[i]) for i, (src, dst) in enumerate(pairs)]
        self.started = []

    def start(self, *which):
        for i in which:
            self.copies[i].start()
            self.started.append(i)

    def wait(self, *which):
        for i in which:
            self.copies[i].wait()
            self.started.remove(i)

    def finish(self):
        self.wait(*list(self.started))


BIAS, GAIN_ONE, GAIN_TWO, SHIFT_ONE, SHIFT_TWO = 9, 10, 11, 12, 13
QKV, OUT, UP, DOWN, CONV, GATE_IN, GATE_OUT = range(7)


def row_of(pack, index):
    return pack[index : index + 1, :]


def beside(field):
    cells, width = field.shape
    index = lax.broadcasted_iota(jnp.int32, (cells, width), 0)
    col = index - lax.shift_right_logical(index * 2731, 16) * GRID
    before = jnp.where(col >= 1, pltpu.roll(field, 1, 0), 0.0)
    behind = jnp.where(col <= GRID - 2, pltpu.roll(field, cells - 1, 0), 0.0)
    return before, field, behind


def depthwise(field, kernel):
    cells, width = field.shape
    shifted = beside(field)
    lines = [sum(kernel[3 * i + j] * shifted[j] for j in range(3)) for i in range(3)]
    none = jnp.zeros((GRID, width), F32)
    above = jnp.concatenate([none, lines[0][: cells - GRID]], axis=0)
    below = jnp.concatenate([lines[2][GRID:], none], axis=0)
    return above + lines[1] + below


def lane_halves():
    lane = lax.broadcasted_iota(jnp.int32, (1, 2 * HEAD), 1)
    return [lane < HEAD, lane >= HEAD]


def pair_slices(pair, share):
    return [slice(base + pair * 2 * HEAD, base + (pair + 1) * 2 * HEAD) for base in (0, share, 2 * share)]


def forward_kernel(layer, groups, copies, *refs):
    x_ref, pack, pooled = refs[:3]
    out_ref, after_ref, gate_ref = refs[17:20]
    saved_hbm = refs[20:29]
    first, qkv, probs, mixed, second, hidden, slope, conv, depth = refs[29:38]
    weights = refs[38:45]
    wq, wo, wu, wd, wc, gate_in, gate_out = weights
    own = refs[45]
    bufs_one, bufs_two = refs[46:52], refs[52:58]
    value, slots, sum_send, sum_recv = refs[58:62]
    load_sem, save_sem, ag_send, ag_recv, rs_send, rs_recv = refs[62:]

    size, width = x_ref.shape
    tokens, share, ff = first.shape[0], mixed.shape[1], hidden.shape[1]
    spot = place()
    me, xn, yn, dn = spot

    def rows(i):
        return pl.ds(pl.multiple_of(i * size, 16), size)

    loads = Loads(layer, refs[3:10], refs[10:17], weights, load_sem)
    loads.start(CONV, QKV, OUT, GATE_IN, GATE_OUT)
    saves = Copies(list(zip((first, qkv, probs, mixed, second, hidden, slope, conv, depth), saved_hbm)), save_sem)
    greet([{"mp": xn}, {"mp": yn}, {"mp": dn}] + others("dp", copies))

    x = x_ref[...].astype(F32)
    first[rows(me), :] = norm_rows(x, row_of(pack, GAIN_ONE), row_of(pack, SHIFT_ONE)).astype(BF16)
    gather = Gather(first, ag_send.at[0], ag_recv.at[0], spot, rows)

    loads.wait(CONV)
    mapped = mm(pooled[...], wc[...])
    for t in range(width // TILE):
        lanes = slice(t * TILE, (t + 1) * TILE)
        conv[:, lanes] = mapped[:, lanes].astype(BF16)
        filtered = depthwise(mapped[:, lanes], [pack[k : k + 1, lanes] for k in range(9)])
        depth[:, lanes] = filtered.astype(BF16)
        value[0, :, lanes] = jnp.sum(filtered, axis=0, keepdims=True)
    sum_one = Sum(value.at[0], slots.at[0], sum_send.at[0], sum_recv.at[0], "mp", groups)
    saves.start(7, 8)

    def project(i):
        qkv[rows(i), :] = mm(first[rows(i), :], wq[...]).astype(BF16)

    loads.wait(QKV)
    project(me)
    gather.forward()
    loads.start(UP, DOWN)
    value[1] = sum_one.finish()
    sum_two = Sum(value.at[1], slots.at[1], sum_send.at[1], sum_recv.at[1], "dp", copies)
    project(xn)
    project(yn)
    gather.finish()
    project(dn)
    saves.start(0, 1)

    halves = lane_halves()
    for pair in range(share // (2 * HEAD)):
        at_query, at_key, at_value = pair_slices(pair, share)
        query = qkv[:, at_query] * jnp.asarray(HEAD**-0.5, BF16)
        parts = []
        for h in range(2):
            scores = mm(jnp.where(halves[h], query, jnp.zeros_like(query)), qkv[:, at_key], 1, 1)
            raised = jnp.exp(scores - jnp.max(scores, axis=-1, keepdims=True))
            chances = (raised * (1.0 / jnp.sum(raised, axis=-1, keepdims=True))).astype(BF16)
            probs[2 * pair + h] = chances
            parts.append(mm(chances, qkv[:, at_value]))
        mixed[:, at_query] = jnp.where(halves[0], parts[0], parts[1]).astype(BF16)

    loads.wait(OUT, GATE_IN, GATE_OUT)
    scatter = Scatter(bufs_one, rs_send.at[0], rs_recv.at[0], spot)

    def out_part(i):
        return mm(mixed[rows(i), :], wo[...])

    scatter.pd[...] = out_part(dn).astype(BF16)
    scatter.far()
    scatter.px[...] = out_part(xn).astype(BF16)
    scatter.near_x()
    scatter.py[...] = out_part(yn).astype(BF16)
    scatter.near_y()
    own[...] = out_part(me)
    saves.start(2, 3)
    mean = sum_two.finish() * (1.0 / (copies * tokens)) + row_of(pack, BIAS)
    level = gelu_parts(jnp.sum(gate_in[...].astype(F32) * mean, axis=1, keepdims=True))[0]
    value[2] = jnp.sum(level * gate_out[...].astype(F32), axis=0, keepdims=True)
    sum_three = Sum(value.at[2], slots.at[2], sum_send.at[2], sum_recv.at[2], "mp", groups)
    scatter.relay()
    after = x + scatter.total(own[...])
    after_ref[...] = after
    second[rows(me), :] = norm_rows(after, row_of(pack, GAIN_TWO), row_of(pack, SHIFT_TWO)).astype(BF16)
    gather.drain()
    gather = Gather(second, ag_send.at[1], ag_recv.at[1], spot, rows)
    scatter.drain()
    gate = jnp.tanh(sum_three.finish())
    gate_ref[...] = jnp.concatenate([gate, mean, jnp.zeros((6, width), F32)], axis=0)
    loads.wait(UP, DOWN)

    def feed(i):
        for t in range(ff // TILE):
            lanes = slice(t * TILE, (t + 1) * TILE)
            level, grad = gelu_parts(mm(second[rows(i), :], wu[:, lanes]))
            hidden[rows(i), lanes] = level.astype(BF16)
            slope[rows(i), lanes] = grad.astype(BF16)
        return mm(hidden[rows(i), :], wd[...]) + gate * depth[rows(i), :].astype(F32)

    scatter = Scatter(bufs_two, rs_send.at[1], rs_recv.at[1], spot)
    own[...] = feed(me)
    gather.forward()
    scatter.px[...] = feed(xn).astype(BF16)
    scatter.near_x()
    scatter.py[...] = feed(yn).astype(BF16)
    scatter.near_y()
    gather.finish()
    scatter.pd[...] = feed(dn).astype(BF16)
    scatter.far()
    saves.start(4, 5, 6)
    scatter.relay()
    out_ref[...] = (after_ref[...] + scatter.total(own[...]) + gate * row_of(pack, BIAS)).astype(BF16)
    gather.drain()
    scatter.drain()
    for one in (sum_one, sum_two, sum_three):
        one.drain()
    saves.finish()


def forward_layer(layer, ident, groups, copies, x, pack, pooled, own, got):
    size, width = x.shape
    tokens = pooled.shape[0]
    share, ff = own[OUT].shape[0], own[UP].shape[1]
    heads = share // HEAD
    vmem, anywhere = pl.BlockSpec(memory_space=pltpu.VMEM), pl.BlockSpec(memory_space=pl.ANY)
    saved = [
        ((tokens, width), BF16),
        ((tokens, 3 * share), BF16),
        ((heads, tokens, tokens), BF16),
        ((tokens, share), BF16),
        ((tokens, width), BF16),
        ((tokens, ff), BF16),
        ((tokens, ff), BF16),
        ((tokens, width), BF16),
        ((tokens, width), BF16),
    ]
    outs = pl.pallas_call(
        functools.partial(forward_kernel, layer, groups, copies),
        out_shape=[
            jax.ShapeDtypeStruct((size, width), BF16),
            jax.ShapeDtypeStruct((size, width), F32),
            jax.ShapeDtypeStruct((8, width), F32),
        ]
        + [jax.ShapeDtypeStruct(*s) for s in saved],
        in_specs=[vmem] * 3 + [anywhere] * 14,
        out_specs=[vmem] * 3 + [anywhere] * 9,
        scratch_shapes=[pltpu.VMEM(*s) for s in saved]
        + [pltpu.VMEM(w.shape, BF16) for w in own]
        + [pltpu.VMEM((size, width), F32)]
        + scatter_scratch(size, width)
        + scatter_scratch(size, width)
        + sum_scratch(groups, copies, width)
        + [
            pltpu.SemaphoreType.DMA((7,)),
            pltpu.SemaphoreType.DMA((9,)),
            pltpu.SemaphoreType.DMA((2, 4)),
            pltpu.SemaphoreType.DMA((2, 4)),
            pltpu.SemaphoreType.DMA((2, 6)),
            pltpu.SemaphoreType.DMA((2, 6)),
        ],
        compiler_params=talk(ident),
        cost_estimate=pl.CostEstimate(flops=20_000_000_000, bytes_accessed=30_000_000, transcendentals=0),
        name="layer_forward",
    )(x, pack, pooled, *own, *got)
    return outs[0], outs[1], outs[2], outs[3:]


def backward_kernel(layer, groups, copies, *refs):
    dy_ref, x_ref, after_ref, pack, pooled, gate_ref = refs[:6]
    saved_hbm = refs[6:15]
    dx_ref, small_ref, grad_in, grad_out, grads_hbm = refs[29:34]
    held = refs[34:43]
    first, qkv, probs, mixed, second, hidden, slope, conv, depth = held
    weights = refs[43:49]
    wq, wo, wu, wd, gate_in, gate_out = weights
    own = refs[49]
    bufs_one, bufs_two = refs[50:56], refs[56:62]
    dyf, dhp, daf, dmixed, dqkv, dafter, grads = refs[62:69]
    value, slots, sum_send, sum_recv = refs[69:73]
    load_sem, saved_sem, save_sem, ag_send, ag_recv, rs_send, rs_recv = refs[73:]

    size, width = dy_ref.shape
    tokens, share, ff = first.shape[0], mixed.shape[1], hidden.shape[1]
    channels = pooled.shape[1]
    shards = grads.shape[0]
    cols = width // shards
    spot = place()
    me, xn, yn, dn = spot
    base_out = 3 * share
    base_conv = base_out + share
    base_up = base_conv + channels
    base_down = base_up + ff

    def rows(i):
        return pl.ds(pl.multiple_of(i * size, 16), size)

    def by_rows(base, grad, s):
        for t in range(grad.shape[1] // cols):
            grads[s, base + t * cols : base + (t + 1) * cols, :] = grad[:, t * cols : (t + 1) * cols].astype(BF16)

    def by_cols(base, grad):
        for s in range(shards):
            grads[s, base : base + grad.shape[0], :] = grad[:, s * cols : (s + 1) * cols].astype(BF16)

    own_w, got_w = refs[15:22], refs[22:29]
    keep = (QKV, OUT, UP, DOWN, GATE_IN, GATE_OUT)
    loads = Loads(layer, [own_w[i] for i in keep], [got_w[i] for i in keep], weights, load_sem)
    saved = Copies(list(zip(saved_hbm, held)), saved_sem)
    saved.start(6)
    loads.start(3, 2)
    saves = Copies([(grads, grads_hbm)], save_sem)
    greet([{"mp": xn}, {"mp": yn}, {"mp": dn}] + others("dp", copies))

    dyf[rows(me), :] = dy_ref[...]
    gather = Gather(dyf, ag_send.at[0], ag_recv.at[0], spot, rows)
    scatter = Scatter(bufs_one, rs_send.at[0], rs_recv.at[0], spot)
    dy = dy_ref[...].astype(F32)
    dy_bias = jnp.sum(dy, axis=0, keepdims=True) * row_of(pack, BIAS)
    small_ref[...] = jnp.zeros_like(small_ref)
    saved.wait(6)
    loads.wait(3, 2)

    def feed_back(i):
        for t in range(ff // TILE):
            lanes = slice(t * TILE, (t + 1) * TILE)
            back = mm(dyf[rows(i), :], wd[lanes, :], 1, 1)
            dhp[rows(i), lanes] = (back * slope[rows(i), lanes].astype(F32)).astype(BF16)
        return mm(dhp[rows(i), :], wu[...], 1, 1)

    own[...] = feed_back(me)
    saved.start(5, 8, 4)
    gather.forward()
    scatter.px[...] = feed_back(xn).astype(BF16)
    scatter.near_x()
    scatter.py[...] = feed_back(yn).astype(BF16)
    scatter.near_y()
    loads.start(1, 0, 4, 5)
    saved.start(1, 2, 3, 0, 7)
    gather.finish()
    scatter.pd[...] = feed_back(dn).astype(BF16)
    scatter.far()
    saved.wait(8)
    value[0] = dy_bias + jnp.sum(dyf[...].astype(F32) * depth[...].astype(F32), axis=0, keepdims=True)
    sum_one = Sum(value.at[0], slots.at[0], sum_send.at[0], sum_recv.at[0], "mp", groups)
    saved.wait(5)
    by_cols(base_down, mm(hidden[...], dyf[...], 0, 0))
    scatter.relay()
    value[1] = sum_one.finish()
    sum_two = Sum(value.at[1], slots.at[1], sum_send.at[1], sum_recv.at[1], "dp", copies)
    saved.wait(4)
    for s in range(shards):
        by_rows(base_up, mm(second[:, s * cols : (s + 1) * cols], dhp[...], 0, 0), s)
    back, gain_grad, bias_grad = norm_back(after_ref[...], row_of(pack, GAIN_TWO), scatter.total(own[...]))
    small_ref[1:2, :] = gain_grad
    small_ref[3:4, :] = bias_grad
    dafter[...] = dy + back
    daf[rows(me), :] = dafter[...].astype(BF16)
    gather.drain()
    gather = Gather(daf, ag_send.at[1], ag_recv.at[1], spot, rows)
    scatter.drain()
    scatter = Scatter(bufs_two, rs_send.at[1], rs_recv.at[1], spot)

    loads.wait(4, 5, 1)
    gate, mean = gate_ref[0:1, :], gate_ref[1:2, :]
    pre = sum_two.finish() * (1.0 - gate * gate)
    level, steep = gelu_parts(jnp.sum(gate_in[...].astype(F32) * mean, axis=1, keepdims=True))
    inner = jnp.sum(gate_out[...].astype(F32) * pre, axis=1, keepdims=True) * steep
    grad_out[...] = level * pre
    grad_in[...] = inner * mean
    value[2] = jnp.sum(gate_in[...].astype(F32) * inner, axis=0, keepdims=True)
    sum_three = Sum(value.at[2], slots.at[2], sum_send.at[2], sum_recv.at[2], "mp", groups)

    def mix_back(i):
        dmixed[rows(i), :] = mm(daf[rows(i), :], wo[...], 1, 1).astype(BF16)

    mix_back(me)
    gather.forward()
    mix_back(xn)
    mix_back(yn)
    mean_grad = sum_three.finish() * (1.0 / (copies * tokens))
    saved.wait(7)
    for t in range(shards):
        lanes = slice(t * cols, (t + 1) * cols)
        grad = gate[:, lanes] * dyf[:, lanes].astype(F32) + mean_grad[:, lanes]
        shifted = beside(conv[:, lanes].astype(F32))
        for i in range(3):
            for j in range(3):
                if i == 0:
                    terms = shifted[j][: tokens - GRID] * grad[GRID:]
                elif i == 1:
                    terms = shifted[j] * grad
                else:
                    terms = shifted[j][GRID:] * grad[: tokens - GRID]
                small_ref[4 + 3 * i + j : 5 + 3 * i + j, lanes] = jnp.sum(terms, axis=0, keepdims=True)
        small_ref[13:14, lanes] = jnp.sum(grad, axis=0, keepdims=True) * (1.0 / groups)
        back = depthwise(grad, [pack[8 - k : 9 - k, lanes] for k in range(9)])
        grads[t, base_conv : base_conv + channels, :] = mm(pooled[...], back.astype(BF16), 0, 0).astype(BF16)
    gather.finish()
    mix_back(dn)

    saved.wait(1, 2)
    halves = lane_halves()
    scale = HEAD**-0.5
    for pair in range(share // (2 * HEAD)):
        at_query, at_key, at_value = pair_slices(pair, share)
        upper = dmixed[:, at_query]
        parts, key_grads, value_grads = [], [], []
        for h in range(2):
            low = probs[2 * pair + h]
            exact = low.astype(F32)
            grad_probs = mm(jnp.where(halves[h], upper, jnp.zeros_like(upper)), qkv[:, at_value], 1, 1)
            delta = jnp.sum(exact * grad_probs, axis=-1, keepdims=True)
            grad_scores = (exact * (grad_probs - delta)).astype(BF16)
            parts.append(mm(grad_scores, qkv[:, at_key]))
            key_grads.append(mm(grad_scores, qkv[:, at_query], 0, 0))
            value_grads.append(mm(low, upper, 0, 0))
        dqkv[:, at_query] = (jnp.where(halves[0], parts[0], parts[1]) * scale).astype(BF16)
        dqkv[:, at_key] = (jnp.where(halves[0], key_grads[0], key_grads[1]) * scale).astype(BF16)
        dqkv[:, at_value] = jnp.where(halves[0], value_grads[0], value_grads[1]).astype(BF16)
    loads.wait(0)

    def first_back(i):
        return mm(dqkv[rows(i), :], wq[...], 1, 1)

    scatter.pd[...] = first_back(dn).astype(BF16)
    scatter.far()
    scatter.px[...] = first_back(xn).astype(BF16)
    scatter.near_x()
    scatter.py[...] = first_back(yn).astype(BF16)
    scatter.near_y()
    own[...] = first_back(me)
    saved.wait(3)
    by_cols(base_out, mm(mixed[...], daf[...], 0, 0))
    scatter.relay()
    saved.wait(0)
    for s in range(shards):
        by_rows(0, mm(first[:, s * cols : (s + 1) * cols], dqkv[...], 0, 0), s)
    saves.start(0)
    back, gain_grad, bias_grad = norm_back(
        x_ref[...].astype(F32), row_of(pack, GAIN_ONE), scatter.total(own[...])
    )
    small_ref[0:1, :] = gain_grad
    small_ref[2:3, :] = bias_grad
    dx_ref[...] = (dafter[...] + back).astype(BF16)
    gather.drain()
    scatter.drain()
    for one in (sum_one, sum_two, sum_three):
        one.drain()
    saves.finish()


def backward_layer(layer, ident, groups, copies, shards, dy, x, after, pack, pooled, gate, saved, own, got):
    size, width = dy.shape
    tokens, channels = pooled.shape
    share, ff = own[OUT].shape[0], own[UP].shape[1]
    hidden = own[GATE_IN].shape[0]
    vmem, anywhere = pl.BlockSpec(memory_space=pltpu.VMEM), pl.BlockSpec(memory_space=pl.ANY)
    grads_shape = (shards, 4 * share + channels + 2 * ff, width // shards)
    return pl.pallas_call(
        functools.partial(backward_kernel, layer, groups, copies),
        out_shape=[
            jax.ShapeDtypeStruct((size, width), BF16),
            jax.ShapeDtypeStruct((16, width), F32),
            jax.ShapeDtypeStruct((hidden, width), F32),
            jax.ShapeDtypeStruct((hidden, width), F32),
            jax.ShapeDtypeStruct(grads_shape, BF16),
        ],
        in_specs=[vmem] * 6 + [anywhere] * 23,
        out_specs=[vmem] * 4 + [anywhere],
        scratch_shapes=[pltpu.VMEM(s.shape, s.dtype) for s in saved]
        + [pltpu.VMEM(own[i].shape, BF16) for i in (QKV, OUT, UP, DOWN, GATE_IN, GATE_OUT)]
        + [pltpu.VMEM((size, width), F32)]
        + scatter_scratch(size, width)
        + scatter_scratch(size, width)
        + [
            pltpu.VMEM((tokens, width), BF16),
            pltpu.VMEM((tokens, ff), BF16),
            pltpu.VMEM((tokens, width), BF16),
            pltpu.VMEM((tokens, share), BF16),
            pltpu.VMEM((tokens, 3 * share), BF16),
            pltpu.VMEM((size, width), F32),
            pltpu.VMEM(grads_shape, BF16),
        ]
        + sum_scratch(groups, copies, width)
        + [
            pltpu.SemaphoreType.DMA((6,)),
            pltpu.SemaphoreType.DMA((9,)),
            pltpu.SemaphoreType.DMA((1,)),
            pltpu.SemaphoreType.DMA((2, 4)),
            pltpu.SemaphoreType.DMA((2, 4)),
            pltpu.SemaphoreType.DMA((2, 6)),
            pltpu.SemaphoreType.DMA((2, 6)),
        ],
        compiler_params=talk(ident),
        cost_estimate=pl.CostEstimate(flops=40_000_000_000, bytes_accessed=40_000_000, transcendentals=0),
        name="layer_backward",
    )(dy, x, after, pack, pooled, gate, *saved, *own, *got)


def last_kernel(groups, copies, value_ref, out_ref, value, slot_p, slot_a, slot_b, send_p, recv_p, send, recv):
    me = lax.axis_index("pipe")
    greet([{"pipe": 1 - me}] + others("mp", groups) + others("dp", copies))
    copy = push(value_ref.at[1 - me], slot_p, send_p, recv_p, 0, {"pipe": 1 - me})
    copy.wait_recv()
    value[0] = value_ref[me] + slot_p[...]
    over_groups = Sum(value.at[0], slot_a, send.at[0], recv.at[0], "mp", groups)
    value[1] = over_groups.finish()
    over_copies = Sum(value.at[1], slot_b, send.at[1], recv.at[1], "dp", copies)
    out_ref[...] = over_copies.finish()
    copy.wait_send()
    over_groups.drain()
    over_copies.drain()


def talk(ident):
    return pltpu.CompilerParams(collective_id=ident, has_side_effects=True, vmem_limit_bytes=VMEM_BYTES)


def pool_weights(side, count, offset):
    rows_index = jnp.arange(GRID, dtype=jnp.int32)[:, None]
    cols_index = jnp.arange(count, dtype=jnp.int32)[None, :] + offset
    lower = rows_index * side // GRID
    upper = ((rows_index + 1) * side + GRID - 1) // GRID
    inside = (cols_index >= lower) & (cols_index < upper)
    return jnp.where(inside, 1.0 / (upper - lower).astype(F32), 0.0)


def pool_partial(feature, pixels, row_start):
    side = pixels * GRID // 768
    row_matrix = pool_weights(side, feature.shape[0], row_start)
    col_matrix = pool_weights(side, feature.shape[1], 0)
    first = jnp.einsum("ia,abc->ibc", row_matrix.astype(BF16), feature, preferred_element_type=F32)
    second = jnp.einsum("jb,ibc->ijc", col_matrix, first, precision=lax.Precision.HIGHEST)
    return second.reshape(GRID * GRID, feature.shape[2])


def per_device(
    inputs, cotangent, highres, resolution, assign, norm_gain, norm_bias, qkv_weight, out_weight, up_weight,
    down_weight, conv_weight, depth_weight, depth_bias, gate_in, gate_out,
):
    section = lax.axis_index("pipe")
    groups, copies = lax.axis_size("mp"), lax.axis_size("dp")
    first_half = section == 0
    order = assign[0]
    slot, other_slot = order[section], order[1 - section]

    def swap(block):
        return lax.ppermute(block, "pipe", SWAP)

    def both(own):
        got = swap(own)
        return jnp.stack([jnp.where(first_half, own, got), jnp.where(first_half, got, own)])

    def pick(array, index):
        return lax.dynamic_index_in_dim(array, index, 0, keepdims=False)

    width = inputs.shape[2]
    share, channels, ff = out_weight.shape[1], conv_weight.shape[1], up_weight.shape[2]
    wide = both(
        jnp.concatenate(
            [depth_weight[0], depth_bias, norm_gain[0], norm_bias[0], jnp.zeros((2, width), F32)], axis=0
        )
    )
    own = (
        qkv_weight[0].reshape(width, 3 * share), out_weight[0], up_weight[0], down_weight[0], conv_weight[0],
        gate_in[0], gate_out[0],
    )
    got = tuple(swap(w) for w in own)

    row_start = section * highres.shape[1]
    parts = jax.vmap(pool_partial, in_axes=(0, 0, None))(highres, resolution, row_start).astype(BF16)
    pooled = pick(parts, slot) + swap(pick(parts, other_slot))

    x0 = pick(inputs, slot)
    out0, after0, gate0, saved0 = forward_layer(0, 0, groups, copies, x0, wide[0], pooled, own, got)
    out1, after1, gate1, saved1 = forward_layer(1, 1, groups, copies, out0, wide[1], pooled, own, got)
    dy = pick(cotangent, slot)
    cols = width // copies
    blocks = width // TILE
    ends = [3 * share, 4 * share, 4 * share + channels, 4 * share + channels + ff]

    def halves(grads):
        if copies != blocks:
            return grads
        count = grads.shape[1] // 2
        kept = lax.dynamic_slice_in_dim(grads, section * count, count, 1)
        sent = lax.dynamic_slice_in_dim(grads, (1 - section) * count, count, 1)
        summed = (kept.astype(F32) + swap(sent).astype(F32)).astype(BF16)
        return lax.psum_scatter(summed, "dp", scatter_dimension=0, tiled=True)[0]

    dx1, small1, grad_in1, grad_out1, grads1 = backward_layer(
        1, 2, groups, copies, blocks, dy, out0, after1, wide[1], pooled, gate1, saved1, own, got
    )
    part1 = halves(grads1)
    dx0, small0, grad_in0, grad_out0, grads0 = backward_layer(
        0, 3, groups, copies, blocks, dx1, x0, after0, wide[0], pooled, gate0, saved0, own, got
    )
    part0 = halves(grads0)

    def owned(first, second):
        kept = jnp.where(first_half, first, second)
        return kept, swap(jnp.where(first_half, second, first))

    def cores_sum(first, second):
        kept, received = owned(first, second)
        return (kept.astype(F32) + received.astype(F32)).astype(BF16)

    def scattered(blocked, dim):
        return lax.psum_scatter(blocked, "dp", scatter_dimension=dim, tiled=True)

    vmem = pl.BlockSpec(memory_space=pltpu.VMEM)
    last = pl.pallas_call(
        functools.partial(last_kernel, groups, copies),
        out_shape=jax.ShapeDtypeStruct((16, width), F32),
        in_specs=[vmem],
        out_specs=vmem,
        scratch_shapes=[
            pltpu.VMEM((2, 16, width), F32),
            pltpu.VMEM((16, width), F32),
            pltpu.VMEM((groups - 1, 16, width), F32),
            pltpu.VMEM((copies - 1, 16, width), F32),
            pltpu.SemaphoreType.DMA((1,)),
            pltpu.SemaphoreType.DMA((1,)),
            pltpu.SemaphoreType.DMA((2, max(groups, copies) - 1)),
            pltpu.SemaphoreType.DMA((2, max(groups, copies) - 1)),
        ],
        compiler_params=talk(4),
        name="last_sums",
    )(jnp.stack([small0, small1]))

    gate_kept, gate_got = owned(
        jnp.stack([grad_in0, grad_out0]), jnp.stack([grad_in1, grad_out1])
    )
    gate_sum = gate_kept + gate_got

    def by_image(kept, received):
        return jnp.where(slot == 0, jnp.stack([kept, received]), jnp.stack([received, kept]))

    layer_out = by_image(*owned(out0, out1))
    input_grad = by_image(*owned(dx0, dx1))
    if copies == blocks:
        kept, received = owned(part0, part1)
        full = jnp.where(
            first_half, jnp.concatenate([kept, received]), jnp.concatenate([received, kept])
        ).astype(F32)
        qkv_grad = full[: ends[0]].reshape(3 * share // cols, cols, cols).transpose(1, 0, 2).reshape(cols, 3, share)
        out_grad = full[ends[0] : ends[1]]
        conv_grad = full[ends[1] : ends[2]]
        up_grad = full[ends[2] : ends[3]].reshape(ff // cols, cols, cols).transpose(1, 0, 2).reshape(cols, ff)
        down_grad = full[ends[3] :]
    else:
        whole = cores_sum(part0, part1)

        def by_rows(block):
            tiles = block.reshape(blocks, block.shape[1] // TILE, TILE, TILE)
            return scattered(tiles.transpose(0, 2, 1, 3).reshape(width, block.shape[1]), 0).astype(F32)

        def by_cols(block):
            return scattered(block.transpose(1, 0, 2).reshape(block.shape[1], width), 1).astype(F32)

        qkv_grad = by_rows(whole[:, : ends[0]]).reshape(cols, 3, share)
        out_grad = by_cols(whole[:, ends[0] : ends[1]])
        conv_grad = by_cols(whole[:, ends[1] : ends[2]])
        up_grad = by_rows(whole[:, ends[2] : ends[3]])
        down_grad = by_cols(whole[:, ends[3] :])
    return (
        layer_out[None],
        input_grad[None],
        last[0:2][None],
        last[2:4][None],
        qkv_grad[None],
        out_grad[None],
        up_grad[None],
        down_grad[None],
        conv_grad[None],
        last[4:13][None],
        last[13][None],
        gate_sum[0][None],
        gate_sum[1][None],
    )


def solution(mesh):
    return jax.shard_map(
        per_device,
        mesh=mesh,
        in_specs=(
            P("dp", "mp", None),
            P("dp", "mp", None),
            P("dp", "pipe", None, "mp"),
            P("dp"),
            P("dp", None),
            P("pipe", None, None),
            P("pipe", None, None),
            P("pipe", None, None, "mp"),
            P("pipe", "mp", None),
            P("pipe", None, "mp"),
            P("pipe", "mp", None),
            P("pipe", "mp", None),
            P("pipe", None, None),
            P("pipe", None),
            P("pipe", "mp", None),
            P("pipe", "mp", None),
        ),
        out_specs=(
            P("pipe", "dp", "mp", None),
            P("pipe", "dp", "mp", None),
            P("pipe", None, None),
            P("pipe", None, None),
            P("pipe", "dp", None, "mp"),
            P("pipe", "mp", "dp"),
            P("pipe", "dp", "mp"),
            P("pipe", "mp", "dp"),
            P("pipe", "mp", "dp"),
            P("pipe", None, None),
            P("pipe", None),
            P("pipe", "mp", None),
            P("pipe", "mp", None),
        ),
        check_vma=False,
    )
```

```python
import functools
import types

import jax
import jax.numpy as jnp
from jax import lax
from jax.experimental import pallas as pl
from jax.experimental.pallas import tpu as pltpu
from jax.sharding import PartitionSpec as P

GRID = 24
HEAD = 64
EPS = 1e-06
TILE = 256
VMEM_BYTES = 60 * 1024 * 1024
MESH = pl.DeviceIdType.MESH
F32 = jnp.float32
BF16 = jnp.bfloat16
SWAP = [(0, 1), (1, 0)]


def mm(a, b, ca=1, cb=0):
    return lax.dot_general(a, b, (((ca,), (cb,)), ((), ())), preferred_element_type=F32)


def tile_of(index, width=TILE):
    return pl.ds(pl.multiple_of(index * width, width), width)


def place():
    me = lax.axis_index("mp")
    col, line = lax.rem(me, 2), lax.div(me, 2)
    return me, line * 2 + 1 - col, (1 - line) * 2 + col, (1 - line) * 2 + 1 - col


def greet(peers):
    barrier = pltpu.get_barrier_semaphore()
    for peer in peers:
        pl.semaphore_signal(barrier, inc=1, device_id=peer, device_id_type=MESH)
    pl.semaphore_wait(barrier, len(peers))


def push(src, dst, send, recv, slot, peer):
    copy = pltpu.make_async_remote_copy(
        src_ref=src,
        dst_ref=dst,
        send_sem=send.at[slot],
        recv_sem=recv.at[slot],
        device_id=peer,
        device_id_type=MESH,
    )
    copy.start()
    return copy


class Gather:
    def __init__(self, buf, send, recv, spot, rows):
        me, xn, yn, dn = spot
        self.buf, self.send, self.recv, self.spot, self.rows = buf, send, recv, spot, rows
        own = buf.at[rows(me)]
        self.near = [
            push(own, own, send, recv, 0, {"mp": xn}),
            push(own, own, send, recv, 1, {"mp": yn}),
        ]

    def forward(self):
        me, xn, yn, dn = self.spot
        half = self.buf.shape[1] // 2
        self.near[0].wait_recv()
        left = self.buf.at[self.rows(xn), pl.ds(0, half)]
        first = push(left, left, self.send, self.recv, 2, {"mp": yn})
        self.near[1].wait_recv()
        right = self.buf.at[self.rows(yn), pl.ds(half, half)]
        self.far = [first, push(right, right, self.send, self.recv, 3, {"mp": xn})]

    def finish(self):
        for copy in self.far:
            copy.wait_recv()

    def drain(self):
        for copy in self.near + self.far:
            copy.wait_send()


class Scatter:
    def __init__(self, bufs, send, recv, spot):
        self.px, self.py, self.pd, self.via, self.rx, self.ry = bufs
        self.send, self.recv, self.spot = send, recv, spot
        width = self.px.shape[1]
        self.low, self.high = pl.ds(0, width // 2), pl.ds(width // 2, width // 2)

    def far(self):
        me, xn, yn, dn = self.spot
        self.far_copies = [
            push(self.pd.at[:, self.low], self.via.at[0], self.send, self.recv, 0, {"mp": xn}),
            push(self.pd.at[:, self.high], self.via.at[1], self.send, self.recv, 1, {"mp": yn}),
        ]

    def near_x(self):
        self.x_copy = push(
            self.px.at[:, self.low], self.rx.at[:, self.low], self.send, self.recv, 2, {"mp": self.spot[1]}
        )

    def near_y(self):
        self.y_copy = push(
            self.py.at[:, self.high], self.ry.at[:, self.high], self.send, self.recv, 3, {"mp": self.spot[2]}
        )

    def relay(self):
        me, xn, yn, dn = self.spot
        self.far_copies[0].wait_recv()
        self.py[:, self.low] = (self.py[:, self.low].astype(F32) + self.via[0].astype(F32)).astype(BF16)
        first = push(self.py.at[:, self.low], self.ry.at[:, self.low], self.send, self.recv, 4, {"mp": yn})
        self.far_copies[1].wait_recv()
        self.px[:, self.high] = (self.px[:, self.high].astype(F32) + self.via[1].astype(F32)).astype(BF16)
        second = push(self.px.at[:, self.high], self.rx.at[:, self.high], self.send, self.recv, 5, {"mp": xn})
        self.last_copies = [first, second]

    def total(self, own):
        for copy in [self.x_copy, self.y_copy] + self.last_copies:
            copy.wait_recv()
        return own + self.rx[...].astype(F32) + self.ry[...].astype(F32)

    def drain(self):
        for copy in self.far_copies + [self.x_copy, self.y_copy] + self.last_copies:
            copy.wait_send()


def scatter_scratch(rows, width):
    return [
        pltpu.VMEM((rows, width), BF16),
        pltpu.VMEM((rows, width), BF16),
        pltpu.VMEM((rows, width), BF16),
        pltpu.VMEM((2, rows, width // 2), BF16),
        pltpu.VMEM((rows, width), BF16),
        pltpu.VMEM((rows, width), BF16),
    ]


def norm_rows(values, gain, shift):
    center = values - jnp.mean(values, axis=-1, keepdims=True)
    spread = jnp.mean(center * center, axis=-1, keepdims=True)
    return center * lax.rsqrt(spread + EPS) * gain + shift


def norm_back(values, gain, grad):
    center = values - jnp.mean(values, axis=-1, keepdims=True)
    scale = lax.rsqrt(jnp.mean(center * center, axis=-1, keepdims=True) + EPS)
    unit = center * scale
    scaled = grad * gain
    mean_one = jnp.mean(scaled, axis=-1, keepdims=True)
    mean_two = jnp.mean(scaled * unit, axis=-1, keepdims=True)
    back = scale * (scaled - mean_one - unit * mean_two)
    return back, jnp.sum(grad * unit, axis=0, keepdims=True), jnp.sum(grad, axis=0, keepdims=True)


def gelu_parts(values):
    below = 0.5 * (1.0 + lax.erf(values * 0.7071067811865476))
    bell = jnp.exp(-0.5 * values * values) * 0.3989422804014327
    return values * below, below + values * bell


class Sum:
    def __init__(self, value, slots, send, recv, axis, count):
        self.value, self.slots = value, slots
        self.copies = [push(value, slots.at[j], send, recv, j, peer) for j, peer in enumerate(others(axis, count))]

    def finish(self):
        for copy in self.copies:
            copy.wait_recv()
        total = self.value[...]
        for j in range(len(self.copies)):
            total = total + self.slots[j]
        return total

    def drain(self):
        for copy in self.copies:
            copy.wait_send()


def others(axis, count):
    me = lax.axis_index(axis)
    return [{axis: lax.rem(me + j, count)} for j in range(1, count)]


def sum_scratch(groups, copies, width):
    most = max(groups, copies) - 1
    return [
        pltpu.VMEM((3, 1, width), F32),
        pltpu.VMEM((3, most, 1, width), F32),
        pltpu.SemaphoreType.DMA((3, most)),
        pltpu.SemaphoreType.DMA((3, most)),
    ]


class Loads:
    def __init__(self, layer, own, got, held, sems):
        self.mine = lax.axis_index("pipe") == layer
        self.own, self.got, self.held, self.sems = own, got, held, sems

    def start(self, *which):
        for i in which:

            @pl.when(self.mine)
            def _():
                pltpu.make_async_copy(self.own[i], self.held[i], self.sems.at[i]).start()

            @pl.when(jnp.logical_not(self.mine))
            def _():
                pltpu.make_async_copy(self.got[i], self.held[i], self.sems.at[i]).start()

    def wait(self, *which):
        for i in which:
            pltpu.make_async_copy(self.own[i], self.held[i], self.sems.at[i]).wait()


class Copies:
    def __init__(self, pairs, sems):
        self.copies = [pltpu.make_async_copy(src, dst, sems.at[i]) for i, (src, dst) in enumerate(pairs)]
        self.started = []

    def start(self, *which):
        for i in which:
            self.copies[i].start()
            self.started.append(i)

    def wait(self, *which):
        for i in which:
            self.copies[i].wait()
            self.started.remove(i)

    def finish(self):
        self.wait(*list(self.started))


BIAS, GAIN_ONE, GAIN_TWO, SHIFT_ONE, SHIFT_TWO = 9, 10, 11, 12, 13
QKV, OUT, UP, DOWN, CONV, GATE_IN, GATE_OUT = range(7)


def row_of(pack, index):
    return pack[index : index + 1, :]


def beside(field):
    cells, width = field.shape
    index = lax.broadcasted_iota(jnp.int32, (cells, width), 0)
    col = index - lax.shift_right_logical(index * 2731, 16) * GRID
    before = jnp.where(col >= 1, pltpu.roll(field, 1, 0), 0.0)
    behind = jnp.where(col <= GRID - 2, pltpu.roll(field, cells - 1, 0), 0.0)
    return before, field, behind


def depthwise(field, kernel):
    cells, width = field.shape
    shifted = beside(field)
    lines = [sum(kernel[3 * i + j] * shifted[j] for j in range(3)) for i in range(3)]
    none = jnp.zeros((GRID, width), F32)
    above = jnp.concatenate([none, lines[0][: cells - GRID]], axis=0)
    below = jnp.concatenate([lines[2][GRID:], none], axis=0)
    return above + lines[1] + below


def lane_halves():
    lane = lax.broadcasted_iota(jnp.int32, (1, 2 * HEAD), 1)
    return [lane < HEAD, lane >= HEAD]


def pair_slices(pair, share):
    return [slice(base + pair * 2 * HEAD, base + (pair + 1) * 2 * HEAD) for base in (0, share, 2 * share)]


class GradScatter:
    def __init__(self, r, key, layer, src):
        get = lambda name: getattr(r, key + "_" + name)
        self.src, self.layer = src, layer
        self.got, self.came, self.res = get("got"), get("came"), get("res")
        self.send, self.recv = get("send"), get("recv")
        self.core, self.z = lax.axis_index("pipe"), lax.axis_index("dp")
        half = src.shape[1] // 2
        self.mine = pl.ds(pl.multiple_of(self.core * half, 16), half)
        self.theirs = pl.ds(pl.multiple_of((1 - self.core) * half, 16), half)
        self.steps = [[self.travel(way, k) for k in range(3)] for way in range(2)]
        self.final = self.describe(self.part(self.z), self.res.at[self.core], 7, {"pipe": 1 - self.core})

    def part(self, shard):
        return self.src.at[shard, self.mine, :]

    def describe(self, src, dst, slot, peer):
        return pltpu.make_async_remote_copy(
            src_ref=src,
            dst_ref=dst,
            send_sem=self.send.at[slot],
            recv_sem=self.recv.at[slot],
            device_id=peer,
            device_id_type=MESH,
        )

    def place(self, way):
        return self.z if way == 0 else 3 - self.z

    def shard(self, way, k):
        far = lax.rem(3 - k + self.place(way), 4)
        return far if way == 0 else 3 - far

    def travel(self, way, k):
        peer = lax.rem(self.z + (1 if way == 0 else 3), 4)
        return self.describe(
            self.part(self.shard(way, k)), self.came.at[way, k], 1 + 3 * way + k, {"dp": peer}
        )

    def add(self, shard, way, k):
        self.steps[way][k].wait_recv()
        self.src[shard, self.mine, :] = (
            self.src[shard, self.mine, :].astype(F32) + self.came[way, k].astype(F32)
        ).astype(BF16)

    def begin(self):
        self.swap = push(self.src.at[:, self.theirs, :], self.got, self.send, self.recv, 0, {"pipe": 1 - self.core})

    def step(self, k):
        if k == 0:
            self.swap.wait_recv()
            for s in range(4):
                self.src[s, self.mine, :] = (
                    self.src[s, self.mine, :].astype(F32) + self.got[s].astype(F32)
                ).astype(BF16)
        for way in range(2):
            if k > 0:

                @pl.when((self.place(way) >= 1) & (self.place(way) <= k))
                def _():
                    self.add(self.shard(way, k), way, k - 1)

            @pl.when(self.place(way) <= k)
            def _():
                self.steps[way][k].start()

    def close(self):
        for way in range(2):

            @pl.when(self.place(way) >= 1)
            def _():
                self.add(self.z, way, 2)

        @pl.when(self.core == self.layer)
        def _():
            self.res[self.core] = self.src[self.z, self.mine, :]

        @pl.when(self.core != self.layer)
        def _():
            self.final.start()

    def finish(self):
        @pl.when(self.core == self.layer)
        def _():
            self.final.wait_recv()

        @pl.when(self.core != self.layer)
        def _():
            self.final.wait_send()

        for way in range(2):
            for k in range(3):

                @pl.when(self.place(way) <= k)
                def _():
                    self.steps[way][k].wait_send()

        self.swap.wait_send()


def grad_scratch(key, shards, rows, cols):
    half = rows // 2
    return {
        f"{key}_got": pltpu.VMEM((shards, half, cols), BF16),
        f"{key}_came": pltpu.VMEM((2, 3, half, cols), BF16),
        f"{key}_res": pltpu.VMEM((2, half, cols), BF16),
        f"{key}_send": pltpu.SemaphoreType.DMA((8,)),
        f"{key}_recv": pltpu.SemaphoreType.DMA((8,)),
    }


def launch(body, name, ident, near_in, far_in, near_out, far_out, scratch, flops):
    names = [*near_in, *far_in, *near_out, *far_out, *scratch]

    def kernel(*refs):
        body(types.SimpleNamespace(**dict(zip(names, refs))))

    vmem, anywhere = pl.BlockSpec(memory_space=pltpu.VMEM), pl.BlockSpec(memory_space=pl.ANY)
    outs = pl.pallas_call(
        kernel,
        out_shape=[jax.ShapeDtypeStruct(*s) for s in (*near_out.values(), *far_out.values())],
        in_specs=[vmem] * len(near_in) + [anywhere] * len(far_in),
        out_specs=[vmem] * len(near_out) + [anywhere] * len(far_out),
        scratch_shapes=list(scratch.values()),
        compiler_params=talk(ident),
        cost_estimate=pl.CostEstimate(flops=flops, bytes_accessed=40_000_000, transcendentals=0),
        name=name,
    )(*near_in.values(), *far_in.values())
    return types.SimpleNamespace(**dict(zip([*near_out, *far_out], outs)))


def forward_kernel(layer, groups, copies, *refs):
    x_ref, pack, pooled = refs[:3]
    out_ref, after_ref, gate_ref = refs[17:20]
    saved_hbm = refs[20:29]
    first, qkv, probs, mixed, second, hidden, slope, conv, depth = refs[29:38]
    weights = refs[38:45]
    wq, wo, wu, wd, wc, gate_in, gate_out = weights
    own = refs[45]
    bufs_one, bufs_two = refs[46:52], refs[52:58]
    value, slots, sum_send, sum_recv = refs[58:62]
    load_sem, save_sem, ag_send, ag_recv, rs_send, rs_recv = refs[62:]

    size, width = x_ref.shape
    tokens, share, ff = first.shape[0], mixed.shape[1], hidden.shape[1]
    spot = place()
    me, xn, yn, dn = spot

    def rows(i):
        return pl.ds(pl.multiple_of(i * size, 16), size)

    loads = Loads(layer, refs[3:10], refs[10:17], weights, load_sem)
    loads.start(CONV, QKV, OUT, GATE_IN, GATE_OUT)
    saves = Copies(list(zip((first, qkv, probs, mixed, second, hidden, slope, conv, depth), saved_hbm)), save_sem)
    greet([{"mp": xn}, {"mp": yn}, {"mp": dn}] + others("dp", copies))

    x = x_ref[...].astype(F32)
    first[rows(me), :] = norm_rows(x, row_of(pack, GAIN_ONE), row_of(pack, SHIFT_ONE)).astype(BF16)
    gather = Gather(first, ag_send.at[0], ag_recv.at[0], spot, rows)

    loads.wait(CONV)
    mapped = mm(pooled[...], wc[...])
    for t in range(width // TILE):
        lanes = slice(t * TILE, (t + 1) * TILE)
        conv[:, lanes] = mapped[:, lanes].astype(BF16)
        filtered = depthwise(mapped[:, lanes], [pack[k : k + 1, lanes] for k in range(9)])
        depth[:, lanes] = filtered.astype(BF16)
        value[0, :, lanes] = jnp.sum(filtered, axis=0, keepdims=True)
    sum_one = Sum(value.at[0], slots.at[0], sum_send.at[0], sum_recv.at[0], "mp", groups)
    saves.start(7, 8)

    def project(i):
        qkv[rows(i), :] = mm(first[rows(i), :], wq[...]).astype(BF16)

    loads.wait(QKV)
    project(me)
    gather.forward()
    loads.start(UP, DOWN)
    value[1] = sum_one.finish()
    sum_two = Sum(value.at[1], slots.at[1], sum_send.at[1], sum_recv.at[1], "dp", copies)
    project(xn)
    project(yn)
    gather.finish()
    project(dn)
    saves.start(0, 1)

    halves = lane_halves()
    for pair in range(share // (2 * HEAD)):
        at_query, at_key, at_value = pair_slices(pair, share)
        query = qkv[:, at_query] * jnp.asarray(HEAD**-0.5, BF16)
        parts = []
        for h in range(2):
            scores = mm(jnp.where(halves[h], query, jnp.zeros_like(query)), qkv[:, at_key], 1, 1)
            raised = jnp.exp(scores - jnp.max(scores, axis=-1, keepdims=True))
            chances = (raised * (1.0 / jnp.sum(raised, axis=-1, keepdims=True))).astype(BF16)
            probs[2 * pair + h] = chances
            parts.append(mm(chances, qkv[:, at_value]))
        mixed[:, at_query] = jnp.where(halves[0], parts[0], parts[1]).astype(BF16)

    loads.wait(OUT, GATE_IN, GATE_OUT)
    scatter = Scatter(bufs_one, rs_send.at[0], rs_recv.at[0], spot)

    def out_part(i):
        return mm(mixed[rows(i), :], wo[...])

    scatter.pd[...] = out_part(dn).astype(BF16)
    scatter.far()
    scatter.px[...] = out_part(xn).astype(BF16)
    scatter.near_x()
    scatter.py[...] = out_part(yn).astype(BF16)
    scatter.near_y()
    own[...] = out_part(me)
    saves.start(2, 3)
    mean = sum_two.finish() * (1.0 / (copies * tokens)) + row_of(pack, BIAS)
    level = gelu_parts(jnp.sum(gate_in[...].astype(F32) * mean, axis=1, keepdims=True))[0]
    value[2] = jnp.sum(level * gate_out[...].astype(F32), axis=0, keepdims=True)
    sum_three = Sum(value.at[2], slots.at[2], sum_send.at[2], sum_recv.at[2], "mp", groups)
    scatter.relay()
    after = x + scatter.total(own[...])
    after_ref[...] = after
    second[rows(me), :] = norm_rows(after, row_of(pack, GAIN_TWO), row_of(pack, SHIFT_TWO)).astype(BF16)
    gather.drain()
    gather = Gather(second, ag_send.at[1], ag_recv.at[1], spot, rows)
    scatter.drain()
    gate = jnp.tanh(sum_three.finish())
    gate_ref[...] = jnp.concatenate([gate, mean, jnp.zeros((6, width), F32)], axis=0)
    loads.wait(UP, DOWN)

    def feed(i):
        for t in range(ff // TILE):
            lanes = slice(t * TILE, (t + 1) * TILE)
            level, grad = gelu_parts(mm(second[rows(i), :], wu[:, lanes]))
            hidden[rows(i), lanes] = level.astype(BF16)
            slope[rows(i), lanes] = grad.astype(BF16)
        return mm(hidden[rows(i), :], wd[...]) + gate * depth[rows(i), :].astype(F32)

    scatter = Scatter(bufs_two, rs_send.at[1], rs_recv.at[1], spot)
    own[...] = feed(me)
    gather.forward()
    scatter.px[...] = feed(xn).astype(BF16)
    scatter.near_x()
    scatter.py[...] = feed(yn).astype(BF16)
    scatter.near_y()
    gather.finish()
    scatter.pd[...] = feed(dn).astype(BF16)
    scatter.far()
    saves.start(4, 5, 6)
    scatter.relay()
    out_ref[...] = (after_ref[...] + scatter.total(own[...]) + gate * row_of(pack, BIAS)).astype(BF16)
    gather.drain()
    scatter.drain()
    for one in (sum_one, sum_two, sum_three):
        one.drain()
    saves.finish()


def forward_layer(layer, ident, groups, copies, x, pack, pooled, own, got):
    size, width = x.shape
    tokens = pooled.shape[0]
    share, ff = own[OUT].shape[0], own[UP].shape[1]
    heads = share // HEAD
    vmem, anywhere = pl.BlockSpec(memory_space=pltpu.VMEM), pl.BlockSpec(memory_space=pl.ANY)
    saved = [
        ((tokens, width), BF16),
        ((tokens, 3 * share), BF16),
        ((heads, tokens, tokens), BF16),
        ((tokens, share), BF16),
        ((tokens, width), BF16),
        ((tokens, ff), BF16),
        ((tokens, ff), BF16),
        ((tokens, width), BF16),
        ((tokens, width), BF16),
    ]
    outs = pl.pallas_call(
        functools.partial(forward_kernel, layer, groups, copies),
        out_shape=[
            jax.ShapeDtypeStruct((size, width), BF16),
            jax.ShapeDtypeStruct((size, width), F32),
            jax.ShapeDtypeStruct((8, width), F32),
        ]
        + [jax.ShapeDtypeStruct(*s) for s in saved],
        in_specs=[vmem] * 3 + [anywhere] * 14,
        out_specs=[vmem] * 3 + [anywhere] * 9,
        scratch_shapes=[pltpu.VMEM(*s) for s in saved]
        + [pltpu.VMEM(w.shape, BF16) for w in own]
        + [pltpu.VMEM((size, width), F32)]
        + scatter_scratch(size, width)
        + scatter_scratch(size, width)
        + sum_scratch(groups, copies, width)
        + [
            pltpu.SemaphoreType.DMA((7,)),
            pltpu.SemaphoreType.DMA((9,)),
            pltpu.SemaphoreType.DMA((2, 4)),
            pltpu.SemaphoreType.DMA((2, 4)),
            pltpu.SemaphoreType.DMA((2, 6)),
            pltpu.SemaphoreType.DMA((2, 6)),
        ],
        compiler_params=talk(ident),
        cost_estimate=pl.CostEstimate(flops=20_000_000_000, bytes_accessed=30_000_000, transcendentals=0),
        name="layer_forward",
    )(x, pack, pooled, *own, *got)
    return outs[0], outs[1], outs[2], outs[3:]


def backward_kernel(layer, groups, copies, scatters, carried, r):
    dy_ref, x_ref, after_ref, pack, pooled, gate_ref = r.dy, r.x, r.after, r.pack, r.pooled, r.gate
    dx_ref, small_ref, grad_in, grad_out = r.dx, r.small, r.grad_in, r.grad_out
    held = [getattr(r, f"held{i}") for i in range(9)]
    first, qkv, probs, mixed, second, hidden, slope, conv, depth = held
    wq, wo, wu, wd, gate_in, gate_out = weights = [getattr(r, f"weight{i}") for i in range(6)]
    own, dyf, dhp, daf, dmixed, dqkv, dafter, grads = r.own, r.dyf, r.dhp, r.daf, r.dmixed, r.dqkv, r.dafter, r.grads
    bufs_one, bufs_two = ([getattr(r, f"buf{k}{i}") for i in range(6)] for k in range(2))
    value, slots, sum_send, sum_recv = r.value, r.slots, r.sum_send, r.sum_recv
    ag_send, ag_recv, rs_send, rs_recv = r.ag_send, r.ag_recv, r.rs_send, r.rs_recv

    size, width = dy_ref.shape
    tokens, share, ff = first.shape[0], mixed.shape[1], hidden.shape[1]
    channels = pooled.shape[1]
    shards = grads.shape[0]
    cols = width // shards
    spot = place()
    me, xn, yn, dn = spot
    base_out = 3 * share
    base_conv = base_out + share
    base_up = base_conv + channels
    base_down = base_up + ff

    def rows(i):
        return pl.ds(pl.multiple_of(i * size, 16), size)

    def by_rows(base, grad, s):
        for t in range(grad.shape[1] // cols):
            grads[s, base + t * cols : base + (t + 1) * cols, :] = grad[:, t * cols : (t + 1) * cols].astype(BF16)

    def by_cols(base, grad):
        for s in range(shards):
            grads[s, base : base + grad.shape[0], :] = grad[:, s * cols : (s + 1) * cols].astype(BF16)

    own_w, got_w = ([getattr(r, f"{k}{i}") for i in BACK_WEIGHTS] for k in ("mine", "got"))
    loads = Loads(layer, own_w, got_w, weights, r.load_sem)
    saved = Copies([(getattr(r, f"saved{i}"), held[i]) for i in range(9)], r.saved_sem)
    saved.start(6)
    loads.start(3, 2)
    peers = [{"mp": xn}, {"mp": yn}, {"mp": dn}] + others("dp", copies)
    if scatters:
        saves = Copies([(grads.at[:, :base_down, :], r.late_out)], r.save_sem)
        peers.append({"pipe": 1 - lax.axis_index("pipe")})
        piece = GradScatter(r, "down", layer, grads.at[:, base_down : base_down + ff, :])
        if carried:
            late = GradScatter(r, "late", 1 - layer, r.late_held.at[:, :base_up, :])
            up = GradScatter(r, "up", 1 - layer, r.late_held.at[:, base_up:base_down, :])
            late_load = pltpu.make_async_copy(r.late_in, r.late_held, r.late_sem.at[0])
            late_load.start()
    else:
        saves = Copies([(grads, r.grads_out)], r.save_sem)
    greet(peers)

    dyf[rows(me), :] = dy_ref[...]
    gather = Gather(dyf, ag_send.at[0], ag_recv.at[0], spot, rows)
    scatter = Scatter(bufs_one, rs_send.at[0], rs_recv.at[0], spot)
    dy = dy_ref[...].astype(F32)
    dy_bias = jnp.sum(dy, axis=0, keepdims=True) * row_of(pack, BIAS)
    small_ref[...] = jnp.zeros_like(small_ref)
    saved.wait(6)
    loads.wait(3, 2)

    def feed_back(i):
        for t in range(ff // TILE):
            lanes = slice(t * TILE, (t + 1) * TILE)
            back = mm(dyf[rows(i), :], wd[lanes, :], 1, 1)
            dhp[rows(i), lanes] = (back * slope[rows(i), lanes].astype(F32)).astype(BF16)
        return mm(dhp[rows(i), :], wu[...], 1, 1)

    if carried:
        late_load.wait()
        late.begin()
        up.begin()
    own[...] = feed_back(me)
    saved.start(5, 8, 4)
    if carried:
        late.step(0)
    gather.forward()
    scatter.px[...] = feed_back(xn).astype(BF16)
    scatter.near_x()
    scatter.py[...] = feed_back(yn).astype(BF16)
    scatter.near_y()
    if carried:
        up.step(0)
    loads.start(1, 0, 4, 5)
    saved.start(1, 2, 3, 0, 7)
    gather.finish()
    scatter.pd[...] = feed_back(dn).astype(BF16)
    scatter.far()
    saved.wait(8)
    value[0] = dy_bias + jnp.sum(dyf[...].astype(F32) * depth[...].astype(F32), axis=0, keepdims=True)
    sum_one = Sum(value.at[0], slots.at[0], sum_send.at[0], sum_recv.at[0], "mp", groups)
    saved.wait(5)
    by_cols(base_down, mm(hidden[...], dyf[...], 0, 0))
    if scatters:
        piece.begin()
    if carried:
        late.step(1)
    scatter.relay()
    value[1] = sum_one.finish()
    sum_two = Sum(value.at[1], slots.at[1], sum_send.at[1], sum_recv.at[1], "dp", copies)
    saved.wait(4)
    for s in range(shards):
        by_rows(base_up, mm(second[:, s * cols : (s + 1) * cols], dhp[...], 0, 0), s)
    if scatters:
        piece.step(0)
    if carried:
        up.step(1)
    back, gain_grad, bias_grad = norm_back(after_ref[...], row_of(pack, GAIN_TWO), scatter.total(own[...]))
    small_ref[1:2, :] = gain_grad
    small_ref[3:4, :] = bias_grad
    dafter[...] = dy + back
    daf[rows(me), :] = dafter[...].astype(BF16)
    gather.drain()
    gather = Gather(daf, ag_send.at[1], ag_recv.at[1], spot, rows)
    scatter.drain()
    scatter = Scatter(bufs_two, rs_send.at[1], rs_recv.at[1], spot)

    loads.wait(4, 5, 1)
    gate, mean = gate_ref[0:1, :], gate_ref[1:2, :]
    pre = sum_two.finish() * (1.0 - gate * gate)
    level, steep = gelu_parts(jnp.sum(gate_in[...].astype(F32) * mean, axis=1, keepdims=True))
    inner = jnp.sum(gate_out[...].astype(F32) * pre, axis=1, keepdims=True) * steep
    grad_out[...] = level * pre
    grad_in[...] = inner * mean
    value[2] = jnp.sum(gate_in[...].astype(F32) * inner, axis=0, keepdims=True)
    sum_three = Sum(value.at[2], slots.at[2], sum_send.at[2], sum_recv.at[2], "mp", groups)

    def mix_back(i):
        dmixed[rows(i), :] = mm(daf[rows(i), :], wo[...], 1, 1).astype(BF16)

    mix_back(me)
    gather.forward()
    mix_back(xn)
    mix_back(yn)
    if carried:
        late.step(2)
    elif scatters:
        piece.step(1)
    mean_grad = sum_three.finish() * (1.0 / (copies * tokens))
    saved.wait(7)
    for t in range(shards):
        lanes = slice(t * cols, (t + 1) * cols)
        grad = gate[:, lanes] * dyf[:, lanes].astype(F32) + mean_grad[:, lanes]
        shifted = beside(conv[:, lanes].astype(F32))
        for i in range(3):
            for j in range(3):
                if i == 0:
                    terms = shifted[j][: tokens - GRID] * grad[GRID:]
                elif i == 1:
                    terms = shifted[j] * grad
                else:
                    terms = shifted[j][GRID:] * grad[: tokens - GRID]
                small_ref[4 + 3 * i + j : 5 + 3 * i + j, lanes] = jnp.sum(terms, axis=0, keepdims=True)
        small_ref[13:14, lanes] = jnp.sum(grad, axis=0, keepdims=True) * (1.0 / groups)
        back = depthwise(grad, [pack[8 - k : 9 - k, lanes] for k in range(9)])
        grads[t, base_conv : base_conv + channels, :] = mm(pooled[...], back.astype(BF16), 0, 0).astype(BF16)
    gather.finish()
    mix_back(dn)
    if carried:
        up.step(2)
        piece.step(1)
    elif scatters:
        piece.step(2)

    saved.wait(1, 2)
    halves = lane_halves()
    scale = HEAD**-0.5
    for pair in range(share // (2 * HEAD)):
        at_query, at_key, at_value = pair_slices(pair, share)
        upper = dmixed[:, at_query]
        parts, key_grads, value_grads = [], [], []
        for h in range(2):
            low = probs[2 * pair + h]
            exact = low.astype(F32)
            grad_probs = mm(jnp.where(halves[h], upper, jnp.zeros_like(upper)), qkv[:, at_value], 1, 1)
            delta = jnp.sum(exact * grad_probs, axis=-1, keepdims=True)
            grad_scores = (exact * (grad_probs - delta)).astype(BF16)
            parts.append(mm(grad_scores, qkv[:, at_key]))
            key_grads.append(mm(grad_scores, qkv[:, at_query], 0, 0))
            value_grads.append(mm(low, upper, 0, 0))
        dqkv[:, at_query] = (jnp.where(halves[0], parts[0], parts[1]) * scale).astype(BF16)
        dqkv[:, at_key] = (jnp.where(halves[0], key_grads[0], key_grads[1]) * scale).astype(BF16)
        dqkv[:, at_value] = jnp.where(halves[0], value_grads[0], value_grads[1]).astype(BF16)
    loads.wait(0)

    def first_back(i):
        return mm(dqkv[rows(i), :], wq[...], 1, 1)

    scatter.pd[...] = first_back(dn).astype(BF16)
    scatter.far()
    scatter.px[...] = first_back(xn).astype(BF16)
    scatter.near_x()
    scatter.py[...] = first_back(yn).astype(BF16)
    scatter.near_y()
    own[...] = first_back(me)
    saved.wait(3)
    by_cols(base_out, mm(mixed[...], daf[...], 0, 0))
    if carried:
        piece.step(2)
        late.close()
    scatter.relay()
    saved.wait(0)
    for s in range(shards):
        by_rows(0, mm(first[:, s * cols : (s + 1) * cols], dqkv[...], 0, 0), s)
    saves.start(0)
    back, gain_grad, bias_grad = norm_back(
        x_ref[...].astype(F32), row_of(pack, GAIN_ONE), scatter.total(own[...])
    )
    small_ref[0:1, :] = gain_grad
    small_ref[2:3, :] = bias_grad
    dx_ref[...] = (dafter[...] + back).astype(BF16)
    if scatters:
        if carried:
            up.close()
        piece.close()
    gather.drain()
    scatter.drain()
    for one in (sum_one, sum_two, sum_three):
        one.drain()
    saves.finish()
    if scatters:
        done = [(piece, r.down_out, layer)]
        if carried:
            done += [(late, r.late_sum, 1 - layer), (up, r.up_sum, 1 - layer)]
        for i, (piece, out, owner) in enumerate(done):
            piece.finish()

            @pl.when(lax.axis_index("pipe") == owner)
            def _():
                copy = pltpu.make_async_copy(piece.res, out, r.done_sem.at[i])
                copy.start()
                copy.wait()


BACK_WEIGHTS = (QKV, OUT, UP, DOWN, GATE_IN, GATE_OUT)


def backward_layer(layer, ident, groups, copies, scatters, dy, x, after, pack, pooled, gate, saved, own, got, late=None):
    size, width = dy.shape
    tokens, channels = pooled.shape
    share, ff = own[OUT].shape[0], own[UP].shape[1]
    hidden = own[GATE_IN].shape[0]
    shards = width // TILE
    late_rows = 4 * share + channels
    grads_shape = (shards, late_rows + 2 * ff, TILE)
    late_shape = (shards, late_rows + ff, TILE)
    carried = late is not None
    far_in = {f"saved{i}": s for i, s in enumerate(saved)}
    far_in |= {f"mine{i}": own[i] for i in BACK_WEIGHTS} | {f"got{i}": got[i] for i in BACK_WEIGHTS}
    scratch = {f"held{i}": pltpu.VMEM(s.shape, s.dtype) for i, s in enumerate(saved)}
    scratch |= {f"weight{k}": pltpu.VMEM(own[i].shape, BF16) for k, i in enumerate(BACK_WEIGHTS)}
    for k in range(2):
        scratch |= {f"buf{k}{i}": buf for i, buf in enumerate(scatter_scratch(size, width))}
    scratch |= {
        "own": pltpu.VMEM((size, width), F32),
        "dyf": pltpu.VMEM((tokens, width), BF16),
        "dhp": pltpu.VMEM((tokens, ff), BF16),
        "daf": pltpu.VMEM((tokens, width), BF16),
        "dmixed": pltpu.VMEM((tokens, share), BF16),
        "dqkv": pltpu.VMEM((tokens, 3 * share), BF16),
        "dafter": pltpu.VMEM((size, width), F32),
        "grads": pltpu.VMEM(grads_shape, BF16),
        "load_sem": pltpu.SemaphoreType.DMA((6,)),
        "saved_sem": pltpu.SemaphoreType.DMA((9,)),
        "save_sem": pltpu.SemaphoreType.DMA((1,)),
        "ag_send": pltpu.SemaphoreType.DMA((2, 4)),
        "ag_recv": pltpu.SemaphoreType.DMA((2, 4)),
        "rs_send": pltpu.SemaphoreType.DMA((2, 6)),
        "rs_recv": pltpu.SemaphoreType.DMA((2, 6)),
    }
    scratch |= dict(zip(("value", "slots", "sum_send", "sum_recv"), sum_scratch(groups, copies, width)))
    if scatters:
        far_out = {"late_out": (late_shape, BF16)}
        far_out |= {"down_out": ((2, ff // 2, TILE), BF16)}
        scratch |= grad_scratch("down", shards, ff, TILE)
        scratch |= {"done_sem": pltpu.SemaphoreType.DMA((3,))}
        if carried:
            far_in |= {"late_in": late}
            far_out |= {"late_sum": ((2, late_rows // 2, TILE), BF16), "up_sum": ((2, ff // 2, TILE), BF16)}
            scratch |= grad_scratch("late", shards, late_rows, TILE) | grad_scratch("up", shards, ff, TILE)
            scratch |= {"late_held": pltpu.VMEM(late_shape, BF16), "late_sem": pltpu.SemaphoreType.DMA((1,))}
    else:
        far_out = {"grads_out": (grads_shape, BF16)}
    return launch(
        functools.partial(backward_kernel, layer, groups, copies, scatters, carried),
        "layer_backward",
        ident,
        dict(dy=dy, x=x, after=after, pack=pack, pooled=pooled, gate=gate),
        far_in,
        dict(
            dx=((size, width), BF16),
            small=((16, width), F32),
            grad_in=((hidden, width), F32),
            grad_out=((hidden, width), F32),
        ),
        far_out,
        scratch,
        40_000_000_000,
    )


def last_kernel(groups, copies, share, channels, r):
    core = lax.axis_index("pipe")
    mine = core == 0
    split = 2 * r.late_res.shape[1]
    piece = GradScatter(r, "late", 0, r.late_held.at[:, :split, :])
    up = GradScatter(r, "up", 0, r.late_held.at[:, split:, :])
    late_load = pltpu.make_async_copy(r.late_in, r.late_held, r.load_sem.at[0])
    late_load.start()
    @pl.when(mine)
    def _():
        pltpu.make_async_copy(r.down0, r.down_held, r.load_sem.at[1]).start()

    others_loads = [
        pltpu.make_async_copy(r.late1, piece.res, r.load_sem.at[2]),
        pltpu.make_async_copy(r.up1, up.res, r.load_sem.at[3]),
    ]

    @pl.when(jnp.logical_not(mine))
    def _():
        pltpu.make_async_copy(r.down1, r.down_held, r.load_sem.at[1]).start()
        for load in others_loads:
            load.start()

    other = {"pipe": 1 - core}
    greet([other] + others("mp", groups) + others("dp", copies))
    r.small_stage[...] = jnp.where(mine, r.small1[...], r.small0[...])
    small_copy = push(r.small_stage, r.small_got, r.core_send, r.core_recv, 0, other)
    r.gate_stage[0] = jnp.where(mine, r.grad_in1[...], r.grad_in0[...])
    r.gate_stage[1] = jnp.where(mine, r.grad_out1[...], r.grad_out0[...])
    gate_copy = push(r.gate_stage, r.gate_got, r.core_send, r.core_recv, 1, other)
    late_load.wait()
    piece.begin()
    up.begin()
    small_copy.wait_recv()
    r.value[0] = jnp.where(mine, r.small0[...], r.small1[...]) + r.small_got[...]
    over_groups = Sum(r.value.at[0], r.slot_a, r.sum_send.at[0], r.sum_recv.at[0], "mp", groups)
    piece.step(0)
    up.step(0)
    gate_copy.wait_recv()
    r.gate_in_grad[...] = jnp.where(mine, r.grad_in0[...], r.grad_in1[...]) + r.gate_got[0]
    r.gate_out_grad[...] = jnp.where(mine, r.grad_out0[...], r.grad_out1[...]) + r.gate_got[1]
    r.value[1] = over_groups.finish()
    over_copies = Sum(r.value.at[1], r.slot_b, r.sum_send.at[1], r.sum_recv.at[1], "dp", copies)
    pltpu.make_async_copy(r.down0, r.down_held, r.load_sem.at[1]).wait()
    half = r.down_held.shape[1]
    cols = r.down_held.shape[2]
    for k in range(2):
        r.down_grad[k * half : (k + 1) * half, :] = r.down_held[k].astype(F32)
    piece.step(1)
    up.step(1)
    total = over_copies.finish()
    r.gain_grad[...] = total[0:2]
    r.shift_grad[...] = total[2:4]
    r.depth_grad[...] = total[4:13]
    r.bias_grad[...] = total[13:14]
    piece.step(2)
    up.step(2)
    piece.close()
    up.close()

    @pl.when(jnp.logical_not(mine))
    def _():
        for load in others_loads:
            load.wait()

    piece.finish()
    up.finish()
    for k in range(2):
        for t in range(half // cols):
            lanes = slice((k * (half // cols) + t) * cols, (k * (half // cols) + t + 1) * cols)
            r.up_grad[:, lanes] = up.res[k, t * cols : (t + 1) * cols, :].astype(F32)
    half = piece.res.shape[1]

    def put(base, count, store):
        at = base
        while at < base + count:
            stop = min(base + count, (at // half + 1) * half)
            store(at - base, stop - at, piece.res[at // half, at % half : at % half + stop - at, :].astype(F32))
            at = stop

    for k in range(3):

        def store(at, count, rows):
            r.qkv_grad[at : at + count, k, :] = rows

        put(k * cols, cols, store)

    def store_out(at, count, rows):
        r.out_grad[at : at + count, :] = rows

    def store_conv(at, count, rows):
        r.conv_grad[at : at + count, :] = rows

    put(3 * share, share, store_out)
    put(4 * share, channels, store_conv)
    small_copy.wait_send()
    gate_copy.wait_send()
    over_groups.drain()
    over_copies.drain()


def last_sums(ident, groups, copies, share, channels, back0, back1):
    shards, all_rows, cols = back0.late_out.shape
    width = shards * cols
    ff = 2 * back0.down_out.shape[1]
    late_rows = all_rows - ff
    hidden = back0.grad_in.shape[0]
    most = max(groups, copies) - 1
    small = (16, width)
    scratch = grad_scratch("late", shards, late_rows, cols) | grad_scratch("up", shards, ff, cols)
    scratch |= {
        "late_held": pltpu.VMEM((shards, all_rows, cols), BF16),
        "down_held": pltpu.VMEM((2, ff // 2, cols), BF16),
        "small_stage": pltpu.VMEM(small, F32),
        "small_got": pltpu.VMEM(small, F32),
        "gate_stage": pltpu.VMEM((2, hidden, width), F32),
        "gate_got": pltpu.VMEM((2, hidden, width), F32),
        "value": pltpu.VMEM((2, *small), F32),
        "slot_a": pltpu.VMEM((groups - 1, *small), F32),
        "slot_b": pltpu.VMEM((copies - 1, *small), F32),
        "load_sem": pltpu.SemaphoreType.DMA((4,)),
        "core_send": pltpu.SemaphoreType.DMA((2,)),
        "core_recv": pltpu.SemaphoreType.DMA((2,)),
        "sum_send": pltpu.SemaphoreType.DMA((2, most)),
        "sum_recv": pltpu.SemaphoreType.DMA((2, most)),
    }
    near_in = {}
    for k, back in enumerate((back0, back1)):
        near_in |= {f"small{k}": back.small, f"grad_in{k}": back.grad_in, f"grad_out{k}": back.grad_out}
    far_in = dict(late_in=back0.late_out, late1=back0.late_sum, up1=back0.up_sum)
    far_in |= dict(down0=back0.down_out, down1=back1.down_out)
    return launch(
        functools.partial(last_kernel, groups, copies, share, channels),
        "last_sums",
        ident,
        near_in,
        far_in,
        dict(
            gain_grad=((2, width), F32),
            shift_grad=((2, width), F32),
            qkv_grad=((cols, 3, share), F32),
            out_grad=((share, cols), F32),
            up_grad=((cols, ff), F32),
            down_grad=((ff, cols), F32),
            conv_grad=((channels, cols), F32),
            depth_grad=((9, width), F32),
            bias_grad=((1, width), F32),
            gate_in_grad=((hidden, width), F32),
            gate_out_grad=((hidden, width), F32),
        ),
        {},
        scratch,
        1_000_000_000,
    )


def talk(ident):
    return pltpu.CompilerParams(collective_id=ident, has_side_effects=True, vmem_limit_bytes=VMEM_BYTES)


def pool_weights(side, count, offset):
    rows_index = jnp.arange(GRID, dtype=jnp.int32)[:, None]
    cols_index = jnp.arange(count, dtype=jnp.int32)[None, :] + offset
    lower = rows_index * side // GRID
    upper = ((rows_index + 1) * side + GRID - 1) // GRID
    inside = (cols_index >= lower) & (cols_index < upper)
    return jnp.where(inside, 1.0 / (upper - lower).astype(F32), 0.0)


def pool_partial(feature, pixels, row_start):
    side = pixels * GRID // 768
    row_matrix = pool_weights(side, feature.shape[0], row_start)
    col_matrix = pool_weights(side, feature.shape[1], 0)
    first = jnp.einsum("ia,abc->ibc", row_matrix.astype(BF16), feature, preferred_element_type=F32)
    second = jnp.einsum("jb,ibc->ijc", col_matrix, first, precision=lax.Precision.HIGHEST)
    return second.reshape(GRID * GRID, feature.shape[2])


def per_device(
    inputs, cotangent, highres, resolution, assign, norm_gain, norm_bias, qkv_weight, out_weight, up_weight,
    down_weight, conv_weight, depth_weight, depth_bias, gate_in, gate_out,
):
    section = lax.axis_index("pipe")
    groups, copies = lax.axis_size("mp"), lax.axis_size("dp")
    first_half = section == 0
    order = assign[0]
    slot, other_slot = order[section], order[1 - section]

    def swap(block):
        return lax.ppermute(block, "pipe", SWAP)

    def both(own):
        got = swap(own)
        return jnp.stack([jnp.where(first_half, own, got), jnp.where(first_half, got, own)])

    def pick(array, index):
        return lax.dynamic_index_in_dim(array, index, 0, keepdims=False)

    width = inputs.shape[2]
    share, channels, ff = out_weight.shape[1], conv_weight.shape[1], up_weight.shape[2]
    wide = both(
        jnp.concatenate(
            [depth_weight[0], depth_bias, norm_gain[0], norm_bias[0], jnp.zeros((2, width), F32)], axis=0
        )
    )
    own = (
        qkv_weight[0].reshape(width, 3 * share), out_weight[0], up_weight[0], down_weight[0], conv_weight[0],
        gate_in[0], gate_out[0],
    )
    got = tuple(swap(w) for w in own)

    row_start = section * highres.shape[1]
    parts = jax.vmap(pool_partial, in_axes=(0, 0, None))(highres, resolution, row_start).astype(BF16)
    pooled = pick(parts, slot) + swap(pick(parts, other_slot))

    x0 = pick(inputs, slot)
    out0, after0, gate0, saved0 = forward_layer(0, 0, groups, copies, x0, wide[0], pooled, own, got)
    out1, after1, gate1, saved1 = forward_layer(1, 1, groups, copies, out0, wide[1], pooled, own, got)
    dy = pick(cotangent, slot)
    scatters = copies == 4 and width // TILE == copies
    back1 = backward_layer(
        1, 2, groups, copies, scatters, dy, out0, after1, wide[1], pooled, gate1, saved1, own, got
    )
    back0 = backward_layer(
        0, 3, groups, copies, scatters, back1.dx, x0, after0, wide[0], pooled, gate0, saved0, own, got,
        back1.late_out if scatters else None,
    )

    def owned(first, second):
        kept = jnp.where(first_half, first, second)
        return kept, swap(jnp.where(first_half, second, first))

    def by_image(first, second):
        kept, received = owned(first, second)
        return jnp.where(slot == 0, jnp.stack([kept, received]), jnp.stack([received, kept]))[None]

    layer_out, input_grad = by_image(out0, out1), by_image(back0.dx, back1.dx)
    if scatters:
        last = last_sums(4, groups, copies, share, channels, back0, back1)
        return (
            layer_out,
            input_grad,
            last.gain_grad[None],
            last.shift_grad[None],
            last.qkv_grad[None],
            last.out_grad[None],
            last.up_grad[None],
            last.down_grad[None],
            last.conv_grad[None],
            last.depth_grad[None],
            last.bias_grad,
            last.gate_in_grad[None],
            last.gate_out_grad[None],
        )

    cols, blocks = width // copies, width // TILE
    ends = [3 * share, 4 * share, 4 * share + channels, 4 * share + channels + ff]

    def cores_sum(first, second, kind):
        kept, received = owned(first, second)
        return (kept.astype(F32) + received.astype(F32)).astype(kind)

    def scattered(blocked, dim):
        return lax.psum_scatter(blocked, "dp", scatter_dimension=dim, tiled=True).astype(F32)

    def by_rows(block):
        tiles = block.reshape(blocks, block.shape[1] // TILE, TILE, TILE)
        return scattered(tiles.transpose(0, 2, 1, 3).reshape(width, block.shape[1]), 0)

    def by_cols(block):
        return scattered(block.transpose(1, 0, 2).reshape(block.shape[1], width), 1)

    whole = cores_sum(back0.grads_out, back1.grads_out, BF16)
    small = lax.psum(cores_sum(back0.small, back1.small, F32), ("dp", "mp"))
    return (
        layer_out,
        input_grad,
        small[0:2][None],
        small[2:4][None],
        by_rows(whole[:, : ends[0]]).reshape(cols, 3, share)[None],
        by_cols(whole[:, ends[0] : ends[1]])[None],
        by_rows(whole[:, ends[2] : ends[3]])[None],
        by_cols(whole[:, ends[3] :])[None],
        by_cols(whole[:, ends[1] : ends[2]])[None],
        small[4:13][None],
        small[13][None],
        cores_sum(back0.grad_in, back1.grad_in, F32)[None],
        cores_sum(back0.grad_out, back1.grad_out, F32)[None],
    )


def solution(mesh):
    return jax.shard_map(
        per_device,
        mesh=mesh,
        in_specs=(
            P("dp", "mp", None),
            P("dp", "mp", None),
            P("dp", "pipe", None, "mp"),
            P("dp"),
            P("dp", None),
            P("pipe", None, None),
            P("pipe", None, None),
            P("pipe", None, None, "mp"),
            P("pipe", "mp", None),
            P("pipe", None, "mp"),
            P("pipe", "mp", None),
            P("pipe", "mp", None),
            P("pipe", None, None),
            P("pipe", None),
            P("pipe", "mp", None),
            P("pipe", "mp", None),
        ),
        out_specs=(
            P("pipe", "dp", "mp", None),
            P("pipe", "dp", "mp", None),
            P("pipe", None, None),
            P("pipe", None, None),
            P("pipe", "dp", None, "mp"),
            P("pipe", "mp", "dp"),
            P("pipe", "dp", "mp"),
            P("pipe", "mp", "dp"),
            P("pipe", "mp", "dp"),
            P("pipe", None, None),
            P("pipe", None),
            P("pipe", "mp", None),
            P("pipe", "mp", None),
        ),
        check_vma=False,
    )
```

```python
import functools
import types

import jax
import jax.numpy as jnp
from jax import lax
from jax.experimental import pallas as pl
from jax.experimental.pallas import tpu as pltpu
from jax.sharding import PartitionSpec as P

GRID = 24
HEAD = 64
EPS = 1e-06
TILE = 256
VMEM_BYTES = 60 * 1024 * 1024
MESH = pl.DeviceIdType.MESH
F32 = jnp.float32
BF16 = jnp.bfloat16
SWAP = [(0, 1), (1, 0)]


def mm(a, b, ca=1, cb=0):
    return lax.dot_general(a, b, (((ca,), (cb,)), ((), ())), preferred_element_type=F32)


def tile_of(index, width=TILE):
    return pl.ds(pl.multiple_of(index * width, width), width)


def place():
    me = lax.axis_index("mp")
    col, line = lax.rem(me, 2), lax.div(me, 2)
    return me, line * 2 + 1 - col, (1 - line) * 2 + col, (1 - line) * 2 + 1 - col


def greet(peers):
    barrier = pltpu.get_barrier_semaphore()
    for peer in peers:
        pl.semaphore_signal(barrier, inc=1, device_id=peer, device_id_type=MESH)
    pl.semaphore_wait(barrier, len(peers))


def push(src, dst, send, recv, slot, peer):
    copy = pltpu.make_async_remote_copy(
        src_ref=src,
        dst_ref=dst,
        send_sem=send.at[slot],
        recv_sem=recv.at[slot],
        device_id=peer,
        device_id_type=MESH,
    )
    copy.start()
    return copy


class Gather:
    def __init__(self, buf, send, recv, spot, rows):
        me, xn, yn, dn = spot
        half = buf.shape[1] // 2
        self.buf, self.send, self.recv, self.spot, self.rows = buf, send, recv, spot, rows
        self.low, self.high = pl.ds(0, half), pl.ds(half, half)
        self.near = [
            self.push(me, self.low, 0, xn),
            self.push(me, self.high, 1, yn),
            self.push(me, self.high, 2, xn),
            self.push(me, self.low, 3, yn),
        ]

    def push(self, block, half, slot, peer):
        part = self.buf.at[self.rows(block), half]
        return push(part, part, self.send, self.recv, slot, {"mp": peer})

    def forward(self):
        me, xn, yn, dn = self.spot
        self.near[0].wait_recv()
        first = self.push(xn, self.low, 4, yn)
        self.near[1].wait_recv()
        self.far = [first, self.push(yn, self.high, 5, xn)]
        self.near[2].wait_recv()
        self.near[3].wait_recv()

    def finish(self):
        for copy in self.far:
            copy.wait_recv()

    def drain(self):
        for copy in self.near + self.far:
            copy.wait_send()


class Scatter:
    def __init__(self, bufs, send, recv, spot):
        self.px, self.py, self.pd, self.via, self.rx, self.ry = bufs
        self.send, self.recv, self.spot = send, recv, spot
        width = self.px.shape[1]
        self.low, self.high = pl.ds(0, width // 2), pl.ds(width // 2, width // 2)

    def far(self):
        me, xn, yn, dn = self.spot
        self.far_copies = [
            push(self.pd.at[:, self.low], self.via.at[0], self.send, self.recv, 0, {"mp": xn}),
            push(self.pd.at[:, self.high], self.via.at[1], self.send, self.recv, 1, {"mp": yn}),
        ]

    def near_x(self):
        self.x_copy = push(
            self.px.at[:, self.low], self.rx.at[:, self.low], self.send, self.recv, 2, {"mp": self.spot[1]}
        )

    def near_y(self):
        self.y_copy = push(
            self.py.at[:, self.high], self.ry.at[:, self.high], self.send, self.recv, 3, {"mp": self.spot[2]}
        )

    def relay(self):
        me, xn, yn, dn = self.spot
        self.far_copies[0].wait_recv()
        self.py[:, self.low] = (self.py[:, self.low].astype(F32) + self.via[0].astype(F32)).astype(BF16)
        first = push(self.py.at[:, self.low], self.ry.at[:, self.low], self.send, self.recv, 4, {"mp": yn})
        self.far_copies[1].wait_recv()
        self.px[:, self.high] = (self.px[:, self.high].astype(F32) + self.via[1].astype(F32)).astype(BF16)
        second = push(self.px.at[:, self.high], self.rx.at[:, self.high], self.send, self.recv, 5, {"mp": xn})
        self.last_copies = [first, second]

    def total(self, own):
        for copy in [self.x_copy, self.y_copy] + self.last_copies:
            copy.wait_recv()
        return own + self.rx[...].astype(F32) + self.ry[...].astype(F32)

    def drain(self):
        for copy in self.far_copies + [self.x_copy, self.y_copy] + self.last_copies:
            copy.wait_send()


def scatter_scratch(rows, width):
    return [
        pltpu.VMEM((rows, width), BF16),
        pltpu.VMEM((rows, width), BF16),
        pltpu.VMEM((rows, width), BF16),
        pltpu.VMEM((2, rows, width // 2), BF16),
        pltpu.VMEM((rows, width), BF16),
        pltpu.VMEM((rows, width), BF16),
    ]


def norm_rows(values, gain, shift):
    center = values - jnp.mean(values, axis=-1, keepdims=True)
    spread = jnp.mean(center * center, axis=-1, keepdims=True)
    return center * lax.rsqrt(spread + EPS) * gain + shift


def norm_back(values, gain, grad):
    center = values - jnp.mean(values, axis=-1, keepdims=True)
    scale = lax.rsqrt(jnp.mean(center * center, axis=-1, keepdims=True) + EPS)
    unit = center * scale
    scaled = grad * gain
    mean_one = jnp.mean(scaled, axis=-1, keepdims=True)
    mean_two = jnp.mean(scaled * unit, axis=-1, keepdims=True)
    back = scale * (scaled - mean_one - unit * mean_two)
    return back, jnp.sum(grad * unit, axis=0, keepdims=True), jnp.sum(grad, axis=0, keepdims=True)


def gelu_parts(values):
    below = 0.5 * (1.0 + lax.erf(values * 0.7071067811865476))
    bell = jnp.exp(-0.5 * values * values) * 0.3989422804014327
    return values * below, below + values * bell


class Sum:
    def __init__(self, value, slots, send, recv, axis, count):
        self.value, self.slots = value, slots
        self.copies = [push(value, slots.at[j], send, recv, j, peer) for j, peer in enumerate(others(axis, count))]

    def finish(self):
        for copy in self.copies:
            copy.wait_recv()
        total = self.value[...]
        for j in range(len(self.copies)):
            total = total + self.slots[j]
        return total

    def drain(self):
        for copy in self.copies:
            copy.wait_send()


def others(axis, count):
    me = lax.axis_index(axis)
    return [{axis: lax.rem(me + j, count)} for j in range(1, count)]


def sum_scratch(groups, copies, width):
    most = max(groups, copies) - 1
    return dict(
        value=pltpu.VMEM((3, 1, width), F32),
        slots=pltpu.VMEM((3, most, 1, width), F32),
        sum_send=pltpu.SemaphoreType.DMA((3, most)),
        sum_recv=pltpu.SemaphoreType.DMA((3, most)),
    )


class Loads:
    def __init__(self, layer, own, got, held, sems):
        self.mine = lax.axis_index("pipe") == layer
        self.own, self.got, self.held, self.sems = own, got, held, sems

    def start(self, *which):
        for i in which:

            @pl.when(self.mine)
            def _():
                pltpu.make_async_copy(self.own[i], self.held[i], self.sems.at[i]).start()

            @pl.when(jnp.logical_not(self.mine))
            def _():
                pltpu.make_async_copy(self.got[i], self.held[i], self.sems.at[i]).start()

    def wait(self, *which):
        for i in which:
            pltpu.make_async_copy(self.own[i], self.held[i], self.sems.at[i]).wait()


class Copies:
    def __init__(self, pairs, sems):
        self.copies = [pltpu.make_async_copy(src, dst, sems.at[i]) for i, (src, dst) in enumerate(pairs)]
        self.started = []

    def start(self, *which):
        for i in which:
            self.copies[i].start()
            self.started.append(i)

    def wait(self, *which):
        for i in which:
            self.copies[i].wait()
            self.started.remove(i)

    def finish(self):
        self.wait(*list(self.started))


BIAS, GAIN_ONE, GAIN_TWO, SHIFT_ONE, SHIFT_TWO = 9, 10, 11, 12, 13
QKV, OUT, UP, DOWN, CONV, GATE_IN, GATE_OUT = range(7)


def row_of(pack, index):
    return pack[index : index + 1, :]


def beside(field):
    cells, width = field.shape
    index = lax.broadcasted_iota(jnp.int32, (cells, width), 0)
    col = index - lax.shift_right_logical(index * 2731, 16) * GRID
    before = jnp.where(col >= 1, pltpu.roll(field, 1, 0), 0.0)
    behind = jnp.where(col <= GRID - 2, pltpu.roll(field, cells - 1, 0), 0.0)
    return before, field, behind


def depthwise(field, kernel):
    cells, width = field.shape
    shifted = beside(field)
    lines = [sum(kernel[3 * i + j] * shifted[j] for j in range(3)) for i in range(3)]
    none = jnp.zeros((GRID, width), F32)
    above = jnp.concatenate([none, lines[0][: cells - GRID]], axis=0)
    below = jnp.concatenate([lines[2][GRID:], none], axis=0)
    return above + lines[1] + below


def lane_halves():
    lane = lax.broadcasted_iota(jnp.int32, (1, 2 * HEAD), 1)
    return [lane < HEAD, lane >= HEAD]


def pair_slices(pair, share):
    return [slice(base + pair * 2 * HEAD, base + (pair + 1) * 2 * HEAD) for base in (0, share, 2 * share)]


class GradScatter:
    def __init__(self, bufs, signals, layer, src):
        self.src, self.layer = src, layer
        self.got, self.came, self.res = bufs
        self.send, self.recv = signals
        self.core, self.z = lax.axis_index("pipe"), lax.axis_index("dp")
        half = src.shape[1] // 2
        self.mine = pl.ds(pl.multiple_of(self.core * half, 16), half)
        self.theirs = pl.ds(pl.multiple_of((1 - self.core) * half, 16), half)
        self.steps = [[self.travel(way, k) for k in range(3)] for way in range(2)]
        self.final = self.describe(self.part(self.z), self.res.at[self.core], 7, {"pipe": 1 - self.core})

    def part(self, shard):
        return self.src.at[shard, self.mine, :]

    def describe(self, src, dst, slot, peer):
        return pltpu.make_async_remote_copy(
            src_ref=src,
            dst_ref=dst,
            send_sem=self.send.at[slot],
            recv_sem=self.recv.at[slot],
            device_id=peer,
            device_id_type=MESH,
        )

    def place(self, way):
        return self.z if way == 0 else 3 - self.z

    def shard(self, way, k):
        far = lax.rem(3 - k + self.place(way), 4)
        return far if way == 0 else 3 - far

    def travel(self, way, k):
        peer = lax.rem(self.z + (1 if way == 0 else 3), 4)
        return self.describe(
            self.part(self.shard(way, k)), self.came.at[way, k], 1 + 3 * way + k, {"dp": peer}
        )

    def add(self, shard, way, k):
        self.steps[way][k].wait_recv()
        self.src[shard, self.mine, :] = (
            self.src[shard, self.mine, :].astype(F32) + self.came[way, k].astype(F32)
        ).astype(BF16)

    def begin(self):
        self.swap = push(self.src.at[:, self.theirs, :], self.got, self.send, self.recv, 0, {"pipe": 1 - self.core})

    def step(self, k):
        if k == 0:
            self.swap.wait_recv()
            for s in range(4):
                self.src[s, self.mine, :] = (
                    self.src[s, self.mine, :].astype(F32) + self.got[s].astype(F32)
                ).astype(BF16)
        for way in range(2):
            if k > 0:

                @pl.when((self.place(way) >= 1) & (self.place(way) <= k))
                def _():
                    self.add(self.shard(way, k), way, k - 1)

            @pl.when(self.place(way) <= k)
            def _():
                self.steps[way][k].start()

    def close(self):
        for way in range(2):

            @pl.when(self.place(way) >= 1)
            def _():
                self.add(self.z, way, 2)

        @pl.when(self.core == self.layer)
        def _():
            self.res[self.core] = self.src[self.z, self.mine, :]

        @pl.when(self.core != self.layer)
        def _():
            self.final.start()

    def finish(self):
        @pl.when(self.core == self.layer)
        def _():
            self.final.wait_recv()

        @pl.when(self.core != self.layer)
        def _():
            self.final.wait_send()

        for way in range(2):
            for k in range(3):

                @pl.when(self.place(way) <= k)
                def _():
                    self.steps[way][k].wait_send()

        self.swap.wait_send()


def grad_scratch(shards, rows, cols):
    half = rows // 2
    return [
        pltpu.VMEM((shards, half, cols), BF16),
        pltpu.VMEM((2, 3, half, cols), BF16),
        pltpu.VMEM((2, half, cols), BF16),
    ]


def talk(ident):
    if ident is None:
        return pltpu.CompilerParams(vmem_limit_bytes=VMEM_BYTES)
    return pltpu.CompilerParams(collective_id=ident, has_side_effects=True, vmem_limit_bytes=VMEM_BYTES)


def launch(body, name, ident, near_in, far_in, near_out, far_out, scratch, flops):
    def flat(group):
        return [item for value in group.values() for item in (value if isinstance(value, list) else [value])]

    def named(groups, items):
        rest = iter(items)
        space = types.SimpleNamespace()
        for key, value in (pair for group in groups for pair in group.items()):
            setattr(space, key, [next(rest) for _ in value] if isinstance(value, list) else next(rest))
        return space

    def kernel(*refs):
        body(named((near_in, far_in, near_out, far_out, scratch), refs))

    vmem, anywhere = pl.BlockSpec(memory_space=pltpu.VMEM), pl.BlockSpec(memory_space=pl.ANY)
    outs = pl.pallas_call(
        kernel,
        out_shape=[jax.ShapeDtypeStruct(*shape) for shape in flat(near_out) + flat(far_out)],
        in_specs=[vmem] * len(flat(near_in)) + [anywhere] * len(flat(far_in)),
        out_specs=[vmem] * len(flat(near_out)) + [anywhere] * len(flat(far_out)),
        scratch_shapes=flat(scratch),
        compiler_params=talk(ident),
        cost_estimate=pl.CostEstimate(flops=flops, bytes_accessed=40_000_000, transcendentals=0),
        name=name,
    )(*flat(near_in), *flat(far_in))
    return named((near_out, far_out), outs)


def hold_pack(layer, r):
    mine = lax.axis_index("pipe") == layer
    at = 0
    for own, got in zip(r.own_vectors, r.got_vectors):
        r.pack[at : at + own.shape[0], :] = jnp.where(mine, own[...], got[...])
        at += own.shape[0]


def forward_kernel(layer, groups, copies, r):
    trade = layer == 0
    saved, weights = r.held, r.weights
    first, qkv, probs, mixed, second, hidden, slope, conv, depth = saved
    wq, wo, wu, wd, wc, gate_in, gate_out = weights
    own_w, got_w = r.own_weights, r.got_weights
    own, value, slots, pack, turn = r.own, r.value, r.slots, r.pack, r.turn

    size, width = own.shape
    half = width // 2
    tokens, share, ff = first.shape[0], mixed.shape[1], hidden.shape[1]
    spot = place()
    me, xn, yn, dn = spot
    core = lax.axis_index("pipe")
    mine = core == layer

    def rows(i):
        return pl.ds(pl.multiple_of(i * size, 16), size)

    loads = Loads(layer, own_w, got_w, weights, r.load_sem)
    saves = Copies(
        list(zip(saved, r.saved)) + [(turn, r.turn_out)], r.save_sem
    )
    peers = [{"mp": xn}, {"mp": yn}, {"mp": dn}] + others("dp", copies)
    if trade:

        @pl.when(mine)
        def _():
            for i in (CONV, QKV, OUT, GATE_IN, GATE_OUT):
                pltpu.make_async_copy(own_w[i], weights[i], r.load_sem.at[i]).start()

        other = {"pipe": 1 - core}
        ahead = r.flag[...] > 0.0
        r.x[...] = jnp.where(ahead, r.images[0], r.images[1])
        r.cot[...] = jnp.where(ahead, r.cotangents[0], r.cotangents[1])
        channels = r.pooled.shape[1]
        r.part_other[...] = jnp.where(ahead[:, :channels], r.parts[1], r.parts[0])
        greet(peers + [other])
        part_copy = push(r.part_other, r.part_land, r.core_send, r.core_recv, 7, other)
        trades = {
            i: push(own_w[i], got_w[i], r.core_send, r.core_recv, i, other)
            for i in (CONV, QKV, OUT, GATE_IN, GATE_OUT, UP, DOWN)
        }

        def arrive(*which):
            @pl.when(jnp.logical_not(mine))
            def _():
                for i in which:
                    trades[i].wait_recv()
                    pltpu.make_async_copy(got_w[i], weights[i], r.load_sem.at[i]).start()

    else:
        loads.start(CONV, QKV, OUT, GATE_IN, GATE_OUT)

        def arrive(*which):
            pass

        greet(peers)
    hold_pack(layer, r)

    x = r.x[...].astype(F32)
    first[rows(me), :] = norm_rows(x, row_of(pack, GAIN_ONE), row_of(pack, SHIFT_ONE)).astype(BF16)
    gather = Gather(first, r.ag_send.at[0], r.ag_recv.at[0], spot, rows)

    if trade:
        part_copy.wait_recv()
        part = jnp.where(ahead[:, :channels], r.parts[0], r.parts[1])
        r.pooled[...] = (part.astype(F32) + r.part_land[...].astype(F32)).astype(BF16)
    arrive(CONV)
    loads.wait(CONV)
    mapped = mm(r.pooled[...], wc[...])
    for t in range(width // TILE):
        lanes = slice(t * TILE, (t + 1) * TILE)
        conv[:, lanes] = mapped[:, lanes].astype(BF16)
        filtered = depthwise(mapped[:, lanes], [pack[k : k + 1, lanes] for k in range(9)])
        depth[:, lanes] = filtered.astype(BF16)
        value[0, :, lanes] = jnp.sum(filtered, axis=0, keepdims=True)
    sum_one = Sum(value.at[0], slots.at[0], r.sum_send.at[0], r.sum_recv.at[0], "mp", groups)
    saves.start(7, 8)

    def project(i):
        qkv[rows(i), :] = mm(first[rows(i), :], wq[...]).astype(BF16)

    arrive(QKV)
    loads.wait(QKV)
    project(me)
    gather.forward()
    if trade:
        arrive(OUT, GATE_IN, GATE_OUT, UP, DOWN)

        @pl.when(mine)
        def _():
            for i in (UP, DOWN):
                pltpu.make_async_copy(own_w[i], weights[i], r.load_sem.at[i]).start()

    else:
        loads.start(UP, DOWN)
    value[1] = sum_one.finish()
    sum_two = Sum(value.at[1], slots.at[1], r.sum_send.at[1], r.sum_recv.at[1], "dp", copies)
    project(xn)
    project(yn)
    turn[rows(me), :] = r.cot[:, layer * half : (layer + 1) * half]
    gather.finish()
    turn_gather = Gather(turn, r.ag_send.at[2], r.ag_recv.at[2], spot, rows)
    project(dn)
    saves.start(0, 1)

    halves = lane_halves()
    for pair in range(share // (2 * HEAD)):
        at_query, at_key, at_value = pair_slices(pair, share)
        query = qkv[:, at_query] * jnp.asarray(HEAD**-0.5, BF16)
        parts = []
        for h in range(2):
            scores = mm(jnp.where(halves[h], query, jnp.zeros_like(query)), qkv[:, at_key], 1, 1)
            raised = jnp.exp(scores - jnp.max(scores, axis=-1, keepdims=True))
            chances = (raised * (1.0 / jnp.sum(raised, axis=-1, keepdims=True))).astype(BF16)
            probs[2 * pair + h] = chances
            parts.append(mm(chances, qkv[:, at_value]))
        mixed[:, at_query] = jnp.where(halves[0], parts[0], parts[1]).astype(BF16)

    loads.wait(OUT, GATE_IN, GATE_OUT)
    turn_gather.forward()
    scatter = Scatter(r.bufs_one, r.rs_send.at[0], r.rs_recv.at[0], spot)

    def out_part(i):
        return mm(mixed[rows(i), :], wo[...])

    scatter.pd[...] = out_part(dn).astype(BF16)
    scatter.far()
    scatter.px[...] = out_part(xn).astype(BF16)
    scatter.near_x()
    scatter.py[...] = out_part(yn).astype(BF16)
    scatter.near_y()
    own[...] = out_part(me)
    saves.start(2, 3)
    mean = sum_two.finish() * (1.0 / (copies * tokens)) + row_of(pack, BIAS)
    level = gelu_parts(jnp.sum(gate_in[...].astype(F32) * mean, axis=1, keepdims=True))[0]
    value[2] = jnp.sum(level * gate_out[...].astype(F32), axis=0, keepdims=True)
    sum_three = Sum(value.at[2], slots.at[2], r.sum_send.at[2], r.sum_recv.at[2], "mp", groups)
    scatter.relay()
    after = x + scatter.total(own[...])
    r.after[...] = after
    second[rows(me), :] = norm_rows(after, row_of(pack, GAIN_TWO), row_of(pack, SHIFT_TWO)).astype(BF16)
    gather.drain()
    gather = Gather(second, r.ag_send.at[1], r.ag_recv.at[1], spot, rows)
    scatter.drain()
    turn_gather.finish()
    saves.start(9)
    gate = jnp.tanh(sum_three.finish())
    r.gate[...] = jnp.concatenate([gate, mean, jnp.zeros((6, width), F32)], axis=0)
    loads.wait(UP, DOWN)

    def feed(i):
        for t in range(ff // TILE):
            lanes = slice(t * TILE, (t + 1) * TILE)
            level, grad = gelu_parts(mm(second[rows(i), :], wu[:, lanes]))
            hidden[rows(i), lanes] = level.astype(BF16)
            slope[rows(i), lanes] = grad.astype(BF16)
        return mm(hidden[rows(i), :], wd[...]) + gate * depth[rows(i), :].astype(F32)

    scatter = Scatter(r.bufs_two, r.rs_send.at[1], r.rs_recv.at[1], spot)
    own[...] = feed(me)
    gather.forward()
    scatter.px[...] = feed(xn).astype(BF16)
    scatter.near_x()
    scatter.py[...] = feed(yn).astype(BF16)
    scatter.near_y()
    gather.finish()
    scatter.pd[...] = feed(dn).astype(BF16)
    scatter.far()
    saves.start(4, 5, 6)
    scatter.relay()
    r.out[...] = (r.after[...] + scatter.total(own[...]) + gate * row_of(pack, BIAS)).astype(BF16)
    gather.drain()
    turn_gather.drain()
    scatter.drain()
    for one in (sum_one, sum_two, sum_three):
        one.drain()
    if trade:

        @pl.when(mine)
        def _():
            for copy in trades.values():
                copy.wait_recv()

        for copy in (part_copy, *trades.values()):
            copy.wait_send()
    saves.finish()


def forward_layer(layer, ident, groups, copies, feed, vectors, own):
    trade = layer == 0
    own_vectors, got_vectors = vectors
    size, width = feed.images.shape[1:] if trade else feed.x.shape
    tokens, channels = feed.parts.shape[1:] if trade else feed.pooled.shape
    share, ff = own[OUT].shape[0], own[UP].shape[1]
    heads = share // HEAD
    saved = [
        ((tokens, width), BF16),
        ((tokens, 3 * share), BF16),
        ((heads, tokens, tokens), BF16),
        ((tokens, share), BF16),
        ((tokens, width), BF16),
        ((tokens, ff), BF16),
        ((tokens, ff), BF16),
        ((tokens, width), BF16),
        ((tokens, width), BF16),
    ]
    turned = ((tokens, width // 2), BF16)
    near_in = dict(own_vectors=own_vectors, got_vectors=got_vectors)
    far_in = dict(own_weights=own)
    near_out = dict(out=((size, width), BF16), after=((size, width), F32), gate=((8, width), F32))
    far_out = dict(saved=saved, turn_out=turned)
    scratch = dict(
        held=[pltpu.VMEM(*shape) for shape in saved],
        weights=[pltpu.VMEM(w.shape, BF16) for w in own],
        bufs_one=scatter_scratch(size, width),
        bufs_two=scatter_scratch(size, width),
        turn=pltpu.VMEM(*turned),
        own=pltpu.VMEM((size, width), F32),
        pack=pltpu.VMEM((16, width), F32),
        load_sem=pltpu.SemaphoreType.DMA((7,)),
        save_sem=pltpu.SemaphoreType.DMA((10,)),
        ag_send=pltpu.SemaphoreType.DMA((3, 6)),
        ag_recv=pltpu.SemaphoreType.DMA((3, 6)),
        rs_send=pltpu.SemaphoreType.DMA((2, 6)),
        rs_recv=pltpu.SemaphoreType.DMA((2, 6)),
        **sum_scratch(groups, copies, width),
    )
    if trade:
        near_in |= dict(flag=feed.flag, images=feed.images, cotangents=feed.cotangents, parts=feed.parts)
        near_out |= dict(x=((size, width), BF16), cot=((size, width), BF16), pooled=((tokens, channels), BF16))
        far_out |= dict(got_weights=[(w.shape, BF16) for w in own])
        scratch |= dict(
            part_other=pltpu.VMEM((tokens, channels), BF16),
            part_land=pltpu.VMEM((tokens, channels), BF16),
            core_send=pltpu.SemaphoreType.DMA((8,)),
            core_recv=pltpu.SemaphoreType.DMA((8,)),
        )
    else:
        near_in |= dict(x=feed.x, cot=feed.cot, pooled=feed.pooled)
        far_in |= dict(got_weights=feed.got_weights)
    return launch(
        functools.partial(forward_kernel, layer, groups, copies),
        "layer_forward",
        ident,
        near_in,
        far_in,
        near_out,
        far_out,
        scratch,
        20_000_000_000,
    )


def backward_kernel(layer, groups, copies, scatters, carried, gathered, r):
    dy_ref, x_ref, after_ref, pack, pooled, gate_ref = r.dy, r.x, r.after, r.pack, r.pooled, r.gate
    dx_ref, small_ref, grad_in, grad_out = r.dx, r.small, r.grad_in, r.grad_out
    held, weights, bufs = r.held, r.weights, r.bufs
    first, qkv, probs, mixed, second, hidden, slope, conv, depth = held
    dhp = slope
    wq, wo, wu, wd, gate_in, gate_out = weights
    own, dyf, daf, dmixed, dqkv, dafter, grads = r.own, r.dyf, r.daf, r.dmixed, r.dqkv, r.dafter, r.grads
    value, slots, sum_send, sum_recv = r.value, r.slots, r.sum_send, r.sum_recv
    ag_send, ag_recv, rs_send, rs_recv = r.ag_send, r.ag_recv, r.rs_send, r.rs_recv

    size, width = dy_ref.shape
    tokens, share, ff = first.shape[0], mixed.shape[1], hidden.shape[1]
    channels = pooled.shape[1]
    shards = grads.shape[0]
    cols = width // shards
    spot = place()
    me, xn, yn, dn = spot
    base_out = 3 * share
    base_conv = base_out + share
    base_up = base_conv + channels
    base_down = base_up + ff

    def rows(i):
        return pl.ds(pl.multiple_of(i * size, 16), size)

    def by_rows(base, grad, s):
        for t in range(grad.shape[1] // cols):
            grads[s, base + t * cols : base + (t + 1) * cols, :] = grad[:, t * cols : (t + 1) * cols].astype(BF16)

    def by_cols(base, grad):
        for s in range(shards):
            grads[s, base : base + grad.shape[0], :] = grad[:, s * cols : (s + 1) * cols].astype(BF16)

    loads = Loads(layer, r.own_weights, r.got_weights, weights, r.load_sem)
    saved = Copies(list(zip(r.saved, held)), r.saved_sem)
    saved.start(6)
    if gathered:
        half = width // 2
        turns = Copies([(r.turns[0], dyf.at[:, :half]), (r.turns[1], dyf.at[:, half:])], r.turn_sem)
        turns.start(0, 1)
    loads.start(3, 2)
    peers = [{"mp": xn}, {"mp": yn}, {"mp": dn}] + others("dp", copies)
    if scatters:
        saves = Copies([] if carried else [(grads.at[:, :base_up, :], r.late_out)], r.save_sem)
        peers.append({"pipe": 1 - lax.axis_index("pipe")})
        down = GradScatter(r.down, r.down_sem, layer, grads.at[:, base_down : base_down + ff, :])
        up = GradScatter(r.up, r.up_sem, layer, grads.at[:, base_up:base_down, :])
        if carried:
            lates = late_parts(r.late, r.late_sems, 1 - layer, r.late_held)
            rests = late_parts(r.late, r.rest_sems, layer, grads.at[:, :base_up, :])
            core = lax.axis_index("pipe")
            mine = core == layer
            other = {"pipe": 1 - core}
            other_loads = [
                pltpu.make_async_copy(r.down_in, down.res, r.late_sem.at[1]),
                pltpu.make_async_copy(r.up_in, up.res, r.late_sem.at[2]),
            ]

            @pl.when(jnp.logical_not(mine))
            def _():
                for load in other_loads:
                    load.start()

            late_load = pltpu.make_async_copy(r.late_in, r.late_held, r.late_sem.at[0])
            late_load.start()
    else:
        saves = Copies([(grads, r.grads_out)], r.save_sem)
    greet(peers)

    hold_pack(layer, r)
    if not gathered:
        dyf[rows(me), :] = dy_ref[...]
        gather = Gather(dyf, ag_send.at[0], ag_recv.at[0], spot, rows)
    scatter = Scatter(bufs, rs_send.at[0], rs_recv.at[0], spot)
    dy = dy_ref[...].astype(F32)
    dy_bias = jnp.sum(dy, axis=0, keepdims=True) * row_of(pack, BIAS)
    small_ref[...] = jnp.zeros_like(small_ref)
    saved.wait(6)
    loads.wait(3, 2)

    def feed_back(i):
        for t in range(ff // TILE):
            lanes = slice(t * TILE, (t + 1) * TILE)
            back = mm(dyf[rows(i), :], wd[lanes, :], 1, 1)
            dhp[rows(i), lanes] = (back * slope[rows(i), lanes].astype(F32)).astype(BF16)
        return mm(dhp[rows(i), :], wu[...], 1, 1)

    if carried:
        late_load.wait()
        for late in lates:
            late.begin()
    if gathered:
        turns.wait(0, 1)
        scatter.pd[...] = feed_back(dn).astype(BF16)
        scatter.far()
        saved.start(5, 8, 4)
        scatter.px[...] = feed_back(xn).astype(BF16)
        scatter.near_x()
        scatter.py[...] = feed_back(yn).astype(BF16)
        scatter.near_y()
        loads.start(1, 0, 4, 5)
        saved.start(1, 2, 3, 0, 7)
        own[...] = feed_back(me)
    else:
        own[...] = feed_back(me)
        saved.start(5, 8, 4)
        if carried:
            for late in lates:
                late.step(0)
        gather.forward()
        scatter.px[...] = feed_back(xn).astype(BF16)
        scatter.near_x()
        scatter.py[...] = feed_back(yn).astype(BF16)
        scatter.near_y()
        loads.start(1, 0, 4, 5)
        saved.start(1, 2, 3, 0, 7)
        gather.finish()
        scatter.pd[...] = feed_back(dn).astype(BF16)
        scatter.far()
    saved.wait(8)
    value[0] = dy_bias + jnp.sum(dyf[...].astype(F32) * depth[...].astype(F32), axis=0, keepdims=True)
    sum_one = Sum(value.at[0], slots.at[0], sum_send.at[0], sum_recv.at[0], "mp", groups)
    saved.wait(5)
    by_cols(base_down, mm(hidden[...], dyf[...], 0, 0))
    if scatters:
        down.begin()
    if carried:
        for late in lates:
            late.step(1)
    scatter.relay()
    value[1] = sum_one.finish()
    sum_two = Sum(value.at[1], slots.at[1], sum_send.at[1], sum_recv.at[1], "dp", copies)
    saved.wait(4)
    for s in range(shards):
        by_rows(base_up, mm(second[:, s * cols : (s + 1) * cols], dhp[...], 0, 0), s)
    if scatters:
        up.begin()
        down.step(0)
    back, gain_grad, bias_grad = norm_back(after_ref[...], row_of(pack, GAIN_TWO), scatter.total(own[...]))
    small_ref[1:2, :] = gain_grad
    small_ref[3:4, :] = bias_grad
    dafter[...] = dy + back
    daf[rows(me), :] = dafter[...].astype(BF16)
    if not gathered:
        gather.drain()
    gather = Gather(daf, ag_send.at[1], ag_recv.at[1], spot, rows)
    scatter.drain()
    scatter = Scatter(bufs, rs_send.at[1], rs_recv.at[1], spot)

    loads.wait(4, 5, 1)
    gate, mean = gate_ref[0:1, :], gate_ref[1:2, :]
    pre = sum_two.finish() * (1.0 - gate * gate)
    level, steep = gelu_parts(jnp.sum(gate_in[...].astype(F32) * mean, axis=1, keepdims=True))
    inner = jnp.sum(gate_out[...].astype(F32) * pre, axis=1, keepdims=True) * steep
    grad_out[...] = level * pre
    grad_in[...] = inner * mean
    value[2] = jnp.sum(gate_in[...].astype(F32) * inner, axis=0, keepdims=True)
    sum_three = Sum(value.at[2], slots.at[2], sum_send.at[2], sum_recv.at[2], "mp", groups)

    def mix_back(i):
        dmixed[rows(i), :] = mm(daf[rows(i), :], wo[...], 1, 1).astype(BF16)

    mix_back(me)
    if scatters:
        up.step(0)
    gather.forward()
    mix_back(xn)
    mix_back(yn)
    if carried:
        for late in lates:
            late.step(2)
    if scatters:
        down.step(1)
    mean_grad = sum_three.finish() * (1.0 / (copies * tokens))
    saved.wait(7)
    for t in range(shards):
        lanes = slice(t * cols, (t + 1) * cols)
        grad = gate[:, lanes] * dyf[:, lanes].astype(F32) + mean_grad[:, lanes]
        shifted = beside(conv[:, lanes].astype(F32))
        for i in range(3):
            for j in range(3):
                if i == 0:
                    terms = shifted[j][: tokens - GRID] * grad[GRID:]
                elif i == 1:
                    terms = shifted[j] * grad
                else:
                    terms = shifted[j][GRID:] * grad[: tokens - GRID]
                small_ref[4 + 3 * i + j : 5 + 3 * i + j, lanes] = jnp.sum(terms, axis=0, keepdims=True)
        small_ref[13:14, lanes] = jnp.sum(grad, axis=0, keepdims=True) * (1.0 / groups)
        back = depthwise(grad, [pack[8 - k : 9 - k, lanes] for k in range(9)])
        grads[t, base_conv : base_conv + channels, :] = mm(pooled[...], back.astype(BF16), 0, 0).astype(BF16)
    gather.finish()
    mix_back(dn)
    if scatters:
        up.step(1)

    saved.wait(1, 2)
    halves = lane_halves()
    scale = HEAD**-0.5
    for pair in range(share // (2 * HEAD)):
        at_query, at_key, at_value = pair_slices(pair, share)
        upper = dmixed[:, at_query]
        parts, key_grads, value_grads = [], [], []
        for h in range(2):
            low = probs[2 * pair + h]
            exact = low.astype(F32)
            grad_probs = mm(jnp.where(halves[h], upper, jnp.zeros_like(upper)), qkv[:, at_value], 1, 1)
            delta = jnp.sum(exact * grad_probs, axis=-1, keepdims=True)
            grad_scores = (exact * (grad_probs - delta)).astype(BF16)
            parts.append(mm(grad_scores, qkv[:, at_key]))
            key_grads.append(mm(grad_scores, qkv[:, at_query], 0, 0))
            value_grads.append(mm(low, upper, 0, 0))
        dqkv[:, at_query] = (jnp.where(halves[0], parts[0], parts[1]) * scale).astype(BF16)
        dqkv[:, at_key] = (jnp.where(halves[0], key_grads[0], key_grads[1]) * scale).astype(BF16)
        dqkv[:, at_value] = jnp.where(halves[0], value_grads[0], value_grads[1]).astype(BF16)
    loads.wait(0)

    def first_back(i):
        return mm(dqkv[rows(i), :], wq[...], 1, 1)

    scatter.pd[...] = first_back(dn).astype(BF16)
    scatter.far()
    scatter.px[...] = first_back(xn).astype(BF16)
    scatter.near_x()
    scatter.py[...] = first_back(yn).astype(BF16)
    scatter.near_y()
    own[...] = first_back(me)
    saved.wait(3)
    by_cols(base_out, mm(mixed[...], daf[...], 0, 0))
    if carried:
        for late in lates:
            late.close()
    if scatters:
        down.step(2)
    scatter.relay()
    saved.wait(0)
    for s in range(shards):
        by_rows(0, mm(first[:, s * cols : (s + 1) * cols], dqkv[...], 0, 0), s)
    if carried:
        for rest in rests:
            rest.begin()
    else:
        saves.start(0)
    back, gain_grad, bias_grad = norm_back(
        x_ref[...].astype(F32), row_of(pack, GAIN_ONE), scatter.total(own[...])
    )
    small_ref[0:1, :] = gain_grad
    small_ref[2:3, :] = bias_grad
    dx_ref[...] = (dafter[...] + back).astype(BF16)
    if scatters:
        up.step(2)
        down.close()
    if carried:
        units = grad_in.shape[0]
        dafter[2 * units :, :] = jnp.where(mine, r.small_in[...], small_ref[...])
        small_copy = push(dafter.at[2 * units :, :], r.small_got, r.core_send, r.core_recv, 0, other)
        dafter[:units, :] = jnp.where(mine, r.grad_in_in[...], grad_in[...])
        dafter[units : 2 * units, :] = jnp.where(mine, r.grad_out_in[...], grad_out[...])
        gate_copy = push(dafter.at[: 2 * units, :], r.gate_got, r.core_send, r.core_recv, 1, other)
        r.trade_stage[0] = jnp.where(mine, r.outs[1][...], r.outs[0][...])
        r.trade_stage[1] = jnp.where(mine, dy_ref[...], dx_ref[...])
        trade = push(r.trade_stage, r.trade_land, r.core_send, r.core_recv, 2, other)
        for rest in rests:
            rest.step(0)
    if scatters:
        up.close()
    if carried:
        small_copy.wait_recv()
        r.total[0] = jnp.where(mine, small_ref[...], r.small_in[...]) + r.small_got[...]
        over_groups = Sum(r.total.at[0], r.slot_a, r.last_send.at[0], r.last_recv.at[0], "mp", groups)
        down.finish()
        up.finish()

        @pl.when(jnp.logical_not(mine))
        def _():
            for load in other_loads:
                load.wait()

        results = Copies(
            [(down.res, r.down_sum), (up.res, r.up_sum)] + [(rests[i].res, r.late_sum.at[i]) for i in range(2)],
            r.done_sem,
        )
        results.start(0, 1)
        gate_copy.wait_recv()
        r.gate_sum[:units, :] = jnp.where(mine, grad_in[...], r.grad_in_in[...]) + r.gate_got[:units, :]
        r.gate_sum[units:, :] = jnp.where(mine, grad_out[...], r.grad_out_in[...]) + r.gate_got[units:, :]
        for rest in rests:
            rest.step(1)
        r.total[1] = over_groups.finish()
        over_copies = Sum(r.total.at[1], r.slot_b, r.last_send.at[1], r.last_recv.at[1], "dp", copies)
        for rest in rests:
            rest.step(2)
        r.vector_sum[...] = over_copies.finish()
        for rest in rests:
            rest.close()
        for piece in rests + lates:
            piece.finish()
        results.start(2, 3)
        trade.wait_recv()
        r.traded[...] = r.trade_land[...]
        results.finish()
        trade.wait_send()
        small_copy.wait_send()
        gate_copy.wait_send()
        over_groups.drain()
        over_copies.drain()
    gather.drain()
    scatter.drain()
    for one in (sum_one, sum_two, sum_three):
        one.drain()
    saves.finish()
    if scatters and not carried:
        for i, (piece, out) in enumerate([(down, r.down_out), (up, r.up_out)]):
            piece.finish()

            @pl.when(lax.axis_index("pipe") == layer)
            def _():
                copy = pltpu.make_async_copy(piece.res, out, r.done_sem.at[i])
                copy.start()
                copy.wait()


def late_parts(bufs, signals, layer, src):
    half = src.shape[1] // 2
    return [
        GradScatter(bufs[3 * i : 3 * i + 3], signals[2 * i : 2 * i + 2], layer, src.at[:, i * half : (i + 1) * half, :])
        for i in range(2)
    ]


BACK_WEIGHTS = (QKV, OUT, UP, DOWN, GATE_IN, GATE_OUT)


def backward_layer(layer, ident, groups, copies, scatters, dy, x, fore, vectors, pooled, own, got, later=None, outs=(), turns=()):
    size, width = dy.shape
    tokens, channels = pooled.shape
    share, ff = own[OUT].shape[0], own[UP].shape[1]
    hidden = own[GATE_IN].shape[0]
    shards = width // TILE
    late_rows = 4 * share + channels
    grads_shape = (shards, late_rows + 2 * ff, TILE)
    late_shape = (shards, late_rows, TILE)
    carried, gathered = later is not None, len(turns) > 0
    own, got = ([w[i] for i in BACK_WEIGHTS] for w in (own, got))
    near_in = dict(
        dy=dy, x=x, after=fore.after, own_vectors=vectors[0], got_vectors=vectors[1], pooled=pooled, gate=fore.gate
    )
    far_in = dict(saved=fore.saved, own_weights=own, got_weights=got)
    near_out = dict(dx=((size, width), BF16))
    far_out = {}
    rows = dict(small=((16, width), F32), grad_in=((hidden, width), F32), grad_out=((hidden, width), F32))
    signals = [pltpu.SemaphoreType.DMA((8,)) for _ in range(2)]
    halves = ((2, ff // 2, TILE), BF16)
    scratch = dict(
        held=[pltpu.VMEM(s.shape, s.dtype) for s in fore.saved],
        weights=[pltpu.VMEM(w.shape, BF16) for w in own],
        bufs=scatter_scratch(size, width),
        own=pltpu.VMEM((size, width), F32),
        pack=pltpu.VMEM((16, width), F32),
        dyf=pltpu.VMEM((tokens, width), BF16),
        daf=pltpu.VMEM((tokens, width), BF16),
        dmixed=pltpu.VMEM((tokens, share), BF16),
        dqkv=pltpu.VMEM((tokens, 3 * share), BF16),
        dafter=pltpu.VMEM((size, width), F32),
        grads=pltpu.VMEM(grads_shape, BF16),
        load_sem=pltpu.SemaphoreType.DMA((6,)),
        saved_sem=pltpu.SemaphoreType.DMA((9,)),
        save_sem=pltpu.SemaphoreType.DMA((1,)),
        ag_send=pltpu.SemaphoreType.DMA((2, 6)),
        ag_recv=pltpu.SemaphoreType.DMA((2, 6)),
        rs_send=pltpu.SemaphoreType.DMA((2, 6)),
        rs_recv=pltpu.SemaphoreType.DMA((2, 6)),
        **sum_scratch(groups, copies, width),
    )
    if scatters:
        scratch |= dict(
            down=grad_scratch(shards, ff, TILE), down_sem=signals, up=grad_scratch(shards, ff, TILE), up_sem=signals
        )
    if carried:
        near_in |= dict(small_in=later.small, grad_in_in=later.grad_in, grad_out_in=later.grad_out, outs=outs)
        far_in |= dict(late_in=later.late_out, down_in=later.down_out, up_in=later.up_out)
        near_out |= dict(
            vector_sum=((16, width), F32), gate_sum=((2 * hidden, width), F32), traded=((2, size, width), BF16)
        )
        far_out |= dict(down_sum=halves, up_sum=halves, late_sum=((2, 2, late_rows // 4, TILE), BF16))
        scratch |= {name: pltpu.VMEM(*shape) for name, shape in rows.items()}
        most = max(groups, copies) - 1
        scratch |= dict(
            late=grad_scratch(shards, late_rows // 2, TILE) + grad_scratch(shards, late_rows // 2, TILE),
            late_sems=signals + signals,
            rest_sems=signals + signals,
            late_held=pltpu.VMEM(late_shape, BF16),
            late_sem=pltpu.SemaphoreType.DMA((3,)),
            done_sem=pltpu.SemaphoreType.DMA((4,)),
            small_got=pltpu.VMEM((16, width), F32),
            gate_got=pltpu.VMEM((2 * hidden, width), F32),
            trade_stage=pltpu.VMEM((2, size, width), BF16),
            trade_land=pltpu.VMEM((2, size, width), BF16),
            total=pltpu.VMEM((2, 16, width), F32),
            slot_a=pltpu.VMEM((groups - 1, 16, width), F32),
            slot_b=pltpu.VMEM((copies - 1, 16, width), F32),
            core_send=pltpu.SemaphoreType.DMA((3,)),
            core_recv=pltpu.SemaphoreType.DMA((3,)),
            last_send=pltpu.SemaphoreType.DMA((2, most)),
            last_recv=pltpu.SemaphoreType.DMA((2, most)),
        )
    else:
        near_out |= rows
        if scatters:
            far_out |= dict(late_out=(late_shape, BF16), down_out=halves, up_out=halves)
            scratch |= dict(done_sem=pltpu.SemaphoreType.DMA((2,)))
        else:
            far_out |= dict(grads_out=(grads_shape, BF16))
    if gathered:
        far_in |= dict(turns=turns)
        scratch |= dict(turn_sem=pltpu.SemaphoreType.DMA((2,)))
    return launch(
        functools.partial(backward_kernel, layer, groups, copies, scatters, carried, gathered),
        "layer_backward",
        ident,
        near_in,
        far_in,
        near_out,
        far_out,
        scratch,
        40_000_000_000,
    )


def results_kernel(share, channels, r):
    core = lax.axis_index("pipe")
    ahead = r.flag[...] > 0.0
    for result, mine, got in ((r.layer_out, r.outs, r.traded[0]), (r.input_grad, r.grads, r.traded[1])):
        kept = jnp.where(core == 0, mine[0][...], mine[1][...])
        result[0] = jnp.where(ahead, kept, got)
        result[1] = jnp.where(ahead, got, kept)
    sums = r.vector_sum
    r.gain_grad[...] = sums[0:2, :]
    r.shift_grad[...] = sums[2:4, :]
    r.depth_grad[...] = sums[4:13, :]
    r.bias_grad[...] = sums[13:14, :]
    units = r.gate_in_grad.shape[0]
    r.gate_in_grad[...] = r.gate_sum[:units, :]
    r.gate_out_grad[...] = r.gate_sum[units:, :]
    half, cols = r.down_sum.shape[1:]
    for k in range(2):
        r.down_grad[k * half : (k + 1) * half, :] = r.down_sum[k].astype(F32)
        for t in range(half // cols):
            lanes = slice((k * (half // cols) + t) * cols, (k * (half // cols) + t + 1) * cols)
            r.up_grad[:, lanes] = r.up_sum[k, t * cols : (t + 1) * cols, :].astype(F32)
    part = r.late_sum.shape[2]

    def put(base, count, store):
        at = base
        while at < base + count:
            stop = min(base + count, (at // part + 1) * part)
            line = at % part
            rows = r.late_sum[at // (2 * part), at // part % 2, line : line + stop - at, :]
            store(slice(at - base, stop - base), rows.astype(F32))
            at = stop

    def store_qkv(k, lines, rows):
        r.qkv_grad[lines, k, :] = rows

    def store_out(lines, rows):
        r.out_grad[lines, :] = rows

    def store_conv(lines, rows):
        r.conv_grad[lines, :] = rows

    for k in range(3):
        put(k * cols, cols, functools.partial(store_qkv, k))
    put(3 * share, share, store_out)
    put(4 * share, channels, store_conv)


def results(flag, outs, grads, last, share, channels):
    size, width = outs[0].shape
    cols = last.down_sum.shape[2]
    ff = 2 * last.down_sum.shape[1]
    hidden = last.gate_sum.shape[0] // 2
    return launch(
        functools.partial(results_kernel, share, channels),
        "results",
        None,
        dict(
            flag=flag,
            outs=outs,
            grads=grads,
            traded=last.traded,
            vector_sum=last.vector_sum,
            gate_sum=last.gate_sum,
            down_sum=last.down_sum,
            up_sum=last.up_sum,
            late_sum=last.late_sum,
        ),
        {},
        dict(
            layer_out=((2, size, width), BF16),
            input_grad=((2, size, width), BF16),
            gain_grad=((2, width), F32),
            shift_grad=((2, width), F32),
            qkv_grad=((cols, 3, share), F32),
            out_grad=((share, cols), F32),
            up_grad=((cols, ff), F32),
            down_grad=((ff, cols), F32),
            conv_grad=((channels, cols), F32),
            depth_grad=((9, width), F32),
            bias_grad=((1, width), F32),
            gate_in_grad=((hidden, width), F32),
            gate_out_grad=((hidden, width), F32),
        ),
        {},
        {},
        1_000_000,
    )


def pool_weights(side, count, offset):
    rows_index = jnp.arange(GRID, dtype=jnp.int32)[:, None]
    cols_index = jnp.arange(count, dtype=jnp.int32)[None, :] + offset
    lower = rows_index * side // GRID
    upper = ((rows_index + 1) * side + GRID - 1) // GRID
    inside = (cols_index >= lower) & (cols_index < upper)
    return jnp.where(inside, 1.0 / (upper - lower).astype(F32), 0.0)


def pool_partial(feature, pixels, row_start):
    side = pixels * GRID // 768
    row_matrix = pool_weights(side, feature.shape[0], row_start)
    col_matrix = pool_weights(side, feature.shape[1], 0)
    first = jnp.einsum("ia,abc->ibc", row_matrix.astype(BF16), feature, preferred_element_type=F32)
    second = jnp.einsum("jb,ibc->ijc", col_matrix, first, precision=lax.Precision.HIGHEST)
    return second.reshape(GRID * GRID, feature.shape[2])


def per_device(
    inputs, cotangent, highres, resolution, assign, norm_gain, norm_bias, qkv_weight, out_weight, up_weight,
    down_weight, conv_weight, depth_weight, depth_bias, gate_in, gate_out,
):
    section = lax.axis_index("pipe")
    groups, copies = lax.axis_size("mp"), lax.axis_size("dp")
    first_half = section == 0
    order = assign[0]
    slot = order[section]

    def swap(block):
        return lax.ppermute(block, "pipe", SWAP)

    width = inputs.shape[2]
    share, channels, ff = out_weight.shape[1], conv_weight.shape[1], up_weight.shape[2]
    own_vectors = [depth_weight[0], depth_bias, norm_gain[0], norm_bias[0]]
    vectors = (own_vectors, [swap(v) for v in own_vectors])
    own = [
        qkv_weight[0].reshape(width, 3 * share), out_weight[0], up_weight[0], down_weight[0], conv_weight[0],
        gate_in[0], gate_out[0],
    ]
    row_start = section * highres.shape[1]
    parts = jax.vmap(pool_partial, in_axes=(0, 0, None))(highres, resolution, row_start).astype(BF16)
    flag = jnp.broadcast_to(jnp.where(slot == 0, 1.0, 0.0).astype(F32), (1, width))

    feed = types.SimpleNamespace(flag=flag, images=inputs, cotangents=cotangent, parts=parts)
    fore0 = forward_layer(0, 0, groups, copies, feed, vectors, own)
    pooled, got = fore0.pooled, fore0.got_weights
    feed = types.SimpleNamespace(x=fore0.out, cot=fore0.cot, pooled=pooled, got_weights=got)
    fore1 = forward_layer(1, 1, groups, copies, feed, vectors, own)
    scatters = copies == 4 and width // TILE == copies and inputs.shape[1] == 2 * gate_in.shape[1] + 16
    outs = [fore0.out, fore1.out]
    back1 = backward_layer(
        1, 2, groups, copies, scatters, fore0.cot, fore0.out, fore1, vectors, pooled, own, got,
        turns=[fore0.turn_out, fore1.turn_out],
    )
    back0 = backward_layer(
        0, 3, groups, copies, scatters, back1.dx, fore0.x, fore0, vectors, pooled, own, got,
        back1 if scatters else None, outs,
    )
    if scatters:
        last = results(flag, outs, [back0.dx, back1.dx], back0, share, channels)
        return (
            last.layer_out[None],
            last.input_grad[None],
            last.gain_grad[None],
            last.shift_grad[None],
            last.qkv_grad[None],
            last.out_grad[None],
            last.up_grad[None],
            last.down_grad[None],
            last.conv_grad[None],
            last.depth_grad[None],
            last.bias_grad,
            last.gate_in_grad[None],
            last.gate_out_grad[None],
        )

    def owned(first, second):
        kept = jnp.where(first_half, first, second)
        return kept, swap(jnp.where(first_half, second, first))

    def by_image(first, second):
        kept, received = owned(first, second)
        return jnp.where(slot == 0, jnp.stack([kept, received]), jnp.stack([received, kept]))[None]

    layer_out, input_grad = by_image(*outs), by_image(back0.dx, back1.dx)
    cols, blocks = width // copies, width // TILE
    ends = [3 * share, 4 * share, 4 * share + channels, 4 * share + channels + ff]

    def cores_sum(first, second, kind):
        kept, received = owned(first, second)
        return (kept.astype(F32) + received.astype(F32)).astype(kind)

    def scattered(blocked, dim):
        return lax.psum_scatter(blocked, "dp", scatter_dimension=dim, tiled=True).astype(F32)

    def by_rows(block):
        tiles = block.reshape(blocks, block.shape[1] // TILE, TILE, TILE)
        return scattered(tiles.transpose(0, 2, 1, 3).reshape(width, block.shape[1]), 0)

    def by_cols(block):
        return scattered(block.transpose(1, 0, 2).reshape(block.shape[1], width), 1)

    whole = cores_sum(back0.grads_out, back1.grads_out, BF16)
    small = lax.psum(cores_sum(back0.small, back1.small, F32), ("dp", "mp"))
    return (
        layer_out,
        input_grad,
        small[0:2][None],
        small[2:4][None],
        by_rows(whole[:, : ends[0]]).reshape(cols, 3, share)[None],
        by_cols(whole[:, ends[0] : ends[1]])[None],
        by_rows(whole[:, ends[2] : ends[3]])[None],
        by_cols(whole[:, ends[3] :])[None],
        by_cols(whole[:, ends[1] : ends[2]])[None],
        small[4:13][None],
        small[13][None],
        cores_sum(back0.grad_in, back1.grad_in, F32)[None],
        cores_sum(back0.grad_out, back1.grad_out, F32)[None],
    )


def solution(mesh):
    return jax.shard_map(
        per_device,
        mesh=mesh,
        in_specs=(
            P("dp", "mp", None),
            P("dp", "mp", None),
            P("dp", "pipe", None, "mp"),
            P("dp"),
            P("dp", None),
            P("pipe", None, None),
            P("pipe", None, None),
            P("pipe", None, None, "mp"),
            P("pipe", "mp", None),
            P("pipe", None, "mp"),
            P("pipe", "mp", None),
            P("pipe", "mp", None),
            P("pipe", None, None),
            P("pipe", None),
            P("pipe", "mp", None),
            P("pipe", "mp", None),
        ),
        out_specs=(
            P("pipe", "dp", "mp", None),
            P("pipe", "dp", "mp", None),
            P("pipe", None, None),
            P("pipe", None, None),
            P("pipe", "dp", None, "mp"),
            P("pipe", "mp", "dp"),
            P("pipe", "dp", "mp"),
            P("pipe", "mp", "dp"),
            P("pipe", "mp", "dp"),
            P("pipe", None, None),
            P("pipe", None),
            P("pipe", "mp", None),
            P("pipe", "mp", None),
        ),
        check_vma=False,
    )
```

```python
import functools
import types

import jax
import jax.numpy as jnp
from jax import lax
from jax.experimental import pallas as pl
from jax.experimental.pallas import tpu as pltpu
from jax.sharding import PartitionSpec as P

GRID = 24
HEAD = 64
EPS = 1e-06
TILE = 256
VMEM_BYTES = 60 * 1024 * 1024
MESH = pl.DeviceIdType.MESH
F32 = jnp.float32
BF16 = jnp.bfloat16
SWAP = [(0, 1), (1, 0)]


def mm(a, b, ca=1, cb=0):
    return lax.dot_general(a, b, (((ca,), (cb,)), ((), ())), preferred_element_type=F32)


def tile_of(index, width=TILE):
    return pl.ds(pl.multiple_of(index * width, width), width)


def place():
    me = lax.axis_index("mp")
    col, line = lax.rem(me, 2), lax.div(me, 2)
    return me, line * 2 + 1 - col, (1 - line) * 2 + col, (1 - line) * 2 + 1 - col


def greet(peers):
    barrier = pltpu.get_barrier_semaphore()
    for peer in peers:
        pl.semaphore_signal(barrier, inc=1, device_id=peer, device_id_type=MESH)
    pl.semaphore_wait(barrier, len(peers))


def push(src, dst, send, recv, slot, peer):
    copy = pltpu.make_async_remote_copy(
        src_ref=src,
        dst_ref=dst,
        send_sem=send.at[slot],
        recv_sem=recv.at[slot],
        device_id=peer,
        device_id_type=MESH,
    )
    copy.start()
    return copy


class Gather:
    def __init__(self, buf, send, recv, spot, rows):
        me, xn, yn, dn = spot
        half = buf.shape[1] // 2
        self.buf, self.send, self.recv, self.spot, self.rows = buf, send, recv, spot, rows
        self.low, self.high = pl.ds(0, half), pl.ds(half, half)
        self.near = [
            self.push(me, self.low, 0, xn),
            self.push(me, self.high, 1, yn),
            self.push(me, self.high, 2, xn),
            self.push(me, self.low, 3, yn),
        ]

    def push(self, block, half, slot, peer):
        part = self.buf.at[self.rows(block), half]
        return push(part, part, self.send, self.recv, slot, {"mp": peer})

    def forward(self):
        me, xn, yn, dn = self.spot
        self.near[0].wait_recv()
        first = self.push(xn, self.low, 4, yn)
        self.near[1].wait_recv()
        self.far = [first, self.push(yn, self.high, 5, xn)]
        self.near[2].wait_recv()
        self.near[3].wait_recv()

    def finish(self):
        for copy in self.far:
            copy.wait_recv()

    def drain(self):
        for copy in self.near + self.far:
            copy.wait_send()


class Scatter:
    def __init__(self, bufs, send, recv, spot):
        self.px, self.py, self.pd, self.via, self.rx, self.ry = bufs
        self.send, self.recv, self.spot = send, recv, spot
        width = self.px.shape[1]
        self.low, self.high = pl.ds(0, width // 2), pl.ds(width // 2, width // 2)

    def far(self):
        me, xn, yn, dn = self.spot
        self.far_copies = [
            push(self.pd.at[:, self.low], self.via.at[0], self.send, self.recv, 0, {"mp": xn}),
            push(self.pd.at[:, self.high], self.via.at[1], self.send, self.recv, 1, {"mp": yn}),
        ]

    def near_x(self):
        self.x_copy = push(
            self.px.at[:, self.low], self.rx.at[:, self.low], self.send, self.recv, 2, {"mp": self.spot[1]}
        )

    def near_y(self):
        self.y_copy = push(
            self.py.at[:, self.high], self.ry.at[:, self.high], self.send, self.recv, 3, {"mp": self.spot[2]}
        )

    def relay(self):
        me, xn, yn, dn = self.spot
        self.far_copies[0].wait_recv()
        self.py[:, self.low] = (self.py[:, self.low].astype(F32) + self.via[0].astype(F32)).astype(BF16)
        first = push(self.py.at[:, self.low], self.ry.at[:, self.low], self.send, self.recv, 4, {"mp": yn})
        self.far_copies[1].wait_recv()
        self.px[:, self.high] = (self.px[:, self.high].astype(F32) + self.via[1].astype(F32)).astype(BF16)
        second = push(self.px.at[:, self.high], self.rx.at[:, self.high], self.send, self.recv, 5, {"mp": xn})
        self.last_copies = [first, second]

    def total(self, own):
        for copy in [self.x_copy, self.y_copy] + self.last_copies:
            copy.wait_recv()
        return own + self.rx[...].astype(F32) + self.ry[...].astype(F32)

    def drain(self):
        for copy in self.far_copies + [self.x_copy, self.y_copy] + self.last_copies:
            copy.wait_send()


def scatter_scratch(rows, width):
    return [
        pltpu.VMEM((rows, width), BF16),
        pltpu.VMEM((rows, width), BF16),
        pltpu.VMEM((rows, width), BF16),
        pltpu.VMEM((2, rows, width // 2), BF16),
        pltpu.VMEM((rows, width), BF16),
        pltpu.VMEM((rows, width), BF16),
    ]


def norm_rows(values, gain, shift):
    center = values - jnp.mean(values, axis=-1, keepdims=True)
    spread = jnp.mean(center * center, axis=-1, keepdims=True)
    return center * lax.rsqrt(spread + EPS) * gain + shift


def norm_back(values, gain, grad):
    center = values - jnp.mean(values, axis=-1, keepdims=True)
    scale = lax.rsqrt(jnp.mean(center * center, axis=-1, keepdims=True) + EPS)
    unit = center * scale
    scaled = grad * gain
    mean_one = jnp.mean(scaled, axis=-1, keepdims=True)
    mean_two = jnp.mean(scaled * unit, axis=-1, keepdims=True)
    back = scale * (scaled - mean_one - unit * mean_two)
    return back, jnp.sum(grad * unit, axis=0, keepdims=True), jnp.sum(grad, axis=0, keepdims=True)


def gelu_parts(values):
    below = 0.5 * (1.0 + lax.erf(values * 0.7071067811865476))
    bell = jnp.exp(-0.5 * values * values) * 0.3989422804014327
    return values * below, below + values * bell


class Sum:
    def __init__(self, value, slots, send, recv, axis, count):
        self.value, self.slots = value, slots
        self.copies = [push(value, slots.at[j], send, recv, j, peer) for j, peer in enumerate(others(axis, count))]

    def finish(self):
        for copy in self.copies:
            copy.wait_recv()
        total = self.value[...]
        for j in range(len(self.copies)):
            total = total + self.slots[j]
        return total

    def drain(self):
        for copy in self.copies:
            copy.wait_send()


def others(axis, count):
    me = lax.axis_index(axis)
    return [{axis: lax.rem(me + j, count)} for j in range(1, count)]


def sum_scratch(groups, copies, width):
    most = max(groups, copies) - 1
    return dict(
        value=pltpu.VMEM((3, 1, width), F32),
        slots=pltpu.VMEM((3, most, 1, width), F32),
        sum_send=pltpu.SemaphoreType.DMA((3, most)),
        sum_recv=pltpu.SemaphoreType.DMA((3, most)),
    )


class Loads:
    def __init__(self, layer, own, got, held, sems):
        self.mine = lax.axis_index("pipe") == layer
        self.own, self.got, self.held, self.sems = own, got, held, sems

    def start(self, *which):
        for i in which:

            @pl.when(self.mine)
            def _():
                pltpu.make_async_copy(self.own[i], self.held[i], self.sems.at[i]).start()

            @pl.when(jnp.logical_not(self.mine))
            def _():
                pltpu.make_async_copy(self.got[i], self.held[i], self.sems.at[i]).start()

    def wait(self, *which):
        for i in which:
            pltpu.make_async_copy(self.own[i], self.held[i], self.sems.at[i]).wait()


class Copies:
    def __init__(self, pairs, sems):
        self.copies = [pltpu.make_async_copy(src, dst, sems.at[i]) for i, (src, dst) in enumerate(pairs)]
        self.started = []

    def start(self, *which):
        for i in which:
            self.copies[i].start()
            self.started.append(i)

    def wait(self, *which):
        for i in which:
            self.copies[i].wait()
            self.started.remove(i)

    def finish(self):
        self.wait(*list(self.started))


BIAS, GAIN_ONE, GAIN_TWO, SHIFT_ONE, SHIFT_TWO = 9, 10, 11, 12, 13
QKV, OUT, UP, DOWN, CONV, GATE_IN, GATE_OUT = range(7)


def row_of(pack, index):
    return pack[index : index + 1, :]


def beside(field):
    cells, width = field.shape
    index = lax.broadcasted_iota(jnp.int32, (cells, width), 0)
    col = index - lax.shift_right_logical(index * 2731, 16) * GRID
    before = jnp.where(col >= 1, pltpu.roll(field, 1, 0), 0.0)
    behind = jnp.where(col <= GRID - 2, pltpu.roll(field, cells - 1, 0), 0.0)
    return before, field, behind


def depthwise(field, kernel):
    cells, width = field.shape
    shifted = beside(field)
    lines = [sum(kernel[3 * i + j] * shifted[j] for j in range(3)) for i in range(3)]
    none = jnp.zeros((GRID, width), F32)
    above = jnp.concatenate([none, lines[0][: cells - GRID]], axis=0)
    below = jnp.concatenate([lines[2][GRID:], none], axis=0)
    return above + lines[1] + below


def lane_halves():
    lane = lax.broadcasted_iota(jnp.int32, (1, 2 * HEAD), 1)
    return [lane < HEAD, lane >= HEAD]


def pair_slices(pair, share):
    return [slice(base + pair * 2 * HEAD, base + (pair + 1) * 2 * HEAD) for base in (0, share, 2 * share)]


class GradScatter:
    def __init__(self, bufs, signals, layer, src):
        self.src, self.layer = src, layer
        self.got, self.came, self.res = bufs
        self.send, self.recv = signals
        self.core, self.z = lax.axis_index("pipe"), lax.axis_index("dp")
        half = src.shape[1] // 2
        self.mine = pl.ds(pl.multiple_of(self.core * half, 16), half)
        self.theirs = pl.ds(pl.multiple_of((1 - self.core) * half, 16), half)
        self.steps = [[self.travel(way, k) for k in range(3)] for way in range(2)]
        self.final = self.describe(self.part(self.z), self.res.at[self.core], 7, {"pipe": 1 - self.core})

    def part(self, shard):
        return self.src.at[shard, self.mine, :]

    def describe(self, src, dst, slot, peer):
        return pltpu.make_async_remote_copy(
            src_ref=src,
            dst_ref=dst,
            send_sem=self.send.at[slot],
            recv_sem=self.recv.at[slot],
            device_id=peer,
            device_id_type=MESH,
        )

    def place(self, way):
        return self.z if way == 0 else 3 - self.z

    def shard(self, way, k):
        far = lax.rem(3 - k + self.place(way), 4)
        return far if way == 0 else 3 - far

    def travel(self, way, k):
        peer = lax.rem(self.z + (1 if way == 0 else 3), 4)
        return self.describe(
            self.part(self.shard(way, k)), self.came.at[way, k], 1 + 3 * way + k, {"dp": peer}
        )

    def add(self, shard, way, k):
        self.steps[way][k].wait_recv()
        self.src[shard, self.mine, :] = (
            self.src[shard, self.mine, :].astype(F32) + self.came[way, k].astype(F32)
        ).astype(BF16)

    def begin(self):
        self.swap = push(self.src.at[:, self.theirs, :], self.got, self.send, self.recv, 0, {"pipe": 1 - self.core})

    def step(self, k):
        if k == 0:
            self.swap.wait_recv()
            for s in range(4):
                self.src[s, self.mine, :] = (
                    self.src[s, self.mine, :].astype(F32) + self.got[s].astype(F32)
                ).astype(BF16)
        for way in range(2):
            if k > 0:

                @pl.when((self.place(way) >= 1) & (self.place(way) <= k))
                def _():
                    self.add(self.shard(way, k), way, k - 1)

            @pl.when(self.place(way) <= k)
            def _():
                self.steps[way][k].start()

    def close(self):
        for way in range(2):

            @pl.when(self.place(way) >= 1)
            def _():
                self.add(self.z, way, 2)

        @pl.when(self.core == self.layer)
        def _():
            self.res[self.core] = self.src[self.z, self.mine, :]

        @pl.when(self.core != self.layer)
        def _():
            self.final.start()

    def finish(self):
        @pl.when(self.core == self.layer)
        def _():
            self.final.wait_recv()

        @pl.when(self.core != self.layer)
        def _():
            self.final.wait_send()

        for way in range(2):
            for k in range(3):

                @pl.when(self.place(way) <= k)
                def _():
                    self.steps[way][k].wait_send()

        self.swap.wait_send()


def grad_scratch(shards, rows, cols):
    half = rows // 2
    return [
        pltpu.VMEM((shards, half, cols), BF16),
        pltpu.VMEM((2, 3, half, cols), BF16),
        pltpu.VMEM((2, half, cols), BF16),
    ]


def talk(ident):
    if ident is None:
        return pltpu.CompilerParams(vmem_limit_bytes=VMEM_BYTES)
    return pltpu.CompilerParams(collective_id=ident, has_side_effects=True, vmem_limit_bytes=VMEM_BYTES)


def launch(body, name, ident, near_in, far_in, near_out, far_out, scratch, flops):
    def flat(group):
        return [item for value in group.values() for item in (value if isinstance(value, list) else [value])]

    def named(groups, items):
        rest = iter(items)
        space = types.SimpleNamespace()
        for key, value in (pair for group in groups for pair in group.items()):
            setattr(space, key, [next(rest) for _ in value] if isinstance(value, list) else next(rest))
        return space

    def kernel(*refs):
        body(named((near_in, far_in, near_out, far_out, scratch), refs))

    vmem, anywhere = pl.BlockSpec(memory_space=pltpu.VMEM), pl.BlockSpec(memory_space=pl.ANY)
    outs = pl.pallas_call(
        kernel,
        out_shape=[jax.ShapeDtypeStruct(*shape) for shape in flat(near_out) + flat(far_out)],
        in_specs=[vmem] * len(flat(near_in)) + [anywhere] * len(flat(far_in)),
        out_specs=[vmem] * len(flat(near_out)) + [anywhere] * len(flat(far_out)),
        scratch_shapes=flat(scratch),
        compiler_params=talk(ident),
        cost_estimate=pl.CostEstimate(flops=flops, bytes_accessed=40_000_000, transcendentals=0),
        name=name,
    )(*flat(near_in), *flat(far_in))
    return named((near_out, far_out), outs)


def hold_pack(layer, r):
    mine = lax.axis_index("pipe") == layer
    for k in range(9):
        r.pack[k : k + 1, :] = jnp.where(mine, r.own_vectors[0][k], r.got_vectors[0][k])
    at = BIAS
    for own, got in zip(r.own_vectors[1:], r.got_vectors[1:]):
        r.pack[at : at + own.shape[0], :] = jnp.where(mine, own[...], got[...])
        at += own.shape[0]


def forward_kernel(layer, groups, copies, r):
    trade = layer == 0
    saved, weights = r.held, r.weights
    first, qkv, probs, mixed, second, hidden, slope, conv, depth = saved
    wq, wo, wu, wd, wc, gate_in, gate_out = weights
    own_w, got_w = r.own_weights, r.got_weights
    own, value, slots, pack, turn = r.own, r.value, r.slots, r.pack, r.turn

    size, width = own.shape
    half = width // 2
    tokens, share, ff = first.shape[0], mixed.shape[1], hidden.shape[1]
    spot = place()
    me, xn, yn, dn = spot
    core = lax.axis_index("pipe")
    mine = core == layer

    def rows(i):
        return pl.ds(pl.multiple_of(i * size, 16), size)

    loads = Loads(layer, own_w, got_w, weights, r.load_sem)
    saves = Copies(
        list(zip(saved, r.saved)) + [(turn, r.turn_out)], r.save_sem
    )
    peers = [{"mp": xn}, {"mp": yn}, {"mp": dn}] + others("dp", copies)
    if trade:

        @pl.when(mine)
        def _():
            for i in (CONV, QKV, OUT, GATE_IN, GATE_OUT):
                pltpu.make_async_copy(own_w[i], weights[i], r.load_sem.at[i]).start()

        other = {"pipe": 1 - core}
        ahead = r.flag[...] > 0.0
        r.x[...] = jnp.where(ahead, r.images[0], r.images[1])
        r.cot[...] = jnp.where(ahead, r.cotangents[0], r.cotangents[1])
        channels = r.pooled.shape[1]
        r.part_other[...] = jnp.where(ahead[:, :channels], r.parts[1], r.parts[0])
        greet(peers + [other])
        part_copy = push(r.part_other, r.part_land, r.core_send, r.core_recv, 7, other)
        trades = {
            i: push(own_w[i], got_w[i], r.core_send, r.core_recv, i, other)
            for i in (CONV, QKV, OUT, GATE_IN, GATE_OUT, UP, DOWN)
        }

        def arrive(*which):
            @pl.when(jnp.logical_not(mine))
            def _():
                for i in which:
                    trades[i].wait_recv()
                    pltpu.make_async_copy(got_w[i], weights[i], r.load_sem.at[i]).start()

    else:
        loads.start(CONV, QKV, OUT, GATE_IN, GATE_OUT)

        def arrive(*which):
            pass

        greet(peers)
    hold_pack(layer, r)

    x = r.x[...].astype(F32)
    first[rows(me), :] = norm_rows(x, row_of(pack, GAIN_ONE), row_of(pack, SHIFT_ONE)).astype(BF16)
    gather = Gather(first, r.ag_send.at[0], r.ag_recv.at[0], spot, rows)

    if trade:
        part_copy.wait_recv()
        part = jnp.where(ahead[:, :channels], r.parts[0], r.parts[1])
        r.pooled[...] = (part.astype(F32) + r.part_land[...].astype(F32)).astype(BF16)
    arrive(CONV)
    loads.wait(CONV)
    mapped = mm(r.pooled[...], wc[...])
    for t in range(width // TILE):
        lanes = slice(t * TILE, (t + 1) * TILE)
        conv[:, lanes] = mapped[:, lanes].astype(BF16)
        filtered = depthwise(mapped[:, lanes], [pack[k : k + 1, lanes] for k in range(9)])
        depth[:, lanes] = filtered.astype(BF16)
        value[0, :, lanes] = jnp.sum(filtered, axis=0, keepdims=True)
    sum_one = Sum(value.at[0], slots.at[0], r.sum_send.at[0], r.sum_recv.at[0], "mp", groups)
    saves.start(7, 8)

    def project(i):
        for k in range(3):
            qkv[rows(i), k * share : (k + 1) * share] = mm(first[rows(i), :], wq[k]).astype(BF16)

    arrive(QKV)
    loads.wait(QKV)
    project(me)
    gather.forward()
    if trade:
        arrive(OUT, GATE_IN, GATE_OUT, UP, DOWN)

        @pl.when(mine)
        def _():
            for i in (UP, DOWN):
                pltpu.make_async_copy(own_w[i], weights[i], r.load_sem.at[i]).start()

    else:
        loads.start(UP, DOWN)
    value[1] = sum_one.finish()
    sum_two = Sum(value.at[1], slots.at[1], r.sum_send.at[1], r.sum_recv.at[1], "dp", copies)
    project(xn)
    project(yn)
    turn[rows(me), :] = r.cot[:, layer * half : (layer + 1) * half]
    gather.finish()
    turn_gather = Gather(turn, r.ag_send.at[2], r.ag_recv.at[2], spot, rows)
    project(dn)
    saves.start(0, 1)

    halves = lane_halves()
    for pair in range(share // (2 * HEAD)):
        at_query, at_key, at_value = pair_slices(pair, share)
        query = qkv[:, at_query] * jnp.asarray(HEAD**-0.5, BF16)
        parts = []
        for h in range(2):
            scores = mm(jnp.where(halves[h], query, jnp.zeros_like(query)), qkv[:, at_key], 1, 1)
            raised = jnp.exp(scores - jnp.max(scores, axis=-1, keepdims=True))
            chances = (raised * (1.0 / jnp.sum(raised, axis=-1, keepdims=True))).astype(BF16)
            probs[2 * pair + h] = chances
            parts.append(mm(chances, qkv[:, at_value]))
        mixed[:, at_query] = jnp.where(halves[0], parts[0], parts[1]).astype(BF16)

    loads.wait(OUT, GATE_IN, GATE_OUT)
    turn_gather.forward()
    scatter = Scatter(r.bufs_one, r.rs_send.at[0], r.rs_recv.at[0], spot)

    def out_part(i):
        return mm(mixed[rows(i), :], wo[...])

    scatter.pd[...] = out_part(dn).astype(BF16)
    scatter.far()
    scatter.px[...] = out_part(xn).astype(BF16)
    scatter.near_x()
    scatter.py[...] = out_part(yn).astype(BF16)
    scatter.near_y()
    own[...] = out_part(me)
    saves.start(2, 3)
    mean = sum_two.finish() * (1.0 / (copies * tokens)) + row_of(pack, BIAS)
    level = gelu_parts(jnp.sum(gate_in[...].astype(F32) * mean, axis=1, keepdims=True))[0]
    value[2] = jnp.sum(level * gate_out[...].astype(F32), axis=0, keepdims=True)
    sum_three = Sum(value.at[2], slots.at[2], r.sum_send.at[2], r.sum_recv.at[2], "mp", groups)
    scatter.relay()
    after = x + scatter.total(own[...])
    r.after[...] = after
    second[rows(me), :] = norm_rows(after, row_of(pack, GAIN_TWO), row_of(pack, SHIFT_TWO)).astype(BF16)
    gather.drain()
    gather = Gather(second, r.ag_send.at[1], r.ag_recv.at[1], spot, rows)
    scatter.drain()
    turn_gather.finish()
    saves.start(9)
    gate = jnp.tanh(sum_three.finish())
    r.gate[...] = jnp.concatenate([gate, mean, jnp.zeros((6, width), F32)], axis=0)
    loads.wait(UP, DOWN)

    def feed(i):
        for t in range(ff // TILE):
            lanes = slice(t * TILE, (t + 1) * TILE)
            level, grad = gelu_parts(mm(second[rows(i), :], wu[:, lanes]))
            hidden[rows(i), lanes] = level.astype(BF16)
            slope[rows(i), lanes] = grad.astype(BF16)
        return mm(hidden[rows(i), :], wd[...]) + gate * depth[rows(i), :].astype(F32)

    scatter = Scatter(r.bufs_two, r.rs_send.at[1], r.rs_recv.at[1], spot)
    own[...] = feed(me)
    gather.forward()
    scatter.px[...] = feed(xn).astype(BF16)
    scatter.near_x()
    scatter.py[...] = feed(yn).astype(BF16)
    scatter.near_y()
    gather.finish()
    scatter.pd[...] = feed(dn).astype(BF16)
    scatter.far()
    saves.start(4, 5, 6)
    scatter.relay()
    r.out[...] = (r.after[...] + scatter.total(own[...]) + gate * row_of(pack, BIAS)).astype(BF16)
    gather.drain()
    turn_gather.drain()
    scatter.drain()
    for one in (sum_one, sum_two, sum_three):
        one.drain()
    if trade:

        @pl.when(mine)
        def _():
            for copy in trades.values():
                copy.wait_recv()

        for copy in (part_copy, *trades.values()):
            copy.wait_send()
    saves.finish()


def forward_layer(layer, ident, groups, copies, feed, vectors, own):
    trade = layer == 0
    own_vectors, got_vectors = vectors
    size, width = feed.images.shape[1:] if trade else feed.x.shape
    tokens, channels = feed.parts.shape[1:] if trade else feed.pooled.shape
    share, ff = own[OUT].shape[0], own[UP].shape[1]
    heads = share // HEAD
    saved = [
        ((tokens, width), BF16),
        ((tokens, 3 * share), BF16),
        ((heads, tokens, tokens), BF16),
        ((tokens, share), BF16),
        ((tokens, width), BF16),
        ((tokens, ff), BF16),
        ((tokens, ff), BF16),
        ((tokens, width), BF16),
        ((tokens, width), BF16),
    ]
    turned = ((tokens, width // 2), BF16)
    near_in = dict(own_vectors=own_vectors, got_vectors=got_vectors)
    far_in = dict(own_weights=own)
    near_out = dict(out=((size, width), BF16), after=((size, width), F32), gate=((8, width), F32))
    far_out = dict(saved=saved, turn_out=turned)
    scratch = dict(
        held=[pltpu.VMEM(*shape) for shape in saved],
        weights=[pltpu.VMEM(w.shape, BF16) for w in own],
        bufs_one=scatter_scratch(size, width),
        bufs_two=scatter_scratch(size, width),
        turn=pltpu.VMEM(*turned),
        own=pltpu.VMEM((size, width), F32),
        pack=pltpu.VMEM((16, width), F32),
        load_sem=pltpu.SemaphoreType.DMA((7,)),
        save_sem=pltpu.SemaphoreType.DMA((10,)),
        ag_send=pltpu.SemaphoreType.DMA((3, 6)),
        ag_recv=pltpu.SemaphoreType.DMA((3, 6)),
        rs_send=pltpu.SemaphoreType.DMA((2, 6)),
        rs_recv=pltpu.SemaphoreType.DMA((2, 6)),
        **sum_scratch(groups, copies, width),
    )
    if trade:
        near_in |= dict(flag=feed.flag, images=feed.images, cotangents=feed.cotangents, parts=feed.parts)
        near_out |= dict(x=((size, width), BF16), cot=((size, width), BF16), pooled=((tokens, channels), BF16))
        far_out |= dict(got_weights=[(w.shape, BF16) for w in own])
        scratch |= dict(
            part_other=pltpu.VMEM((tokens, channels), BF16),
            part_land=pltpu.VMEM((tokens, channels), BF16),
            core_send=pltpu.SemaphoreType.DMA((8,)),
            core_recv=pltpu.SemaphoreType.DMA((8,)),
        )
    else:
        near_in |= dict(x=feed.x, cot=feed.cot, pooled=feed.pooled)
        far_in |= dict(got_weights=feed.got_weights)
    return launch(
        functools.partial(forward_kernel, layer, groups, copies),
        "layer_forward",
        ident,
        near_in,
        far_in,
        near_out,
        far_out,
        scratch,
        20_000_000_000,
    )


def backward_kernel(layer, groups, copies, scatters, carried, gathered, r):
    dy_ref, x_ref, after_ref, pack, pooled, gate_ref = r.dy, r.x, r.after, r.pack, r.pooled, r.gate
    dx_ref, small_ref, grad_in, grad_out = r.dx, r.small, r.grad_in, r.grad_out
    held, weights, bufs = r.held, r.weights, r.bufs
    first, qkv, probs, mixed, second, hidden, slope, conv, depth = held
    dhp = slope
    wq, wo, wu, wd, gate_in, gate_out = weights
    own, dyf, daf, dmixed, dqkv, dafter, grads = r.own, r.dyf, r.daf, r.dmixed, r.dqkv, r.dafter, r.grads
    value, slots, sum_send, sum_recv = r.value, r.slots, r.sum_send, r.sum_recv
    ag_send, ag_recv, rs_send, rs_recv = r.ag_send, r.ag_recv, r.rs_send, r.rs_recv

    size, width = dy_ref.shape
    tokens, share, ff = first.shape[0], mixed.shape[1], hidden.shape[1]
    channels = pooled.shape[1]
    shards = grads.shape[0]
    cols = width // shards
    spot = place()
    me, xn, yn, dn = spot
    base_out = 3 * share
    base_conv = base_out + share
    base_up = base_conv + channels
    base_down = base_up + ff

    def rows(i):
        return pl.ds(pl.multiple_of(i * size, 16), size)

    def by_rows(base, grad, s):
        for t in range(grad.shape[1] // cols):
            grads[s, base + t * cols : base + (t + 1) * cols, :] = grad[:, t * cols : (t + 1) * cols].astype(BF16)

    def by_cols(base, grad):
        for s in range(shards):
            grads[s, base : base + grad.shape[0], :] = grad[:, s * cols : (s + 1) * cols].astype(BF16)

    loads = Loads(layer, r.own_weights, r.got_weights, weights, r.load_sem)
    saved = Copies(list(zip(r.saved, held)), r.saved_sem)
    saved.start(6)
    if gathered:
        half = width // 2
        turns = Copies([(r.turns[0], dyf.at[:, :half]), (r.turns[1], dyf.at[:, half:])], r.turn_sem)
        turns.start(0, 1)
        saved.start(5)
    loads.start(3, 2)
    peers = [{"mp": xn}, {"mp": yn}, {"mp": dn}] + others("dp", copies)
    if scatters:
        saves = Copies([] if carried else [(grads.at[:, :base_conv, :], r.late_out)], r.save_sem)
        peers.append({"pipe": 1 - lax.axis_index("pipe")})
        down = GradScatter(r.down, r.down_sem, layer, grads.at[:, base_down : base_down + ff, :])
        up = GradScatter(r.up, r.up_sem, layer, grads.at[:, base_up:base_down, :])
        mid = GradScatter(r.mid, r.mid_sem, layer, grads.at[:, base_conv:base_up, :])
        if carried:
            lates = late_parts(r.late, r.late_sems, 1 - layer, r.late_held)
            rests = late_parts(r.late, r.rest_sems, layer, grads.at[:, :base_conv, :])
            core = lax.axis_index("pipe")
            mine = core == layer
            other = {"pipe": 1 - core}
            other_loads = [
                pltpu.make_async_copy(r.down_in, down.res, r.late_sem.at[1]),
                pltpu.make_async_copy(r.up_in, up.res, r.late_sem.at[2]),
                pltpu.make_async_copy(r.mid_in, mid.res, r.late_sem.at[3]),
            ]

            @pl.when(jnp.logical_not(mine))
            def _():
                for load in other_loads:
                    load.start()

            late_load = pltpu.make_async_copy(r.late_in, r.late_held, r.late_sem.at[0])
            late_load.start()
    else:
        saves = Copies([(grads, r.grads_out)], r.save_sem)
    greet(peers)

    hold_pack(layer, r)
    if not gathered:
        dyf[rows(me), :] = dy_ref[...]
        gather = Gather(dyf, ag_send.at[0], ag_recv.at[0], spot, rows)
    scatter = Scatter(bufs, rs_send.at[0], rs_recv.at[0], spot)
    dy = dy_ref[...].astype(F32)
    dy_bias = jnp.sum(dy, axis=0, keepdims=True) * row_of(pack, BIAS)
    small_ref[...] = jnp.zeros_like(small_ref)
    def down_back():
        saved.wait(5)
        by_cols(base_down, mm(hidden[...], dyf[...], 0, 0))
        if scatters:
            down.begin()

    if gathered:
        turns.wait(0, 1)
        down_back()
    saved.wait(6)
    loads.wait(3, 2)

    def feed_back(i):
        for t in range(ff // TILE):
            lanes = slice(t * TILE, (t + 1) * TILE)
            back = mm(dyf[rows(i), :], wd[lanes, :], 1, 1)
            dhp[rows(i), lanes] = (back * slope[rows(i), lanes].astype(F32)).astype(BF16)
        return mm(dhp[rows(i), :], wu[...], 1, 1)

    if carried:
        late_load.wait()
        for late in lates:
            late.begin()
    if gathered:
        scatter.pd[...] = feed_back(dn).astype(BF16)
        scatter.far()
        saved.start(8, 4)
        scatter.px[...] = feed_back(xn).astype(BF16)
        scatter.near_x()
        if scatters:
            down.step(0)
        scatter.py[...] = feed_back(yn).astype(BF16)
        scatter.near_y()
        loads.start(1, 0, 4, 5)
        saved.start(1, 2, 3, 0, 7)
        own[...] = feed_back(me)
    else:
        own[...] = feed_back(me)
        saved.start(5, 8, 4)
        if carried:
            for late in lates:
                late.step(0)
        gather.forward()
        scatter.px[...] = feed_back(xn).astype(BF16)
        scatter.near_x()
        scatter.py[...] = feed_back(yn).astype(BF16)
        scatter.near_y()
        loads.start(1, 0, 4, 5)
        if carried:
            for late in lates:
                late.step(1)
        saved.start(1, 2, 3, 0, 7)
        gather.finish()
        scatter.pd[...] = feed_back(dn).astype(BF16)
        scatter.far()
    saved.wait(8)
    value[0] = dy_bias + jnp.sum(dyf[...].astype(F32) * depth[...].astype(F32), axis=0, keepdims=True)
    sum_one = Sum(value.at[0], slots.at[0], sum_send.at[0], sum_recv.at[0], "mp", groups)
    if not gathered:
        down_back()
    if carried:
        for late in lates:
            late.step(2)
    scatter.relay()
    value[1] = sum_one.finish()
    sum_two = Sum(value.at[1], slots.at[1], sum_send.at[1], sum_recv.at[1], "dp", copies)
    saved.wait(4)
    for s in range(shards):
        by_rows(base_up, mm(second[:, s * cols : (s + 1) * cols], dhp[...], 0, 0), s)
    if scatters:
        up.begin()
        down.step(1 if gathered else 0)
    back, gain_grad, bias_grad = norm_back(after_ref[...], row_of(pack, GAIN_TWO), scatter.total(own[...]))
    small_ref[1:2, :] = gain_grad
    small_ref[3:4, :] = bias_grad
    dafter[...] = dy + back
    daf[rows(me), :] = dafter[...].astype(BF16)
    if not gathered:
        gather.drain()
    gather = Gather(daf, ag_send.at[1], ag_recv.at[1], spot, rows)
    scatter.drain()
    scatter = Scatter(bufs, rs_send.at[1], rs_recv.at[1], spot)

    loads.wait(4, 5, 1)
    gate, mean = gate_ref[0:1, :], gate_ref[1:2, :]
    pre = sum_two.finish() * (1.0 - gate * gate)
    level, steep = gelu_parts(jnp.sum(gate_in[...].astype(F32) * mean, axis=1, keepdims=True))
    inner = jnp.sum(gate_out[...].astype(F32) * pre, axis=1, keepdims=True) * steep
    grad_out[...] = level * pre
    grad_in[...] = inner * mean
    value[2] = jnp.sum(gate_in[...].astype(F32) * inner, axis=0, keepdims=True)
    sum_three = Sum(value.at[2], slots.at[2], sum_send.at[2], sum_recv.at[2], "mp", groups)

    def mix_back(i):
        dmixed[rows(i), :] = mm(daf[rows(i), :], wo[...], 1, 1).astype(BF16)

    mix_back(me)
    if gathered and scatters:
        down.step(2)
    if scatters:
        up.step(0)
    gather.forward()
    mix_back(xn)
    mix_back(yn)
    if scatters and not gathered:
        down.step(1)
    mean_grad = sum_three.finish() * (1.0 / (copies * tokens))
    saved.wait(7)
    for t in range(shards):
        lanes = slice(t * cols, (t + 1) * cols)
        grad = gate[:, lanes] * dyf[:, lanes].astype(F32) + mean_grad[:, lanes]
        shifted = beside(conv[:, lanes].astype(F32))
        for i in range(3):
            for j in range(3):
                if i == 0:
                    terms = shifted[j][: tokens - GRID] * grad[GRID:]
                elif i == 1:
                    terms = shifted[j] * grad
                else:
                    terms = shifted[j][GRID:] * grad[: tokens - GRID]
                small_ref[4 + 3 * i + j : 5 + 3 * i + j, lanes] = jnp.sum(terms, axis=0, keepdims=True)
        small_ref[13:14, lanes] = jnp.sum(grad, axis=0, keepdims=True) * (1.0 / groups)
        back = depthwise(grad, [pack[8 - k : 9 - k, lanes] for k in range(9)])
        grads[t, base_conv : base_conv + channels, :] = mm(pooled[...], back.astype(BF16), 0, 0).astype(BF16)
    if scatters:
        mid.begin()
    if gathered and scatters:
        up.step(1)
        down.close()
    gather.finish()
    mix_back(dn)
    if gathered and scatters:
        mid.step(0)
    elif scatters:
        up.step(1)
        down.step(2)
        mid.step(0)

    saved.wait(1, 2)
    halves = lane_halves()
    scale = HEAD**-0.5
    for pair in range(share // (2 * HEAD)):
        at_query, at_key, at_value = pair_slices(pair, share)
        upper = dmixed[:, at_query]
        parts, key_grads, value_grads = [], [], []
        for h in range(2):
            low = probs[2 * pair + h]
            exact = low.astype(F32)
            grad_probs = mm(jnp.where(halves[h], upper, jnp.zeros_like(upper)), qkv[:, at_value], 1, 1)
            delta = jnp.sum(exact * grad_probs, axis=-1, keepdims=True)
            grad_scores = (exact * (grad_probs - delta)).astype(BF16)
            parts.append(mm(grad_scores, qkv[:, at_key]))
            key_grads.append(mm(grad_scores, qkv[:, at_query], 0, 0))
            value_grads.append(mm(low, upper, 0, 0))
        dqkv[:, at_query] = (jnp.where(halves[0], parts[0], parts[1]) * scale).astype(BF16)
        dqkv[:, at_key] = (jnp.where(halves[0], key_grads[0], key_grads[1]) * scale).astype(BF16)
        dqkv[:, at_value] = jnp.where(halves[0], value_grads[0], value_grads[1]).astype(BF16)
    loads.wait(0)
    if gathered and scatters:
        up.step(2)
        mid.step(1)

    def first_back(i):
        return sum(mm(dqkv[rows(i), k * share : (k + 1) * share], wq[k], 1, 1) for k in range(3))

    scatter.pd[...] = first_back(dn).astype(BF16)
    scatter.far()
    scatter.px[...] = first_back(xn).astype(BF16)
    scatter.near_x()
    scatter.py[...] = first_back(yn).astype(BF16)
    scatter.near_y()
    own[...] = first_back(me)
    saved.wait(3)
    by_cols(base_out, mm(mixed[...], daf[...], 0, 0))
    if carried:
        for late in lates:
            late.close()
        down.close()
        up.step(2)
    elif scatters:
        mid.step(2)
    scatter.relay()
    saved.wait(0)
    for s in range(shards):
        by_rows(0, mm(first[:, s * cols : (s + 1) * cols], dqkv[...], 0, 0), s)
    if carried:
        for rest in rests:
            rest.begin()
        mid.step(1)
    else:
        saves.start(0)
    back, gain_grad, bias_grad = norm_back(
        x_ref[...].astype(F32), row_of(pack, GAIN_ONE), scatter.total(own[...])
    )
    small_ref[0:1, :] = gain_grad
    small_ref[2:3, :] = bias_grad
    dx_ref[...] = (dafter[...] + back).astype(BF16)
    if scatters:
        up.close()
    if carried:
        for rest in rests:
            rest.step(0)
        mid.step(2)
        units = grad_in.shape[0]
        dafter[2 * units :, :] = jnp.where(mine, r.small_in[...], small_ref[...])
        small_copy = push(dafter.at[2 * units :, :], r.small_got, r.core_send, r.core_recv, 0, other)
        dafter[:units, :] = jnp.where(mine, r.grad_in_in[...], grad_in[...])
        dafter[units : 2 * units, :] = jnp.where(mine, r.grad_out_in[...], grad_out[...])
        gate_copy = push(dafter.at[: 2 * units, :], r.gate_got, r.core_send, r.core_recv, 1, other)
        r.trade_stage[0] = jnp.where(mine, r.outs[1][...], r.outs[0][...])
        r.trade_stage[1] = jnp.where(mine, dy_ref[...], dx_ref[...])
        trade = push(r.trade_stage, r.trade_land, r.core_send, r.core_recv, 2, other)
    elif scatters:
        mid.close()
    if carried:
        small_copy.wait_recv()
        r.total[0] = jnp.where(mine, small_ref[...], r.small_in[...]) + r.small_got[...]
        over_groups = Sum(r.total.at[0], r.slot_a, r.last_send.at[0], r.last_recv.at[0], "mp", groups)
        for rest in rests:
            rest.step(1)
        mid.close()
        down.finish()
        up.finish()
        mid.finish()

        @pl.when(jnp.logical_not(mine))
        def _():
            for load in other_loads:
                load.wait()

        results = Copies(
            [(down.res, r.down_sum), (up.res, r.up_sum), (mid.res, r.mid_sum)]
            + [(rests[i].res, r.late_sum.at[i]) for i in range(2)],
            r.done_sem,
        )
        results.start(0, 1, 2)
        gate_copy.wait_recv()
        r.gate_sum[:units, :] = jnp.where(mine, grad_in[...], r.grad_in_in[...]) + r.gate_got[:units, :]
        r.gate_sum[units:, :] = jnp.where(mine, grad_out[...], r.grad_out_in[...]) + r.gate_got[units:, :]
        r.total[1] = over_groups.finish()
        over_copies = Sum(r.total.at[1], r.slot_b, r.last_send.at[1], r.last_recv.at[1], "dp", copies)
        for rest in rests:
            rest.step(2)
        r.vector_sum[...] = over_copies.finish()
        for rest in rests:
            rest.close()
        for piece in rests + lates:
            piece.finish()
        results.start(3, 4)
        trade.wait_recv()
        r.traded[...] = r.trade_land[...]
        results.finish()
        trade.wait_send()
        small_copy.wait_send()
        gate_copy.wait_send()
        over_groups.drain()
        over_copies.drain()
    gather.drain()
    scatter.drain()
    for one in (sum_one, sum_two, sum_three):
        one.drain()
    saves.finish()
    if scatters and not carried:
        for i, (piece, out) in enumerate([(down, r.down_out), (up, r.up_out), (mid, r.mid_out)]):
            piece.finish()

            @pl.when(lax.axis_index("pipe") == layer)
            def _():
                copy = pltpu.make_async_copy(piece.res, out, r.done_sem.at[i])
                copy.start()
                copy.wait()


def late_parts(bufs, signals, layer, src):
    half = src.shape[1] // 2
    return [
        GradScatter(bufs[3 * i : 3 * i + 3], signals[2 * i : 2 * i + 2], layer, src.at[:, i * half : (i + 1) * half, :])
        for i in range(2)
    ]


BACK_WEIGHTS = (QKV, OUT, UP, DOWN, GATE_IN, GATE_OUT)


def backward_layer(layer, ident, groups, copies, scatters, dy, x, fore, vectors, pooled, own, got, later=None, outs=(), turns=()):
    size, width = dy.shape
    tokens, channels = pooled.shape
    share, ff = own[OUT].shape[0], own[UP].shape[1]
    hidden = own[GATE_IN].shape[0]
    shards = width // TILE
    late_rows = 4 * share
    grads_shape = (shards, late_rows + channels + 2 * ff, TILE)
    late_shape = (shards, late_rows, TILE)
    carried, gathered = later is not None, len(turns) > 0
    own, got = ([w[i] for i in BACK_WEIGHTS] for w in (own, got))
    near_in = dict(
        dy=dy, x=x, after=fore.after, own_vectors=vectors[0], got_vectors=vectors[1], pooled=pooled, gate=fore.gate
    )
    far_in = dict(saved=fore.saved, own_weights=own, got_weights=got)
    near_out = dict(dx=((size, width), BF16))
    far_out = {}
    rows = dict(small=((16, width), F32), grad_in=((hidden, width), F32), grad_out=((hidden, width), F32))
    signals = [pltpu.SemaphoreType.DMA((8,)) for _ in range(2)]
    halves, mids = ((2, ff // 2, TILE), BF16), ((2, channels // 2, TILE), BF16)
    scratch = dict(
        held=[pltpu.VMEM(s.shape, s.dtype) for s in fore.saved],
        weights=[pltpu.VMEM(w.shape, BF16) for w in own],
        bufs=scatter_scratch(size, width),
        own=pltpu.VMEM((size, width), F32),
        pack=pltpu.VMEM((16, width), F32),
        dyf=pltpu.VMEM((tokens, width), BF16),
        daf=pltpu.VMEM((tokens, width), BF16),
        dmixed=pltpu.VMEM((tokens, share), BF16),
        dqkv=pltpu.VMEM((tokens, 3 * share), BF16),
        dafter=pltpu.VMEM((size, width), F32),
        grads=pltpu.VMEM(grads_shape, BF16),
        load_sem=pltpu.SemaphoreType.DMA((6,)),
        saved_sem=pltpu.SemaphoreType.DMA((9,)),
        save_sem=pltpu.SemaphoreType.DMA((1,)),
        ag_send=pltpu.SemaphoreType.DMA((2, 6)),
        ag_recv=pltpu.SemaphoreType.DMA((2, 6)),
        rs_send=pltpu.SemaphoreType.DMA((2, 6)),
        rs_recv=pltpu.SemaphoreType.DMA((2, 6)),
        **sum_scratch(groups, copies, width),
    )
    if scatters:
        scratch |= dict(
            down=grad_scratch(shards, ff, TILE),
            down_sem=signals,
            up=grad_scratch(shards, ff, TILE),
            up_sem=signals,
            mid=grad_scratch(shards, channels, TILE),
            mid_sem=signals,
        )
    if carried:
        near_in |= dict(small_in=later.small, grad_in_in=later.grad_in, grad_out_in=later.grad_out, outs=outs)
        far_in |= dict(late_in=later.late_out, down_in=later.down_out, up_in=later.up_out, mid_in=later.mid_out)
        near_out |= dict(
            vector_sum=((16, width), F32), gate_sum=((2 * hidden, width), F32), traded=((2, size, width), BF16)
        )
        far_out |= dict(down_sum=halves, up_sum=halves, mid_sum=mids, late_sum=((2, 2, late_rows // 4, TILE), BF16))
        scratch |= {name: pltpu.VMEM(*shape) for name, shape in rows.items()}
        most = max(groups, copies) - 1
        scratch |= dict(
            late=grad_scratch(shards, late_rows // 2, TILE) + grad_scratch(shards, late_rows // 2, TILE),
            late_sems=signals + signals,
            rest_sems=signals + signals,
            late_held=pltpu.VMEM(late_shape, BF16),
            late_sem=pltpu.SemaphoreType.DMA((4,)),
            done_sem=pltpu.SemaphoreType.DMA((5,)),
            small_got=pltpu.VMEM((16, width), F32),
            gate_got=pltpu.VMEM((2 * hidden, width), F32),
            trade_stage=pltpu.VMEM((2, size, width), BF16),
            trade_land=pltpu.VMEM((2, size, width), BF16),
            total=pltpu.VMEM((2, 16, width), F32),
            slot_a=pltpu.VMEM((groups - 1, 16, width), F32),
            slot_b=pltpu.VMEM((copies - 1, 16, width), F32),
            core_send=pltpu.SemaphoreType.DMA((3,)),
            core_recv=pltpu.SemaphoreType.DMA((3,)),
            last_send=pltpu.SemaphoreType.DMA((2, most)),
            last_recv=pltpu.SemaphoreType.DMA((2, most)),
        )
    else:
        near_out |= rows
        if scatters:
            far_out |= dict(late_out=(late_shape, BF16), down_out=halves, up_out=halves, mid_out=mids)
            scratch |= dict(done_sem=pltpu.SemaphoreType.DMA((3,)))
        else:
            far_out |= dict(grads_out=(grads_shape, BF16))
    if gathered:
        far_in |= dict(turns=turns)
        scratch |= dict(turn_sem=pltpu.SemaphoreType.DMA((2,)))
    return launch(
        functools.partial(backward_kernel, layer, groups, copies, scatters, carried, gathered),
        "layer_backward",
        ident,
        near_in,
        far_in,
        near_out,
        far_out,
        scratch,
        40_000_000_000,
    )


def results_kernel(share, r):
    core = lax.axis_index("pipe")
    ahead = r.flag[...] > 0.0
    for result, mine, got in ((r.layer_out, r.outs, r.traded[0]), (r.input_grad, r.grads, r.traded[1])):
        kept = jnp.where(core == 0, mine[0][...], mine[1][...])
        result[0] = jnp.where(ahead, kept, got)
        result[1] = jnp.where(ahead, got, kept)
    sums = r.vector_sum
    r.gain_grad[...] = sums[0:2, :]
    r.shift_grad[...] = sums[2:4, :]
    for k in range(9):
        r.depth_grad[k] = sums[4 + k : 5 + k, :]
    r.bias_grad[...] = sums[13:14, :]
    units = r.gate_in_grad.shape[0]
    r.gate_in_grad[...] = r.gate_sum[:units, :]
    r.gate_out_grad[...] = r.gate_sum[units:, :]
    half, cols = r.down_sum.shape[1:]
    for k in range(2):
        r.down_grad[k * half : (k + 1) * half, :] = r.down_sum[k].astype(F32)
        for t in range(half // cols):
            lanes = slice((k * (half // cols) + t) * cols, (k * (half // cols) + t + 1) * cols)
            r.up_grad[:, lanes] = r.up_sum[k, t * cols : (t + 1) * cols, :].astype(F32)
    part = r.late_sum.shape[2]

    def put(base, count, store):
        at = base
        while at < base + count:
            stop = min(base + count, (at // part + 1) * part)
            line = at % part
            rows = r.late_sum[at // (2 * part), at // part % 2, line : line + stop - at, :]
            store(slice(at - base, stop - base), rows.astype(F32))
            at = stop

    def store_qkv(k, lines, rows):
        r.qkv_grad[k, lines, :] = rows

    def store_out(lines, rows):
        r.out_grad[lines, :] = rows

    for k in range(3):
        put(k * cols, cols, functools.partial(store_qkv, k))
    put(3 * share, share, store_out)
    half = r.mid_sum.shape[1]
    for k in range(2):
        r.conv_grad[k * half : (k + 1) * half, :] = r.mid_sum[k].astype(F32)


def results(flag, outs, grads, last, share, channels):
    size, width = outs[0].shape
    cols = last.down_sum.shape[2]
    ff = 2 * last.down_sum.shape[1]
    hidden = last.gate_sum.shape[0] // 2
    return launch(
        functools.partial(results_kernel, share),
        "results",
        None,
        dict(
            flag=flag,
            outs=outs,
            grads=grads,
            traded=last.traded,
            vector_sum=last.vector_sum,
            gate_sum=last.gate_sum,
            down_sum=last.down_sum,
            up_sum=last.up_sum,
            mid_sum=last.mid_sum,
            late_sum=last.late_sum,
        ),
        {},
        dict(
            layer_out=((2, size, width), BF16),
            input_grad=((2, size, width), BF16),
            gain_grad=((2, width), F32),
            shift_grad=((2, width), F32),
            qkv_grad=((3, cols, share), F32),
            out_grad=((share, cols), F32),
            up_grad=((cols, ff), F32),
            down_grad=((ff, cols), F32),
            conv_grad=((channels, cols), F32),
            depth_grad=((9, 1, width), F32),
            bias_grad=((1, width), F32),
            gate_in_grad=((hidden, width), F32),
            gate_out_grad=((hidden, width), F32),
        ),
        {},
        {},
        1_000_000,
    )


def pool_weights(side, count, offset):
    rows_index = jnp.arange(GRID, dtype=jnp.int32)[:, None]
    cols_index = jnp.arange(count, dtype=jnp.int32)[None, :] + offset
    lower = rows_index * side // GRID
    upper = ((rows_index + 1) * side + GRID - 1) // GRID
    inside = (cols_index >= lower) & (cols_index < upper)
    return jnp.where(inside, 1.0 / (upper - lower).astype(F32), 0.0)


def pool_partial(feature, pixels, row_start):
    side = pixels * GRID // 768
    row_matrix = pool_weights(side, feature.shape[0], row_start)
    col_matrix = pool_weights(side, feature.shape[1], 0)
    first = jnp.einsum("ia,abc->ibc", row_matrix.astype(BF16), feature, preferred_element_type=F32)
    second = jnp.einsum("jb,ibc->ijc", col_matrix, first, precision=lax.Precision.HIGHEST)
    return second.reshape(GRID * GRID, feature.shape[2])


def per_device(
    inputs, cotangent, highres, resolution, assign, norm_gain, norm_bias, qkv_weight, out_weight, up_weight,
    down_weight, conv_weight, depth_weight, depth_bias, gate_in, gate_out,
):
    section = lax.axis_index("pipe")
    groups, copies = lax.axis_size("mp"), lax.axis_size("dp")
    first_half = section == 0
    order = assign[0]
    slot = order[section]

    def swap(block):
        return lax.ppermute(block, "pipe", SWAP)

    width = inputs.shape[2]
    share, channels, ff = out_weight.shape[1], conv_weight.shape[1], up_weight.shape[2]
    own_vectors = [depth_weight.transpose(1, 0, 2), depth_bias, norm_gain[0], norm_bias[0]]
    vectors = (own_vectors, [swap(v) for v in own_vectors])
    own = [
        qkv_weight[0].transpose(1, 0, 2), out_weight[0], up_weight[0], down_weight[0], conv_weight[0],
        gate_in[0], gate_out[0],
    ]
    row_start = section * highres.shape[1]
    parts = jax.vmap(pool_partial, in_axes=(0, 0, None))(highres, resolution, row_start).astype(BF16)
    flag = jnp.broadcast_to(jnp.where(slot == 0, 1.0, 0.0).astype(F32), (1, width))

    feed = types.SimpleNamespace(flag=flag, images=inputs, cotangents=cotangent, parts=parts)
    fore0 = forward_layer(0, 0, groups, copies, feed, vectors, own)
    pooled, got = fore0.pooled, fore0.got_weights
    feed = types.SimpleNamespace(x=fore0.out, cot=fore0.cot, pooled=pooled, got_weights=got)
    fore1 = forward_layer(1, 1, groups, copies, feed, vectors, own)
    scatters = copies == 4 and width // TILE == copies and inputs.shape[1] == 2 * gate_in.shape[1] + 16
    outs = [fore0.out, fore1.out]
    back1 = backward_layer(
        1, 2, groups, copies, scatters, fore0.cot, fore0.out, fore1, vectors, pooled, own, got,
        turns=[fore0.turn_out, fore1.turn_out],
    )
    back0 = backward_layer(
        0, 3, groups, copies, scatters, back1.dx, fore0.x, fore0, vectors, pooled, own, got,
        back1 if scatters else None, outs,
    )
    if scatters:
        last = results(flag, outs, [back0.dx, back1.dx], back0, share, channels)
        return (
            last.layer_out[None],
            last.input_grad[None],
            last.gain_grad[None],
            last.shift_grad[None],
            last.qkv_grad.transpose(1, 0, 2)[None],
            last.out_grad[None],
            last.up_grad[None],
            last.down_grad[None],
            last.conv_grad[None],
            last.depth_grad.transpose(1, 0, 2),
            last.bias_grad,
            last.gate_in_grad[None],
            last.gate_out_grad[None],
        )

    def owned(first, second):
        kept = jnp.where(first_half, first, second)
        return kept, swap(jnp.where(first_half, second, first))

    def by_image(first, second):
        kept, received = owned(first, second)
        return jnp.where(slot == 0, jnp.stack([kept, received]), jnp.stack([received, kept]))[None]

    layer_out, input_grad = by_image(*outs), by_image(back0.dx, back1.dx)
    cols, blocks = width // copies, width // TILE
    ends = [3 * share, 4 * share, 4 * share + channels, 4 * share + channels + ff]

    def cores_sum(first, second, kind):
        kept, received = owned(first, second)
        return (kept.astype(F32) + received.astype(F32)).astype(kind)

    def scattered(blocked, dim):
        return lax.psum_scatter(blocked, "dp", scatter_dimension=dim, tiled=True).astype(F32)

    def by_rows(block):
        tiles = block.reshape(blocks, block.shape[1] // TILE, TILE, TILE)
        return scattered(tiles.transpose(0, 2, 1, 3).reshape(width, block.shape[1]), 0)

    def by_cols(block):
        return scattered(block.transpose(1, 0, 2).reshape(block.shape[1], width), 1)

    whole = cores_sum(back0.grads_out, back1.grads_out, BF16)
    small = lax.psum(cores_sum(back0.small, back1.small, F32), ("dp", "mp"))
    return (
        layer_out,
        input_grad,
        small[0:2][None],
        small[2:4][None],
        by_rows(whole[:, : ends[0]]).reshape(cols, 3, share)[None],
        by_cols(whole[:, ends[0] : ends[1]])[None],
        by_rows(whole[:, ends[2] : ends[3]])[None],
        by_cols(whole[:, ends[3] :])[None],
        by_cols(whole[:, ends[1] : ends[2]])[None],
        small[4:13][None],
        small[13][None],
        cores_sum(back0.grad_in, back1.grad_in, F32)[None],
        cores_sum(back0.grad_out, back1.grad_out, F32)[None],
    )


def solution(mesh):
    return jax.shard_map(
        per_device,
        mesh=mesh,
        in_specs=(
            P("dp", "mp", None),
            P("dp", "mp", None),
            P("dp", "pipe", None, "mp"),
            P("dp"),
            P("dp", None),
            P("pipe", None, None),
            P("pipe", None, None),
            P("pipe", None, None, "mp"),
            P("pipe", "mp", None),
            P("pipe", None, "mp"),
            P("pipe", "mp", None),
            P("pipe", "mp", None),
            P("pipe", None, None),
            P("pipe", None),
            P("pipe", "mp", None),
            P("pipe", "mp", None),
        ),
        out_specs=(
            P("pipe", "dp", "mp", None),
            P("pipe", "dp", "mp", None),
            P("pipe", None, None),
            P("pipe", None, None),
            P("pipe", "dp", None, "mp"),
            P("pipe", "mp", "dp"),
            P("pipe", "dp", "mp"),
            P("pipe", "mp", "dp"),
            P("pipe", "mp", "dp"),
            P("pipe", None, None),
            P("pipe", None),
            P("pipe", "mp", None),
            P("pipe", "mp", None),
        ),
        check_vma=False,
    )
```

```python
import functools
import types

import jax
import jax.numpy as jnp
from jax import lax
from jax.experimental import pallas as pl
from jax.experimental.pallas import tpu as pltpu
from jax.sharding import PartitionSpec as P

GRID = 24
HEAD = 64
EPS = 1e-06
TILE = 256
VMEM_BYTES = 60 * 1024 * 1024
MESH = pl.DeviceIdType.MESH
F32 = jnp.float32
BF16 = jnp.bfloat16
SWAP = [(0, 1), (1, 0)]


def mm(a, b, ca=1, cb=0):
    return lax.dot_general(a, b, (((ca,), (cb,)), ((), ())), preferred_element_type=F32)


def tile_of(index, width=TILE):
    return pl.ds(pl.multiple_of(index * width, width), width)


def place():
    me = lax.axis_index("mp")
    col, line = lax.rem(me, 2), lax.div(me, 2)
    return me, line * 2 + 1 - col, (1 - line) * 2 + col, (1 - line) * 2 + 1 - col


def greet(peers):
    barrier = pltpu.get_barrier_semaphore()
    for peer in peers:
        pl.semaphore_signal(barrier, inc=1, device_id=peer, device_id_type=MESH)
    pl.semaphore_wait(barrier, len(peers))


def push(src, dst, send, recv, slot, peer):
    copy = pltpu.make_async_remote_copy(
        src_ref=src,
        dst_ref=dst,
        send_sem=send.at[slot],
        recv_sem=recv.at[slot],
        device_id=peer,
        device_id_type=MESH,
    )
    copy.start()
    return copy


class Gather:
    def __init__(self, buf, send, recv, spot, rows):
        me, xn, yn, dn = spot
        half = buf.shape[1] // 2
        self.buf, self.send, self.recv, self.spot, self.rows = buf, send, recv, spot, rows
        self.low, self.high = pl.ds(0, half), pl.ds(half, half)
        self.near = [
            self.push(me, self.low, 0, xn),
            self.push(me, self.high, 1, yn),
            self.push(me, self.high, 2, xn),
            self.push(me, self.low, 3, yn),
        ]

    def push(self, block, half, slot, peer):
        part = self.buf.at[self.rows(block), half]
        return push(part, part, self.send, self.recv, slot, {"mp": peer})

    def forward(self):
        me, xn, yn, dn = self.spot
        self.near[0].wait_recv()
        first = self.push(xn, self.low, 4, yn)
        self.near[1].wait_recv()
        self.far = [first, self.push(yn, self.high, 5, xn)]
        self.near[2].wait_recv()
        self.near[3].wait_recv()

    def finish(self):
        for copy in self.far:
            copy.wait_recv()

    def drain(self):
        for copy in self.near + self.far:
            copy.wait_send()


class Scatter:
    def __init__(self, bufs, send, recv, spot):
        self.px, self.py, self.pd, self.via, self.rx, self.ry = bufs
        self.send, self.recv, self.spot = send, recv, spot
        width = self.px.shape[1]
        self.low, self.high = pl.ds(0, width // 2), pl.ds(width // 2, width // 2)

    def far(self):
        me, xn, yn, dn = self.spot
        self.far_copies = [
            push(self.pd.at[:, self.low], self.via.at[0], self.send, self.recv, 0, {"mp": xn}),
            push(self.pd.at[:, self.high], self.via.at[1], self.send, self.recv, 1, {"mp": yn}),
        ]

    def near_x(self):
        self.x_copy = push(
            self.px.at[:, self.low], self.rx.at[:, self.low], self.send, self.recv, 2, {"mp": self.spot[1]}
        )

    def near_y(self):
        self.y_copy = push(
            self.py.at[:, self.high], self.ry.at[:, self.high], self.send, self.recv, 3, {"mp": self.spot[2]}
        )

    def relay(self):
        me, xn, yn, dn = self.spot
        self.far_copies[0].wait_recv()
        self.py[:, self.low] = (self.py[:, self.low].astype(F32) + self.via[0].astype(F32)).astype(BF16)
        first = push(self.py.at[:, self.low], self.ry.at[:, self.low], self.send, self.recv, 4, {"mp": yn})
        self.far_copies[1].wait_recv()
        self.px[:, self.high] = (self.px[:, self.high].astype(F32) + self.via[1].astype(F32)).astype(BF16)
        second = push(self.px.at[:, self.high], self.rx.at[:, self.high], self.send, self.recv, 5, {"mp": xn})
        self.last_copies = [first, second]

    def total(self, own):
        for copy in [self.x_copy, self.y_copy] + self.last_copies:
            copy.wait_recv()
        return own + self.rx[...].astype(F32) + self.ry[...].astype(F32)

    def drain(self):
        for copy in self.far_copies + [self.x_copy, self.y_copy] + self.last_copies:
            copy.wait_send()


def scatter_scratch(rows, width):
    return [
        pltpu.VMEM((rows, width), BF16),
        pltpu.VMEM((rows, width), BF16),
        pltpu.VMEM((rows, width), BF16),
        pltpu.VMEM((2, rows, width // 2), BF16),
        pltpu.VMEM((rows, width), BF16),
        pltpu.VMEM((rows, width), BF16),
    ]


def norm_rows(values, gain, shift):
    center = values - jnp.mean(values, axis=-1, keepdims=True)
    spread = jnp.mean(center * center, axis=-1, keepdims=True)
    return center * lax.rsqrt(spread + EPS) * gain + shift


def norm_back(values, gain, grad):
    center = values - jnp.mean(values, axis=-1, keepdims=True)
    scale = lax.rsqrt(jnp.mean(center * center, axis=-1, keepdims=True) + EPS)
    unit = center * scale
    scaled = grad * gain
    mean_one = jnp.mean(scaled, axis=-1, keepdims=True)
    mean_two = jnp.mean(scaled * unit, axis=-1, keepdims=True)
    back = scale * (scaled - mean_one - unit * mean_two)
    return back, jnp.sum(grad * unit, axis=0, keepdims=True), jnp.sum(grad, axis=0, keepdims=True)


def gelu_parts(values):
    below = 0.5 * (1.0 + lax.erf(values * 0.7071067811865476))
    bell = jnp.exp(-0.5 * values * values) * 0.3989422804014327
    return values * below, below + values * bell


class Sum:
    def __init__(self, value, slots, send, recv, axis, count):
        self.value, self.slots = value, slots
        self.copies = [push(value, slots.at[j], send, recv, j, peer) for j, peer in enumerate(others(axis, count))]

    def finish(self):
        for copy in self.copies:
            copy.wait_recv()
        total = self.value[...]
        for j in range(len(self.copies)):
            total = total + self.slots[j]
        return total

    def drain(self):
        for copy in self.copies:
            copy.wait_send()


def others(axis, count):
    me = lax.axis_index(axis)
    return [{axis: lax.rem(me + j, count)} for j in range(1, count)]


def sum_scratch(groups, copies, width):
    most = max(groups, copies) - 1
    return dict(
        value=pltpu.VMEM((3, 1, width), F32),
        slots=pltpu.VMEM((3, most, 1, width), F32),
        sum_send=pltpu.SemaphoreType.DMA((3, most)),
        sum_recv=pltpu.SemaphoreType.DMA((3, most)),
    )


class Loads:
    def __init__(self, layer, own, got, held, sems):
        self.mine = lax.axis_index("pipe") == layer
        self.own, self.got, self.held, self.sems = own, got, held, sems

    def start(self, *which):
        for i in which:

            @pl.when(self.mine)
            def _():
                pltpu.make_async_copy(self.own[i], self.held[i], self.sems.at[i]).start()

            @pl.when(jnp.logical_not(self.mine))
            def _():
                pltpu.make_async_copy(self.got[i], self.held[i], self.sems.at[i]).start()

    def wait(self, *which):
        for i in which:
            pltpu.make_async_copy(self.own[i], self.held[i], self.sems.at[i]).wait()


class Copies:
    def __init__(self, pairs, sems):
        self.copies = [pltpu.make_async_copy(src, dst, sems.at[i]) for i, (src, dst) in enumerate(pairs)]
        self.started = []

    def start(self, *which):
        for i in which:
            self.copies[i].start()
            self.started.append(i)

    def wait(self, *which):
        for i in which:
            self.copies[i].wait()
            self.started.remove(i)

    def finish(self):
        self.wait(*list(self.started))


BIAS, GAIN_ONE, GAIN_TWO, SHIFT_ONE, SHIFT_TWO = 9, 10, 11, 12, 13
QKV, OUT, UP, DOWN, CONV, GATE_IN, GATE_OUT = range(7)


def row_of(pack, index):
    return pack[index : index + 1, :]


def beside(field):
    cells, width = field.shape
    index = lax.broadcasted_iota(jnp.int32, (cells, width), 0)
    col = index - lax.shift_right_logical(index * 2731, 16) * GRID
    before = jnp.where(col >= 1, pltpu.roll(field, 1, 0), 0.0)
    behind = jnp.where(col <= GRID - 2, pltpu.roll(field, cells - 1, 0), 0.0)
    return before, field, behind


def depthwise(field, kernel):
    cells, width = field.shape
    shifted = beside(field)
    lines = [sum(kernel[3 * i + j] * shifted[j] for j in range(3)) for i in range(3)]
    none = jnp.zeros((GRID, width), F32)
    above = jnp.concatenate([none, lines[0][: cells - GRID]], axis=0)
    below = jnp.concatenate([lines[2][GRID:], none], axis=0)
    return above + lines[1] + below


def lane_halves():
    lane = lax.broadcasted_iota(jnp.int32, (1, 2 * HEAD), 1)
    return [lane < HEAD, lane >= HEAD]


def pair_slices(pair, share):
    return [slice(base + pair * 2 * HEAD, base + (pair + 1) * 2 * HEAD) for base in (0, share, 2 * share)]


class GradScatter:
    def __init__(self, bufs, signals, layer, src):
        self.src, self.layer = src, layer
        self.got, self.came, self.res = bufs
        self.send, self.recv = signals
        self.core, self.z = lax.axis_index("pipe"), lax.axis_index("dp")
        half = src.shape[1] // 2
        self.mine = pl.ds(pl.multiple_of(self.core * half, 16), half)
        self.theirs = pl.ds(pl.multiple_of((1 - self.core) * half, 16), half)
        self.steps = [[self.travel(way, k) for k in range(3)] for way in range(2)]
        self.final = self.describe(self.part(self.z), self.res.at[self.core], 7, {"pipe": 1 - self.core})

    def part(self, shard):
        return self.src.at[shard, self.mine, :]

    def describe(self, src, dst, slot, peer):
        return pltpu.make_async_remote_copy(
            src_ref=src,
            dst_ref=dst,
            send_sem=self.send.at[slot],
            recv_sem=self.recv.at[slot],
            device_id=peer,
            device_id_type=MESH,
        )

    def place(self, way):
        return self.z if way == 0 else 3 - self.z

    def shard(self, way, k):
        far = lax.rem(3 - k + self.place(way), 4)
        return far if way == 0 else 3 - far

    def travel(self, way, k):
        peer = lax.rem(self.z + (1 if way == 0 else 3), 4)
        return self.describe(
            self.part(self.shard(way, k)), self.came.at[way, k], 1 + 3 * way + k, {"dp": peer}
        )

    def add(self, shard, way, k):
        self.steps[way][k].wait_recv()
        self.src[shard, self.mine, :] = (
            self.src[shard, self.mine, :].astype(F32) + self.came[way, k].astype(F32)
        ).astype(BF16)

    def begin(self):
        self.swap = push(self.src.at[:, self.theirs, :], self.got, self.send, self.recv, 0, {"pipe": 1 - self.core})

    def step(self, k):
        if k == 0:
            self.swap.wait_recv()
            for s in range(4):
                self.src[s, self.mine, :] = (
                    self.src[s, self.mine, :].astype(F32) + self.got[s].astype(F32)
                ).astype(BF16)
        for way in range(2):
            if k > 0:

                @pl.when((self.place(way) >= 1) & (self.place(way) <= k))
                def _():
                    self.add(self.shard(way, k), way, k - 1)

            @pl.when(self.place(way) <= k)
            def _():
                self.steps[way][k].start()

    def close(self):
        for way in range(2):

            @pl.when(self.place(way) >= 1)
            def _():
                self.add(self.z, way, 2)

        @pl.when(self.core == self.layer)
        def _():
            self.res[self.core] = self.src[self.z, self.mine, :]

        @pl.when(self.core != self.layer)
        def _():
            self.final.start()

    def finish(self):
        @pl.when(self.core == self.layer)
        def _():
            self.final.wait_recv()

        @pl.when(self.core != self.layer)
        def _():
            self.final.wait_send()

        for way in range(2):
            for k in range(3):

                @pl.when(self.place(way) <= k)
                def _():
                    self.steps[way][k].wait_send()

        self.swap.wait_send()


def grad_scratch(shards, rows, cols):
    half = rows // 2
    return [
        pltpu.VMEM((shards, half, cols), BF16),
        pltpu.VMEM((2, 3, half, cols), BF16),
        pltpu.VMEM((2, half, cols), BF16),
    ]


def talk(ident):
    if ident is None:
        return pltpu.CompilerParams(vmem_limit_bytes=VMEM_BYTES)
    return pltpu.CompilerParams(collective_id=ident, has_side_effects=True, vmem_limit_bytes=VMEM_BYTES)


def launch(body, name, ident, near_in, far_in, near_out, far_out, scratch, flops):
    def flat(group):
        return [item for value in group.values() for item in (value if isinstance(value, list) else [value])]

    def named(groups, items):
        rest = iter(items)
        space = types.SimpleNamespace()
        for key, value in (pair for group in groups for pair in group.items()):
            setattr(space, key, [next(rest) for _ in value] if isinstance(value, list) else next(rest))
        return space

    def kernel(*refs):
        body(named((near_in, far_in, near_out, far_out, scratch), refs))

    vmem, anywhere = pl.BlockSpec(memory_space=pltpu.VMEM), pl.BlockSpec(memory_space=pl.ANY)
    outs = pl.pallas_call(
        kernel,
        out_shape=[jax.ShapeDtypeStruct(*shape) for shape in flat(near_out) + flat(far_out)],
        in_specs=[vmem] * len(flat(near_in)) + [anywhere] * len(flat(far_in)),
        out_specs=[vmem] * len(flat(near_out)) + [anywhere] * len(flat(far_out)),
        scratch_shapes=flat(scratch),
        compiler_params=talk(ident),
        cost_estimate=pl.CostEstimate(flops=flops, bytes_accessed=40_000_000, transcendentals=0),
        name=name,
    )(*flat(near_in), *flat(far_in))
    return named((near_out, far_out), outs)


def hold_pack(layer, r):
    mine = lax.axis_index("pipe") == layer
    for k in range(9):
        r.pack[k : k + 1, :] = jnp.where(mine, r.own_vectors[0][k], r.got_vectors[0][k])
    at = BIAS
    for own, got in zip(r.own_vectors[1:], r.got_vectors[1:]):
        r.pack[at : at + own.shape[0], :] = jnp.where(mine, own[...], got[...])
        at += own.shape[0]


def forward_kernel(layer, groups, copies, r):
    trade = layer == 0
    saved, weights = r.held, r.weights
    first, qkv, probs, mixed, second, hidden, slope, conv, depth = saved
    wq, wo, wu, wd, wc, gate_in, gate_out = weights
    own_w, got_w = r.own_weights, r.got_weights
    own, value, slots, pack, turn = r.own, r.value, r.slots, r.pack, r.turn

    size, width = own.shape
    half = width // 2
    tokens, share, ff = first.shape[0], mixed.shape[1], hidden.shape[1]
    spot = place()
    me, xn, yn, dn = spot
    core = lax.axis_index("pipe")
    mine = core == layer

    def rows(i):
        return pl.ds(pl.multiple_of(i * size, 16), size)

    loads = Loads(layer, own_w, got_w, weights, r.load_sem)
    saves = Copies(
        list(zip(saved, r.saved)) + [(turn, r.turn_out)], r.save_sem
    )
    peers = [{"mp": xn}, {"mp": yn}, {"mp": dn}] + others("dp", copies)
    if trade:

        @pl.when(mine)
        def _():
            for i in (CONV, QKV, OUT, GATE_IN, GATE_OUT):
                pltpu.make_async_copy(own_w[i], weights[i], r.load_sem.at[i]).start()

        other = {"pipe": 1 - core}
        ahead = r.flag[...] > 0.0
        r.x[...] = jnp.where(ahead, r.images[0], r.images[1])
        r.cot[...] = jnp.where(ahead, r.cotangents[0], r.cotangents[1])
        channels = r.pooled.shape[1]
        r.part_other[...] = jnp.where(ahead[:, :channels], r.parts[1], r.parts[0])
        greet(peers + [other])
        part_copy = push(r.part_other, r.part_land, r.core_send, r.core_recv, 7, other)
        trades = {
            i: push(own_w[i], got_w[i], r.core_send, r.core_recv, i, other)
            for i in (CONV, QKV, OUT, GATE_IN, GATE_OUT, UP, DOWN)
        }

        def arrive(*which):
            @pl.when(jnp.logical_not(mine))
            def _():
                for i in which:
                    trades[i].wait_recv()
                    pltpu.make_async_copy(got_w[i], weights[i], r.load_sem.at[i]).start()

    else:
        loads.start(CONV, QKV, OUT, GATE_IN, GATE_OUT)

        def arrive(*which):
            pass

        greet(peers)
    hold_pack(layer, r)

    x = r.x[...].astype(F32)
    first[rows(me), :] = norm_rows(x, row_of(pack, GAIN_ONE), row_of(pack, SHIFT_ONE)).astype(BF16)
    gather = Gather(first, r.ag_send.at[0], r.ag_recv.at[0], spot, rows)

    if trade:
        part_copy.wait_recv()
        part = jnp.where(ahead[:, :channels], r.parts[0], r.parts[1])
        r.pooled[...] = (part.astype(F32) + r.part_land[...].astype(F32)).astype(BF16)
    arrive(CONV)
    loads.wait(CONV)
    mapped = mm(r.pooled[...], wc[...])
    for t in range(width // TILE):
        lanes = slice(t * TILE, (t + 1) * TILE)
        conv[:, lanes] = mapped[:, lanes].astype(BF16)
        filtered = depthwise(mapped[:, lanes], [pack[k : k + 1, lanes] for k in range(9)])
        depth[:, lanes] = filtered.astype(BF16)
        value[0, :, lanes] = jnp.sum(filtered, axis=0, keepdims=True)
    sum_one = Sum(value.at[0], slots.at[0], r.sum_send.at[0], r.sum_recv.at[0], "mp", groups)
    saves.start(7, 8)

    def project(i):
        for k in range(3):
            qkv[rows(i), k * share : (k + 1) * share] = mm(first[rows(i), :], wq[k]).astype(BF16)

    arrive(QKV)
    loads.wait(QKV)
    project(me)
    gather.forward()
    if trade:
        arrive(OUT, GATE_IN, GATE_OUT, UP, DOWN)

        @pl.when(mine)
        def _():
            for i in (UP, DOWN):
                pltpu.make_async_copy(own_w[i], weights[i], r.load_sem.at[i]).start()

    else:
        loads.start(UP, DOWN)
    value[1] = sum_one.finish()
    sum_two = Sum(value.at[1], slots.at[1], r.sum_send.at[1], r.sum_recv.at[1], "dp", copies)
    project(xn)
    project(yn)
    turn[rows(me), :] = r.cot[:, layer * half : (layer + 1) * half]
    gather.finish()
    turn_gather = Gather(turn, r.ag_send.at[2], r.ag_recv.at[2], spot, rows)
    project(dn)
    saves.start(0, 1)

    halves = lane_halves()
    for pair in range(share // (2 * HEAD)):
        at_query, at_key, at_value = pair_slices(pair, share)
        query = qkv[:, at_query] * jnp.asarray(HEAD**-0.5, BF16)
        parts = []
        for h in range(2):
            scores = mm(jnp.where(halves[h], query, jnp.zeros_like(query)), qkv[:, at_key], 1, 1)
            raised = jnp.exp(scores - jnp.max(scores, axis=-1, keepdims=True))
            chances = (raised * (1.0 / jnp.sum(raised, axis=-1, keepdims=True))).astype(BF16)
            probs[2 * pair + h] = chances
            parts.append(mm(chances, qkv[:, at_value]))
        mixed[:, at_query] = jnp.where(halves[0], parts[0], parts[1]).astype(BF16)

    loads.wait(OUT, GATE_IN, GATE_OUT)
    turn_gather.forward()
    scatter = Scatter(r.bufs_one, r.rs_send.at[0], r.rs_recv.at[0], spot)

    def out_part(i):
        return mm(mixed[rows(i), :], wo[...])

    scatter.pd[...] = out_part(dn).astype(BF16)
    scatter.far()
    scatter.px[...] = out_part(xn).astype(BF16)
    scatter.near_x()
    scatter.py[...] = out_part(yn).astype(BF16)
    scatter.near_y()
    own[...] = out_part(me)
    saves.start(2, 3)
    mean = sum_two.finish() * (1.0 / (copies * tokens)) + row_of(pack, BIAS)
    level = gelu_parts(jnp.sum(gate_in[...].astype(F32) * mean, axis=1, keepdims=True))[0]
    value[2] = jnp.sum(level * gate_out[...].astype(F32), axis=0, keepdims=True)
    sum_three = Sum(value.at[2], slots.at[2], r.sum_send.at[2], r.sum_recv.at[2], "mp", groups)
    scatter.relay()
    after = x + scatter.total(own[...])
    r.after[...] = after
    second[rows(me), :] = norm_rows(after, row_of(pack, GAIN_TWO), row_of(pack, SHIFT_TWO)).astype(BF16)
    gather.drain()
    gather = Gather(second, r.ag_send.at[1], r.ag_recv.at[1], spot, rows)
    scatter.drain()
    turn_gather.finish()
    saves.start(9)
    gate = jnp.tanh(sum_three.finish())
    r.gate[...] = jnp.concatenate([gate, mean, jnp.zeros((6, width), F32)], axis=0)
    loads.wait(UP, DOWN)

    def feed(i):
        for t in range(ff // TILE):
            lanes = slice(t * TILE, (t + 1) * TILE)
            level, grad = gelu_parts(mm(second[rows(i), :], wu[:, lanes]))
            hidden[rows(i), lanes] = level.astype(BF16)
            slope[rows(i), lanes] = grad.astype(BF16)
        return mm(hidden[rows(i), :], wd[...]) + gate * depth[rows(i), :].astype(F32)

    scatter = Scatter(r.bufs_two, r.rs_send.at[1], r.rs_recv.at[1], spot)
    own[...] = feed(me)
    gather.forward()
    scatter.px[...] = feed(xn).astype(BF16)
    scatter.near_x()
    scatter.py[...] = feed(yn).astype(BF16)
    scatter.near_y()
    gather.finish()
    scatter.pd[...] = feed(dn).astype(BF16)
    scatter.far()
    saves.start(4, 5, 6)
    scatter.relay()
    r.out[...] = (r.after[...] + scatter.total(own[...]) + gate * row_of(pack, BIAS)).astype(BF16)
    gather.drain()
    turn_gather.drain()
    scatter.drain()
    for one in (sum_one, sum_two, sum_three):
        one.drain()
    if trade:

        @pl.when(mine)
        def _():
            for copy in trades.values():
                copy.wait_recv()

        for copy in (part_copy, *trades.values()):
            copy.wait_send()
    saves.finish()


def forward_layer(layer, ident, groups, copies, feed, vectors, own):
    trade = layer == 0
    own_vectors, got_vectors = vectors
    size, width = feed.images.shape[1:] if trade else feed.x.shape
    tokens, channels = feed.parts.shape[1:] if trade else feed.pooled.shape
    share, ff = own[OUT].shape[0], own[UP].shape[1]
    heads = share // HEAD
    saved = [
        ((tokens, width), BF16),
        ((tokens, 3 * share), BF16),
        ((heads, tokens, tokens), BF16),
        ((tokens, share), BF16),
        ((tokens, width), BF16),
        ((tokens, ff), BF16),
        ((tokens, ff), BF16),
        ((tokens, width), BF16),
        ((tokens, width), BF16),
    ]
    turned = ((tokens, width // 2), BF16)
    near_in = dict(own_vectors=own_vectors, got_vectors=got_vectors)
    far_in = dict(own_weights=own)
    near_out = dict(out=((size, width), BF16), after=((size, width), F32), gate=((8, width), F32))
    far_out = dict(saved=saved, turn_out=turned)
    scratch = dict(
        held=[pltpu.VMEM(*shape) for shape in saved],
        weights=[pltpu.VMEM(w.shape, BF16) for w in own],
        bufs_one=scatter_scratch(size, width),
        bufs_two=scatter_scratch(size, width),
        turn=pltpu.VMEM(*turned),
        own=pltpu.VMEM((size, width), F32),
        pack=pltpu.VMEM((16, width), F32),
        load_sem=pltpu.SemaphoreType.DMA((7,)),
        save_sem=pltpu.SemaphoreType.DMA((10,)),
        ag_send=pltpu.SemaphoreType.DMA((3, 6)),
        ag_recv=pltpu.SemaphoreType.DMA((3, 6)),
        rs_send=pltpu.SemaphoreType.DMA((2, 6)),
        rs_recv=pltpu.SemaphoreType.DMA((2, 6)),
        **sum_scratch(groups, copies, width),
    )
    if trade:
        near_in |= dict(flag=feed.flag, images=feed.images, cotangents=feed.cotangents, parts=feed.parts)
        near_out |= dict(x=((size, width), BF16), cot=((size, width), BF16), pooled=((tokens, channels), BF16))
        far_out |= dict(got_weights=[(w.shape, BF16) for w in own])
        scratch |= dict(
            part_other=pltpu.VMEM((tokens, channels), BF16),
            part_land=pltpu.VMEM((tokens, channels), BF16),
            core_send=pltpu.SemaphoreType.DMA((8,)),
            core_recv=pltpu.SemaphoreType.DMA((8,)),
        )
    else:
        near_in |= dict(x=feed.x, cot=feed.cot, pooled=feed.pooled)
        far_in |= dict(got_weights=feed.got_weights)
    return launch(
        functools.partial(forward_kernel, layer, groups, copies),
        "layer_forward",
        ident,
        near_in,
        far_in,
        near_out,
        far_out,
        scratch,
        20_000_000_000,
    )


def backward_kernel(layer, groups, copies, scatters, carried, gathered, r):
    dy_ref, x_ref, after_ref, pack, pooled, gate_ref = r.dy, r.x, r.after, r.pack, r.pooled, r.gate
    dx_ref, small_ref, grad_in, grad_out = r.dx, r.small, r.grad_in, r.grad_out
    held, weights, bufs = r.held, r.weights, r.bufs
    first, qkv, probs, mixed, second, hidden, slope, conv, depth = held
    dhp = slope
    wq, wo, wu, wd, gate_in, gate_out = weights
    own, dyf, daf, dmixed, dqkv, dafter, grads = r.own, r.dyf, r.daf, r.dmixed, r.dqkv, r.dafter, r.grads
    value, slots, sum_send, sum_recv = r.value, r.slots, r.sum_send, r.sum_recv
    ag_send, ag_recv, rs_send, rs_recv = r.ag_send, r.ag_recv, r.rs_send, r.rs_recv

    size, width = dy_ref.shape
    tokens, share, ff = first.shape[0], mixed.shape[1], hidden.shape[1]
    channels = pooled.shape[1]
    shards = grads.shape[0]
    cols = width // shards
    spot = place()
    me, xn, yn, dn = spot
    base_out = 3 * share
    base_conv = base_out + share
    base_up = base_conv + channels
    base_down = base_up + ff

    def rows(i):
        return pl.ds(pl.multiple_of(i * size, 16), size)

    def by_rows(base, grad, s):
        for t in range(grad.shape[1] // cols):
            grads[s, base + t * cols : base + (t + 1) * cols, :] = grad[:, t * cols : (t + 1) * cols].astype(BF16)

    def by_cols(base, grad):
        for s in range(shards):
            grads[s, base : base + grad.shape[0], :] = grad[:, s * cols : (s + 1) * cols].astype(BF16)

    loads = Loads(layer, r.own_weights, r.got_weights, weights, r.load_sem)
    saved = Copies(list(zip(r.saved, held)), r.saved_sem)
    saved.start(6)
    if gathered:
        half = width // 2
        turns = Copies([(r.turns[0], dyf.at[:, :half]), (r.turns[1], dyf.at[:, half:])], r.turn_sem)
        turns.start(0, 1)
        saved.start(5)
    loads.start(3, 2)
    peers = [{"mp": xn}, {"mp": yn}, {"mp": dn}] + others("dp", copies)
    if scatters:
        saves = Copies([] if carried else [(grads.at[:, :base_conv, :], r.late_out)], r.save_sem)
        peers.append({"pipe": 1 - lax.axis_index("pipe")})
        down = GradScatter(r.down, r.down_sem, layer, grads.at[:, base_down : base_down + ff, :])
        up = GradScatter(r.up, r.up_sem, layer, grads.at[:, base_up:base_down, :])
        mid = GradScatter(r.mid, r.mid_sem, layer, grads.at[:, base_conv:base_up, :])
        if carried:
            lates = late_parts(r.late, r.late_sems, 1 - layer, r.late_held)
            rests = late_parts(r.late, r.rest_sems, layer, grads.at[:, :base_conv, :])
            core = lax.axis_index("pipe")
            mine = core == layer
            other = {"pipe": 1 - core}
            other_loads = [
                pltpu.make_async_copy(r.down_in, down.res, r.late_sem.at[1]),
                pltpu.make_async_copy(r.up_in, up.res, r.late_sem.at[2]),
                pltpu.make_async_copy(r.mid_in, mid.res, r.late_sem.at[3]),
            ]

            @pl.when(jnp.logical_not(mine))
            def _():
                for load in other_loads:
                    load.start()

            late_load = pltpu.make_async_copy(r.late_in, r.late_held, r.late_sem.at[0])
            late_load.start()
    else:
        saves = Copies([(grads, r.grads_out)], r.save_sem)
    greet(peers)

    hold_pack(layer, r)
    if not gathered:
        dyf[rows(me), :] = dy_ref[...]
        gather = Gather(dyf, ag_send.at[0], ag_recv.at[0], spot, rows)
    scatter = Scatter(bufs, rs_send.at[0], rs_recv.at[0], spot)
    dy = dy_ref[...].astype(F32)
    dy_bias = jnp.sum(dy, axis=0, keepdims=True) * row_of(pack, BIAS)
    small_ref[...] = jnp.zeros_like(small_ref)
    def down_back():
        saved.wait(5)
        by_cols(base_down, mm(hidden[...], dyf[...], 0, 0))
        if scatters:
            down.begin()

    if gathered:
        turns.wait(0, 1)
        down_back()
    saved.wait(6)
    loads.wait(3, 2)

    def feed_back(i):
        for t in range(ff // TILE):
            lanes = slice(t * TILE, (t + 1) * TILE)
            back = mm(dyf[rows(i), :], wd[lanes, :], 1, 1)
            dhp[rows(i), lanes] = (back * slope[rows(i), lanes].astype(F32)).astype(BF16)
        return mm(dhp[rows(i), :], wu[...], 1, 1)

    if carried:
        late_load.wait()
        for late in lates:
            late.begin()
    if gathered:
        scatter.pd[...] = feed_back(dn).astype(BF16)
        scatter.far()
        saved.start(8, 4)
        scatter.px[...] = feed_back(xn).astype(BF16)
        scatter.near_x()
        if scatters:
            down.step(0)
        scatter.py[...] = feed_back(yn).astype(BF16)
        scatter.near_y()
        loads.start(1, 0, 4, 5)
        saved.start(1, 2, 3, 0, 7)
        own[...] = feed_back(me)
    else:
        own[...] = feed_back(me)
        saved.start(5, 8, 4)
        if carried:
            for late in lates:
                late.step(0)
        gather.forward()
        scatter.px[...] = feed_back(xn).astype(BF16)
        scatter.near_x()
        scatter.py[...] = feed_back(yn).astype(BF16)
        scatter.near_y()
        loads.start(1, 0, 4, 5)
        if carried:
            for late in lates:
                late.step(1)
        saved.start(1, 2, 3, 0, 7)
        gather.finish()
        scatter.pd[...] = feed_back(dn).astype(BF16)
        scatter.far()
    saved.wait(8)
    value[0] = dy_bias + jnp.sum(dyf[...].astype(F32) * depth[...].astype(F32), axis=0, keepdims=True)
    sum_one = Sum(value.at[0], slots.at[0], sum_send.at[0], sum_recv.at[0], "mp", groups)
    if not gathered:
        down_back()
    if carried:
        for late in lates:
            late.step(2)
    scatter.relay()
    value[1] = sum_one.finish()
    sum_two = Sum(value.at[1], slots.at[1], sum_send.at[1], sum_recv.at[1], "dp", copies)
    saved.wait(4)
    for s in range(shards):
        by_rows(base_up, mm(second[:, s * cols : (s + 1) * cols], dhp[...], 0, 0), s)
    if scatters:
        up.begin()
        down.step(1 if gathered else 0)
    back, gain_grad, bias_grad = norm_back(after_ref[...], row_of(pack, GAIN_TWO), scatter.total(own[...]))
    small_ref[1:2, :] = gain_grad
    small_ref[3:4, :] = bias_grad
    dafter[...] = dy + back
    daf[rows(me), :] = dafter[...].astype(BF16)
    if not gathered:
        gather.drain()
    gather = Gather(daf, ag_send.at[1], ag_recv.at[1], spot, rows)
    scatter.drain()
    scatter = Scatter(bufs, rs_send.at[1], rs_recv.at[1], spot)

    loads.wait(4, 5, 1)
    gate, mean = gate_ref[0:1, :], gate_ref[1:2, :]
    pre = sum_two.finish() * (1.0 - gate * gate)
    level, steep = gelu_parts(jnp.sum(gate_in[...].astype(F32) * mean, axis=1, keepdims=True))
    inner = jnp.sum(gate_out[...].astype(F32) * pre, axis=1, keepdims=True) * steep
    grad_out[...] = level * pre
    grad_in[...] = inner * mean
    value[2] = jnp.sum(gate_in[...].astype(F32) * inner, axis=0, keepdims=True)
    sum_three = Sum(value.at[2], slots.at[2], sum_send.at[2], sum_recv.at[2], "mp", groups)

    def mix_back(i):
        dmixed[rows(i), :] = mm(daf[rows(i), :], wo[...], 1, 1).astype(BF16)

    mix_back(me)
    if gathered and scatters:
        down.step(2)
    if scatters:
        up.step(0)
    gather.forward()
    mix_back(xn)
    mix_back(yn)
    if scatters and not gathered:
        down.step(1)
    mean_grad = sum_three.finish() * (1.0 / (copies * tokens))
    saved.wait(7)
    for t in range(shards):
        lanes = slice(t * cols, (t + 1) * cols)
        grad = gate[:, lanes] * dyf[:, lanes].astype(F32) + mean_grad[:, lanes]
        shifted = beside(conv[:, lanes].astype(F32))
        for i in range(3):
            for j in range(3):
                if i == 0:
                    terms = shifted[j][: tokens - GRID] * grad[GRID:]
                elif i == 1:
                    terms = shifted[j] * grad
                else:
                    terms = shifted[j][GRID:] * grad[: tokens - GRID]
                small_ref[4 + 3 * i + j : 5 + 3 * i + j, lanes] = jnp.sum(terms, axis=0, keepdims=True)
        small_ref[13:14, lanes] = jnp.sum(grad, axis=0, keepdims=True) * (1.0 / groups)
        back = depthwise(grad, [pack[8 - k : 9 - k, lanes] for k in range(9)])
        grads[t, base_conv : base_conv + channels, :] = mm(pooled[...], back.astype(BF16), 0, 0).astype(BF16)
    if scatters:
        mid.begin()
    if gathered and scatters:
        up.step(1)
        down.close()
    gather.finish()
    mix_back(dn)
    if gathered and scatters:
        mid.step(0)
    elif scatters:
        up.step(1)
        down.step(2)
        mid.step(0)

    saved.wait(1, 2)
    halves = lane_halves()
    scale = HEAD**-0.5
    for pair in range(share // (2 * HEAD)):
        at_query, at_key, at_value = pair_slices(pair, share)
        upper = dmixed[:, at_query]
        parts, key_grads, value_grads = [], [], []
        for h in range(2):
            low = probs[2 * pair + h]
            exact = low.astype(F32)
            grad_probs = mm(jnp.where(halves[h], upper, jnp.zeros_like(upper)), qkv[:, at_value], 1, 1)
            delta = jnp.sum(exact * grad_probs, axis=-1, keepdims=True)
            grad_scores = (exact * (grad_probs - delta)).astype(BF16)
            parts.append(mm(grad_scores, qkv[:, at_key]))
            key_grads.append(mm(grad_scores, qkv[:, at_query], 0, 0))
            value_grads.append(mm(low, upper, 0, 0))
        dqkv[:, at_query] = (jnp.where(halves[0], parts[0], parts[1]) * scale).astype(BF16)
        dqkv[:, at_key] = (jnp.where(halves[0], key_grads[0], key_grads[1]) * scale).astype(BF16)
        dqkv[:, at_value] = jnp.where(halves[0], value_grads[0], value_grads[1]).astype(BF16)
    loads.wait(0)
    if gathered and scatters:
        up.step(2)
        mid.step(1)

    def first_back(i):
        return sum(mm(dqkv[rows(i), k * share : (k + 1) * share], wq[k], 1, 1) for k in range(3))

    scatter.pd[...] = first_back(dn).astype(BF16)
    scatter.far()
    scatter.px[...] = first_back(xn).astype(BF16)
    scatter.near_x()
    scatter.py[...] = first_back(yn).astype(BF16)
    scatter.near_y()
    own[...] = first_back(me)
    saved.wait(3)
    by_cols(base_out, mm(mixed[...], daf[...], 0, 0))
    if carried:
        for late in lates:
            late.close()
        down.close()
        up.step(2)
    elif scatters:
        mid.step(2)
    scatter.relay()
    saved.wait(0)
    for s in range(shards):
        by_rows(0, mm(first[:, s * cols : (s + 1) * cols], dqkv[...], 0, 0), s)
    if carried:
        for rest in rests:
            rest.begin()
        mid.step(1)
    else:
        saves.start(0)
    back, gain_grad, bias_grad = norm_back(
        x_ref[...].astype(F32), row_of(pack, GAIN_ONE), scatter.total(own[...])
    )
    small_ref[0:1, :] = gain_grad
    small_ref[2:3, :] = bias_grad
    dx_ref[...] = (dafter[...] + back).astype(BF16)
    if scatters:
        up.close()
    if carried:
        for rest in rests:
            rest.step(0)
        mid.step(2)
        units = grad_in.shape[0]
        dafter[2 * units :, :] = jnp.where(mine, r.small_in[...], small_ref[...])
        small_copy = push(dafter.at[2 * units :, :], r.small_got, r.core_send, r.core_recv, 0, other)
        dafter[:units, :] = jnp.where(mine, r.grad_in_in[...], grad_in[...])
        dafter[units : 2 * units, :] = jnp.where(mine, r.grad_out_in[...], grad_out[...])
        gate_copy = push(dafter.at[: 2 * units, :], r.gate_got, r.core_send, r.core_recv, 1, other)
        r.trade_stage[0] = jnp.where(mine, r.outs[1][...], r.outs[0][...])
        r.trade_stage[1] = jnp.where(mine, dy_ref[...], dx_ref[...])
        trade = push(r.trade_stage, r.trade_land, r.core_send, r.core_recv, 2, other)
    elif scatters:
        mid.close()
    if carried:
        small_copy.wait_recv()
        r.total[...] = jnp.where(mine, small_ref[...], r.small_in[...]) + r.small_got[...]
        peers = [lax.rem(me + j, groups) for j in range(1, groups)]
        spread = [
            push(r.total.at[:, tile_of(peer, cols)], r.slot_a.at[j], r.last_send.at[0], r.last_recv.at[0], j, {"mp": peer})
            for j, peer in enumerate(peers)
        ]
        for rest in rests:
            rest.step(1)
        mid.close()
        down.finish()
        up.finish()
        mid.finish()

        @pl.when(jnp.logical_not(mine))
        def _():
            for load in other_loads:
                load.wait()

        results = Copies(
            [(down.res, r.down_sum), (up.res, r.up_sum), (mid.res, r.mid_sum)]
            + [(rests[i].res, r.late_sum.at[i]) for i in range(2)],
            r.done_sem,
        )
        results.start(0, 1, 2)
        gate_copy.wait_recv()
        r.gate_sum[:units, :] = jnp.where(mine, grad_in[...], r.grad_in_in[...]) + r.gate_got[:units, :]
        r.gate_sum[units:, :] = jnp.where(mine, grad_out[...], r.grad_out_in[...]) + r.gate_got[units:, :]
        for copy in spread:
            copy.wait_recv()
        r.share[...] = r.total[:, tile_of(me, cols)] + sum(r.slot_a[j] for j in range(groups - 1))
        over_copies = Sum(r.share, r.slot_b, r.last_send.at[1], r.last_recv.at[1], "dp", copies)
        for rest in rests:
            rest.step(2)
        at_me = r.whole.at[:, tile_of(me, cols)]
        at_me[...] = over_copies.finish()
        joined = [
            push(at_me, at_me, r.last_send.at[2], r.last_recv.at[2], j, {"mp": peer}) for j, peer in enumerate(peers)
        ]
        for rest in rests:
            rest.close()
        for piece in rests + lates:
            piece.finish()
        results.start(3, 4)
        for copy in joined:
            copy.wait_recv()
        r.vector_sum[...] = r.whole[...]
        trade.wait_recv()
        r.traded[...] = r.trade_land[...]
        results.finish()
        trade.wait_send()
        small_copy.wait_send()
        gate_copy.wait_send()
        over_copies.drain()
        for copy in spread + joined:
            copy.wait_send()
    gather.drain()
    scatter.drain()
    for one in (sum_one, sum_two, sum_three):
        one.drain()
    saves.finish()
    if scatters and not carried:
        for i, (piece, out) in enumerate([(down, r.down_out), (up, r.up_out), (mid, r.mid_out)]):
            piece.finish()

            @pl.when(lax.axis_index("pipe") == layer)
            def _():
                copy = pltpu.make_async_copy(piece.res, out, r.done_sem.at[i])
                copy.start()
                copy.wait()


def late_parts(bufs, signals, layer, src):
    half = src.shape[1] // 2
    return [
        GradScatter(bufs[3 * i : 3 * i + 3], signals[2 * i : 2 * i + 2], layer, src.at[:, i * half : (i + 1) * half, :])
        for i in range(2)
    ]


BACK_WEIGHTS = (QKV, OUT, UP, DOWN, GATE_IN, GATE_OUT)


def backward_layer(layer, ident, groups, copies, scatters, dy, x, fore, vectors, pooled, own, got, later=None, outs=(), turns=()):
    size, width = dy.shape
    tokens, channels = pooled.shape
    share, ff = own[OUT].shape[0], own[UP].shape[1]
    hidden = own[GATE_IN].shape[0]
    shards = width // TILE
    late_rows = 4 * share
    grads_shape = (shards, late_rows + channels + 2 * ff, TILE)
    late_shape = (shards, late_rows, TILE)
    carried, gathered = later is not None, len(turns) > 0
    own, got = ([w[i] for i in BACK_WEIGHTS] for w in (own, got))
    near_in = dict(
        dy=dy, x=x, after=fore.after, own_vectors=vectors[0], got_vectors=vectors[1], pooled=pooled, gate=fore.gate
    )
    far_in = dict(saved=fore.saved, own_weights=own, got_weights=got)
    near_out = dict(dx=((size, width), BF16))
    far_out = {}
    rows = dict(small=((16, width), F32), grad_in=((hidden, width), F32), grad_out=((hidden, width), F32))
    signals = [pltpu.SemaphoreType.DMA((8,)) for _ in range(2)]
    halves, mids = ((2, ff // 2, TILE), BF16), ((2, channels // 2, TILE), BF16)
    scratch = dict(
        held=[pltpu.VMEM(s.shape, s.dtype) for s in fore.saved],
        weights=[pltpu.VMEM(w.shape, BF16) for w in own],
        bufs=scatter_scratch(size, width),
        own=pltpu.VMEM((size, width), F32),
        pack=pltpu.VMEM((16, width), F32),
        dyf=pltpu.VMEM((tokens, width), BF16),
        daf=pltpu.VMEM((tokens, width), BF16),
        dmixed=pltpu.VMEM((tokens, share), BF16),
        dqkv=pltpu.VMEM((tokens, 3 * share), BF16),
        dafter=pltpu.VMEM((size, width), F32),
        grads=pltpu.VMEM(grads_shape, BF16),
        load_sem=pltpu.SemaphoreType.DMA((6,)),
        saved_sem=pltpu.SemaphoreType.DMA((9,)),
        save_sem=pltpu.SemaphoreType.DMA((1,)),
        ag_send=pltpu.SemaphoreType.DMA((2, 6)),
        ag_recv=pltpu.SemaphoreType.DMA((2, 6)),
        rs_send=pltpu.SemaphoreType.DMA((2, 6)),
        rs_recv=pltpu.SemaphoreType.DMA((2, 6)),
        **sum_scratch(groups, copies, width),
    )
    if scatters:
        scratch |= dict(
            down=grad_scratch(shards, ff, TILE),
            down_sem=signals,
            up=grad_scratch(shards, ff, TILE),
            up_sem=signals,
            mid=grad_scratch(shards, channels, TILE),
            mid_sem=signals,
        )
    if carried:
        near_in |= dict(small_in=later.small, grad_in_in=later.grad_in, grad_out_in=later.grad_out, outs=outs)
        far_in |= dict(late_in=later.late_out, down_in=later.down_out, up_in=later.up_out, mid_in=later.mid_out)
        near_out |= dict(
            vector_sum=((16, width), F32), gate_sum=((2 * hidden, width), F32), traded=((2, size, width), BF16)
        )
        far_out |= dict(down_sum=halves, up_sum=halves, mid_sum=mids, late_sum=((2, 2, late_rows // 4, TILE), BF16))
        scratch |= {name: pltpu.VMEM(*shape) for name, shape in rows.items()}
        most = max(groups, copies) - 1
        scratch |= dict(
            late=grad_scratch(shards, late_rows // 2, TILE) + grad_scratch(shards, late_rows // 2, TILE),
            late_sems=signals + signals,
            rest_sems=signals + signals,
            late_held=pltpu.VMEM(late_shape, BF16),
            late_sem=pltpu.SemaphoreType.DMA((4,)),
            done_sem=pltpu.SemaphoreType.DMA((5,)),
            small_got=pltpu.VMEM((16, width), F32),
            gate_got=pltpu.VMEM((2 * hidden, width), F32),
            trade_stage=pltpu.VMEM((2, size, width), BF16),
            trade_land=pltpu.VMEM((2, size, width), BF16),
            total=pltpu.VMEM((16, width), F32),
            share=pltpu.VMEM((16, TILE), F32),
            whole=pltpu.VMEM((16, width), F32),
            slot_a=pltpu.VMEM((groups - 1, 16, TILE), F32),
            slot_b=pltpu.VMEM((copies - 1, 16, TILE), F32),
            core_send=pltpu.SemaphoreType.DMA((3,)),
            core_recv=pltpu.SemaphoreType.DMA((3,)),
            last_send=pltpu.SemaphoreType.DMA((3, most)),
            last_recv=pltpu.SemaphoreType.DMA((3, most)),
        )
    else:
        near_out |= rows
        if scatters:
            far_out |= dict(late_out=(late_shape, BF16), down_out=halves, up_out=halves, mid_out=mids)
            scratch |= dict(done_sem=pltpu.SemaphoreType.DMA((3,)))
        else:
            far_out |= dict(grads_out=(grads_shape, BF16))
    if gathered:
        far_in |= dict(turns=turns)
        scratch |= dict(turn_sem=pltpu.SemaphoreType.DMA((2,)))
    return launch(
        functools.partial(backward_kernel, layer, groups, copies, scatters, carried, gathered),
        "layer_backward",
        ident,
        near_in,
        far_in,
        near_out,
        far_out,
        scratch,
        40_000_000_000,
    )


def results_kernel(share, r):
    core = lax.axis_index("pipe")
    ahead = r.flag[...] > 0.0
    for result, mine, got in ((r.layer_out, r.outs, r.traded[0]), (r.input_grad, r.grads, r.traded[1])):
        kept = jnp.where(core == 0, mine[0][...], mine[1][...])
        result[0] = jnp.where(ahead, kept, got)
        result[1] = jnp.where(ahead, got, kept)
    sums = r.vector_sum
    r.gain_grad[...] = sums[0:2, :]
    r.shift_grad[...] = sums[2:4, :]
    for k in range(9):
        r.depth_grad[k] = sums[4 + k : 5 + k, :]
    r.bias_grad[...] = sums[13:14, :]
    units = r.gate_in_grad.shape[0]
    r.gate_in_grad[...] = r.gate_sum[:units, :]
    r.gate_out_grad[...] = r.gate_sum[units:, :]
    half, cols = r.down_sum.shape[1:]
    for k in range(2):
        r.down_grad[k * half : (k + 1) * half, :] = r.down_sum[k].astype(F32)
        for t in range(half // cols):
            lanes = slice((k * (half // cols) + t) * cols, (k * (half // cols) + t + 1) * cols)
            r.up_grad[:, lanes] = r.up_sum[k, t * cols : (t + 1) * cols, :].astype(F32)
    part = r.late_sum.shape[2]

    def put(base, count, store):
        at = base
        while at < base + count:
            stop = min(base + count, (at // part + 1) * part)
            line = at % part
            rows = r.late_sum[at // (2 * part), at // part % 2, line : line + stop - at, :]
            store(slice(at - base, stop - base), rows.astype(F32))
            at = stop

    def store_qkv(k, lines, rows):
        r.qkv_grad[k, lines, :] = rows

    def store_out(lines, rows):
        r.out_grad[lines, :] = rows

    for k in range(3):
        put(k * cols, cols, functools.partial(store_qkv, k))
    put(3 * share, share, store_out)
    half = r.mid_sum.shape[1]
    for k in range(2):
        r.conv_grad[k * half : (k + 1) * half, :] = r.mid_sum[k].astype(F32)


def results(flag, outs, grads, last, share, channels):
    size, width = outs[0].shape
    cols = last.down_sum.shape[2]
    ff = 2 * last.down_sum.shape[1]
    hidden = last.gate_sum.shape[0] // 2
    return launch(
        functools.partial(results_kernel, share),
        "results",
        None,
        dict(
            flag=flag,
            outs=outs,
            grads=grads,
            traded=last.traded,
            vector_sum=last.vector_sum,
            gate_sum=last.gate_sum,
            down_sum=last.down_sum,
            up_sum=last.up_sum,
            mid_sum=last.mid_sum,
            late_sum=last.late_sum,
        ),
        {},
        dict(
            layer_out=((2, size, width), BF16),
            input_grad=((2, size, width), BF16),
            gain_grad=((2, width), F32),
            shift_grad=((2, width), F32),
            qkv_grad=((3, cols, share), F32),
            out_grad=((share, cols), F32),
            up_grad=((cols, ff), F32),
            down_grad=((ff, cols), F32),
            conv_grad=((channels, cols), F32),
            depth_grad=((9, 1, width), F32),
            bias_grad=((1, width), F32),
            gate_in_grad=((hidden, width), F32),
            gate_out_grad=((hidden, width), F32),
        ),
        {},
        {},
        1_000_000,
    )


def pool_weights(side, count, offset):
    rows_index = jnp.arange(GRID, dtype=jnp.int32)[:, None]
    cols_index = jnp.arange(count, dtype=jnp.int32)[None, :] + offset
    lower = rows_index * side // GRID
    upper = ((rows_index + 1) * side + GRID - 1) // GRID
    inside = (cols_index >= lower) & (cols_index < upper)
    return jnp.where(inside, 1.0 / (upper - lower).astype(F32), 0.0)


def pool_partial(feature, pixels, row_start):
    side = pixels * GRID // 768
    row_matrix = pool_weights(side, feature.shape[0], row_start)
    col_matrix = pool_weights(side, feature.shape[1], 0)
    first = jnp.einsum("ia,abc->ibc", row_matrix.astype(BF16), feature, preferred_element_type=F32)
    second = jnp.einsum("jb,ibc->ijc", col_matrix, first, precision=lax.Precision.HIGHEST)
    return second.reshape(GRID * GRID, feature.shape[2])


def per_device(
    inputs, cotangent, highres, resolution, assign, norm_gain, norm_bias, qkv_weight, out_weight, up_weight,
    down_weight, conv_weight, depth_weight, depth_bias, gate_in, gate_out,
):
    section = lax.axis_index("pipe")
    groups, copies = lax.axis_size("mp"), lax.axis_size("dp")
    first_half = section == 0
    order = assign[0]
    slot = order[section]

    def swap(block):
        return lax.ppermute(block, "pipe", SWAP)

    width = inputs.shape[2]
    share, channels, ff = out_weight.shape[1], conv_weight.shape[1], up_weight.shape[2]
    own_vectors = [depth_weight.transpose(1, 0, 2), depth_bias, norm_gain[0], norm_bias[0]]
    vectors = (own_vectors, [swap(v) for v in own_vectors])
    own = [
        qkv_weight[0].transpose(1, 0, 2), out_weight[0], up_weight[0], down_weight[0], conv_weight[0],
        gate_in[0], gate_out[0],
    ]
    row_start = section * highres.shape[1]
    parts = jax.vmap(pool_partial, in_axes=(0, 0, None))(highres, resolution, row_start).astype(BF16)
    flag = jnp.broadcast_to(jnp.where(slot == 0, 1.0, 0.0).astype(F32), (1, width))

    feed = types.SimpleNamespace(flag=flag, images=inputs, cotangents=cotangent, parts=parts)
    fore0 = forward_layer(0, 0, groups, copies, feed, vectors, own)
    pooled, got = fore0.pooled, fore0.got_weights
    feed = types.SimpleNamespace(x=fore0.out, cot=fore0.cot, pooled=pooled, got_weights=got)
    fore1 = forward_layer(1, 1, groups, copies, feed, vectors, own)
    scatters = copies == groups == 4 and width // TILE == copies and inputs.shape[1] == 2 * gate_in.shape[1] + 16
    outs = [fore0.out, fore1.out]
    back1 = backward_layer(
        1, 2, groups, copies, scatters, fore0.cot, fore0.out, fore1, vectors, pooled, own, got,
        turns=[fore0.turn_out, fore1.turn_out],
    )
    back0 = backward_layer(
        0, 3, groups, copies, scatters, back1.dx, fore0.x, fore0, vectors, pooled, own, got,
        back1 if scatters else None, outs,
    )
    if scatters:
        last = results(flag, outs, [back0.dx, back1.dx], back0, share, channels)
        return (
            last.layer_out[None],
            last.input_grad[None],
            last.gain_grad[None],
            last.shift_grad[None],
            last.qkv_grad.transpose(1, 0, 2)[None],
            last.out_grad[None],
            last.up_grad[None],
            last.down_grad[None],
            last.conv_grad[None],
            last.depth_grad.transpose(1, 0, 2),
            last.bias_grad,
            last.gate_in_grad[None],
            last.gate_out_grad[None],
        )

    def owned(first, second):
        kept = jnp.where(first_half, first, second)
        return kept, swap(jnp.where(first_half, second, first))

    def by_image(first, second):
        kept, received = owned(first, second)
        return jnp.where(slot == 0, jnp.stack([kept, received]), jnp.stack([received, kept]))[None]

    layer_out, input_grad = by_image(*outs), by_image(back0.dx, back1.dx)
    cols, blocks = width // copies, width // TILE
    ends = [3 * share, 4 * share, 4 * share + channels, 4 * share + channels + ff]

    def cores_sum(first, second, kind):
        kept, received = owned(first, second)
        return (kept.astype(F32) + received.astype(F32)).astype(kind)

    def scattered(blocked, dim):
        return lax.psum_scatter(blocked, "dp", scatter_dimension=dim, tiled=True).astype(F32)

    def by_rows(block):
        tiles = block.reshape(blocks, block.shape[1] // TILE, TILE, TILE)
        return scattered(tiles.transpose(0, 2, 1, 3).reshape(width, block.shape[1]), 0)

    def by_cols(block):
        return scattered(block.transpose(1, 0, 2).reshape(block.shape[1], width), 1)

    whole = cores_sum(back0.grads_out, back1.grads_out, BF16)
    small = lax.psum(cores_sum(back0.small, back1.small, F32), ("dp", "mp"))
    return (
        layer_out,
        input_grad,
        small[0:2][None],
        small[2:4][None],
        by_rows(whole[:, : ends[0]]).reshape(cols, 3, share)[None],
        by_cols(whole[:, ends[0] : ends[1]])[None],
        by_rows(whole[:, ends[2] : ends[3]])[None],
        by_cols(whole[:, ends[3] :])[None],
        by_cols(whole[:, ends[1] : ends[2]])[None],
        small[4:13][None],
        small[13][None],
        cores_sum(back0.grad_in, back1.grad_in, F32)[None],
        cores_sum(back0.grad_out, back1.grad_out, F32)[None],
    )


def solution(mesh):
    return jax.shard_map(
        per_device,
        mesh=mesh,
        in_specs=(
            P("dp", "mp", None),
            P("dp", "mp", None),
            P("dp", "pipe", None, "mp"),
            P("dp"),
            P("dp", None),
            P("pipe", None, None),
            P("pipe", None, None),
            P("pipe", None, None, "mp"),
            P("pipe", "mp", None),
            P("pipe", None, "mp"),
            P("pipe", "mp", None),
            P("pipe", "mp", None),
            P("pipe", None, None),
            P("pipe", None),
            P("pipe", "mp", None),
            P("pipe", "mp", None),
        ),
        out_specs=(
            P("pipe", "dp", "mp", None),
            P("pipe", "dp", "mp", None),
            P("pipe", None, None),
            P("pipe", None, None),
            P("pipe", "dp", None, "mp"),
            P("pipe", "mp", "dp"),
            P("pipe", "dp", "mp"),
            P("pipe", "mp", "dp"),
            P("pipe", "mp", "dp"),
            P("pipe", None, None),
            P("pipe", None),
            P("pipe", "mp", None),
            P("pipe", "mp", None),
        ),
        check_vma=False,
    )
```

```python
import functools
import types

import jax
import jax.numpy as jnp
from jax import lax
from jax.experimental import pallas as pl
from jax.experimental.pallas import tpu as pltpu
from jax.sharding import PartitionSpec as P

GRID = 24
HEAD = 64
EPS = 1e-06
TILE = 256
VMEM_BYTES = 60 * 1024 * 1024
MESH = pl.DeviceIdType.MESH
F32 = jnp.float32
BF16 = jnp.bfloat16
SWAP = [(0, 1), (1, 0)]


def mm(a, b, ca=1, cb=0):
    return lax.dot_general(a, b, (((ca,), (cb,)), ((), ())), preferred_element_type=F32)


def tile_of(index, width=TILE):
    return pl.ds(pl.multiple_of(index * width, width), width)


def place():
    me = lax.axis_index("mp")
    col, line = lax.rem(me, 2), lax.div(me, 2)
    return me, line * 2 + 1 - col, (1 - line) * 2 + col, (1 - line) * 2 + 1 - col


def greet(peers):
    barrier = pltpu.get_barrier_semaphore()
    for peer in peers:
        pl.semaphore_signal(barrier, inc=1, device_id=peer, device_id_type=MESH)
    pl.semaphore_wait(barrier, len(peers))


def push(src, dst, send, recv, slot, peer):
    copy = pltpu.make_async_remote_copy(
        src_ref=src,
        dst_ref=dst,
        send_sem=send.at[slot],
        recv_sem=recv.at[slot],
        device_id=peer,
        device_id_type=MESH,
    )
    copy.start()
    return copy


class Gather:
    def __init__(self, buf, send, recv, spot, rows):
        me, xn, yn, dn = spot
        half = buf.shape[1] // 2
        self.buf, self.send, self.recv, self.spot, self.rows = buf, send, recv, spot, rows
        self.low, self.high = pl.ds(0, half), pl.ds(half, half)
        self.near = [
            self.push(me, self.low, 0, xn),
            self.push(me, self.high, 1, yn),
            self.push(me, self.high, 2, xn),
            self.push(me, self.low, 3, yn),
        ]

    def push(self, block, half, slot, peer):
        part = self.buf.at[self.rows(block), half]
        return push(part, part, self.send, self.recv, slot, {"mp": peer})

    def forward(self):
        me, xn, yn, dn = self.spot
        self.near[0].wait_recv()
        first = self.push(xn, self.low, 4, yn)
        self.near[1].wait_recv()
        self.far = [first, self.push(yn, self.high, 5, xn)]
        self.near[2].wait_recv()
        self.near[3].wait_recv()

    def finish(self):
        for copy in self.far:
            copy.wait_recv()

    def drain(self):
        for copy in self.near + self.far:
            copy.wait_send()


class Scatter:
    def __init__(self, bufs, send, recv, spot):
        self.px, self.py, self.pd, self.via, self.rx, self.ry = bufs
        self.send, self.recv, self.spot = send, recv, spot
        width = self.px.shape[1]
        self.low, self.high = pl.ds(0, width // 2), pl.ds(width // 2, width // 2)

    def far(self):
        me, xn, yn, dn = self.spot
        self.far_copies = [
            push(self.pd.at[:, self.low], self.via.at[0], self.send, self.recv, 0, {"mp": xn}),
            push(self.pd.at[:, self.high], self.via.at[1], self.send, self.recv, 1, {"mp": yn}),
        ]

    def near_x(self):
        self.x_copy = push(
            self.px.at[:, self.low], self.rx.at[:, self.low], self.send, self.recv, 2, {"mp": self.spot[1]}
        )

    def near_y(self):
        self.y_copy = push(
            self.py.at[:, self.high], self.ry.at[:, self.high], self.send, self.recv, 3, {"mp": self.spot[2]}
        )

    def relay(self):
        me, xn, yn, dn = self.spot
        self.far_copies[0].wait_recv()
        self.py[:, self.low] = (self.py[:, self.low].astype(F32) + self.via[0].astype(F32)).astype(BF16)
        first = push(self.py.at[:, self.low], self.ry.at[:, self.low], self.send, self.recv, 4, {"mp": yn})
        self.far_copies[1].wait_recv()
        self.px[:, self.high] = (self.px[:, self.high].astype(F32) + self.via[1].astype(F32)).astype(BF16)
        second = push(self.px.at[:, self.high], self.rx.at[:, self.high], self.send, self.recv, 5, {"mp": xn})
        self.last_copies = [first, second]

    def total(self, own):
        for copy in [self.x_copy, self.y_copy] + self.last_copies:
            copy.wait_recv()
        return own + self.rx[...].astype(F32) + self.ry[...].astype(F32)

    def drain(self):
        for copy in self.far_copies + [self.x_copy, self.y_copy] + self.last_copies:
            copy.wait_send()


def scatter_scratch(rows, width):
    return [
        pltpu.VMEM((rows, width), BF16),
        pltpu.VMEM((rows, width), BF16),
        pltpu.VMEM((rows, width), BF16),
        pltpu.VMEM((2, rows, width // 2), BF16),
        pltpu.VMEM((rows, width), BF16),
        pltpu.VMEM((rows, width), BF16),
    ]


def norm_rows(values, gain, shift):
    center = values - jnp.mean(values, axis=-1, keepdims=True)
    spread = jnp.mean(center * center, axis=-1, keepdims=True)
    return center * lax.rsqrt(spread + EPS) * gain + shift


def norm_back(values, gain, grad):
    center = values - jnp.mean(values, axis=-1, keepdims=True)
    scale = lax.rsqrt(jnp.mean(center * center, axis=-1, keepdims=True) + EPS)
    unit = center * scale
    scaled = grad * gain
    mean_one = jnp.mean(scaled, axis=-1, keepdims=True)
    mean_two = jnp.mean(scaled * unit, axis=-1, keepdims=True)
    back = scale * (scaled - mean_one - unit * mean_two)
    return back, jnp.sum(grad * unit, axis=0, keepdims=True), jnp.sum(grad, axis=0, keepdims=True)


def gelu_parts(values):
    below = 0.5 * (1.0 + lax.erf(values * 0.7071067811865476))
    bell = jnp.exp(-0.5 * values * values) * 0.3989422804014327
    return values * below, below + values * bell


class Sum:
    def __init__(self, value, slots, send, recv, axis, count):
        self.value, self.slots = value, slots
        self.copies = [push(value, slots.at[j], send, recv, j, peer) for j, peer in enumerate(others(axis, count))]

    def finish(self):
        for copy in self.copies:
            copy.wait_recv()
        total = self.value[...]
        for j in range(len(self.copies)):
            total = total + self.slots[j]
        return total

    def drain(self):
        for copy in self.copies:
            copy.wait_send()


def others(axis, count):
    me = lax.axis_index(axis)
    return [{axis: lax.rem(me + j, count)} for j in range(1, count)]


def sum_scratch(groups, copies, width):
    most = max(groups, copies) - 1
    return dict(
        value=pltpu.VMEM((3, 1, width), F32),
        slots=pltpu.VMEM((3, most, 1, width), F32),
        sum_send=pltpu.SemaphoreType.DMA((3, most)),
        sum_recv=pltpu.SemaphoreType.DMA((3, most)),
    )


class Loads:
    def __init__(self, layer, own, got, held, sems):
        self.mine = lax.axis_index("pipe") == layer
        self.own, self.got, self.held, self.sems = own, got, held, sems

    def start(self, *which):
        for i in which:

            @pl.when(self.mine)
            def _():
                pltpu.make_async_copy(self.own[i], self.held[i], self.sems.at[i]).start()

            @pl.when(jnp.logical_not(self.mine))
            def _():
                pltpu.make_async_copy(self.got[i], self.held[i], self.sems.at[i]).start()

    def wait(self, *which):
        for i in which:
            pltpu.make_async_copy(self.own[i], self.held[i], self.sems.at[i]).wait()


class Copies:
    def __init__(self, pairs, sems):
        self.copies = [pltpu.make_async_copy(src, dst, sems.at[i]) for i, (src, dst) in enumerate(pairs)]
        self.started = []

    def start(self, *which):
        for i in which:
            self.copies[i].start()
            self.started.append(i)

    def wait(self, *which):
        for i in which:
            self.copies[i].wait()
            self.started.remove(i)

    def finish(self):
        self.wait(*list(self.started))


BIAS, GAIN_ONE, GAIN_TWO, SHIFT_ONE, SHIFT_TWO = 9, 10, 11, 12, 13
QKV, OUT, UP, DOWN, CONV, GATE_IN, GATE_OUT = range(7)


def row_of(pack, index):
    return pack[index : index + 1, :]


def beside(field):
    cells, width = field.shape
    index = lax.broadcasted_iota(jnp.int32, (cells, width), 0)
    col = index - lax.shift_right_logical(index * 2731, 16) * GRID
    before = jnp.where(col >= 1, pltpu.roll(field, 1, 0), 0.0)
    behind = jnp.where(col <= GRID - 2, pltpu.roll(field, cells - 1, 0), 0.0)
    return before, field, behind


def depthwise(field, kernel):
    cells, width = field.shape
    shifted = beside(field)
    lines = [sum(kernel[3 * i + j] * shifted[j] for j in range(3)) for i in range(3)]
    none = jnp.zeros((GRID, width), F32)
    above = jnp.concatenate([none, lines[0][: cells - GRID]], axis=0)
    below = jnp.concatenate([lines[2][GRID:], none], axis=0)
    return above + lines[1] + below


def lane_halves():
    lane = lax.broadcasted_iota(jnp.int32, (1, 2 * HEAD), 1)
    return [lane < HEAD, lane >= HEAD]


def pair_slices(pair, share):
    return [slice(base + pair * 2 * HEAD, base + (pair + 1) * 2 * HEAD) for base in (0, share, 2 * share)]


class GradScatter:
    def __init__(self, bufs, signals, layer, src):
        self.src, self.layer = src, layer
        self.got, self.came, self.res = bufs
        self.send, self.recv = signals
        self.core, self.z = lax.axis_index("pipe"), lax.axis_index("dp")
        half = src.shape[1] // 2
        self.mine = pl.ds(pl.multiple_of(self.core * half, 16), half)
        self.theirs = pl.ds(pl.multiple_of((1 - self.core) * half, 16), half)
        self.steps = [[self.travel(way, k) for k in range(3)] for way in range(2)]
        self.final = self.describe(self.part(self.z), self.res.at[self.core], 7, {"pipe": 1 - self.core})

    def part(self, shard):
        return self.src.at[shard, self.mine, :]

    def describe(self, src, dst, slot, peer):
        return pltpu.make_async_remote_copy(
            src_ref=src,
            dst_ref=dst,
            send_sem=self.send.at[slot],
            recv_sem=self.recv.at[slot],
            device_id=peer,
            device_id_type=MESH,
        )

    def place(self, way):
        return self.z if way == 0 else 3 - self.z

    def shard(self, way, k):
        far = lax.rem(3 - k + self.place(way), 4)
        return far if way == 0 else 3 - far

    def travel(self, way, k):
        peer = lax.rem(self.z + (1 if way == 0 else 3), 4)
        return self.describe(
            self.part(self.shard(way, k)), self.came.at[way, k], 1 + 3 * way + k, {"dp": peer}
        )

    def add(self, shard, way, k):
        self.steps[way][k].wait_recv()
        self.src[shard, self.mine, :] = (
            self.src[shard, self.mine, :].astype(F32) + self.came[way, k].astype(F32)
        ).astype(BF16)

    def begin(self):
        self.swap = push(self.src.at[:, self.theirs, :], self.got, self.send, self.recv, 0, {"pipe": 1 - self.core})

    def step(self, k):
        if k == 0:
            self.swap.wait_recv()
            for s in range(4):
                self.src[s, self.mine, :] = (
                    self.src[s, self.mine, :].astype(F32) + self.got[s].astype(F32)
                ).astype(BF16)
        for way in range(2):
            if k > 0:

                @pl.when((self.place(way) >= 1) & (self.place(way) <= k))
                def _():
                    self.add(self.shard(way, k), way, k - 1)

            @pl.when(self.place(way) <= k)
            def _():
                self.steps[way][k].start()

    def close(self):
        for way in range(2):

            @pl.when(self.place(way) >= 1)
            def _():
                self.add(self.z, way, 2)

        @pl.when(self.core == self.layer)
        def _():
            self.res[self.core] = self.src[self.z, self.mine, :]

        @pl.when(self.core != self.layer)
        def _():
            self.final.start()

    def finish(self):
        @pl.when(self.core == self.layer)
        def _():
            self.final.wait_recv()

        @pl.when(self.core != self.layer)
        def _():
            self.final.wait_send()

        for way in range(2):
            for k in range(3):

                @pl.when(self.place(way) <= k)
                def _():
                    self.steps[way][k].wait_send()

        self.swap.wait_send()


def grad_scratch(shards, rows, cols):
    half = rows // 2
    return [
        pltpu.VMEM((shards, half, cols), BF16),
        pltpu.VMEM((2, 3, half, cols), BF16),
        pltpu.VMEM((2, half, cols), BF16),
    ]


def talk(ident):
    if ident is None:
        return pltpu.CompilerParams(vmem_limit_bytes=VMEM_BYTES)
    return pltpu.CompilerParams(collective_id=ident, has_side_effects=True, vmem_limit_bytes=VMEM_BYTES)


def launch(body, name, ident, near_in, far_in, near_out, far_out, scratch, flops):
    def flat(group):
        return [item for value in group.values() for item in (value if isinstance(value, list) else [value])]

    def named(groups, items):
        rest = iter(items)
        space = types.SimpleNamespace()
        for key, value in (pair for group in groups for pair in group.items()):
            setattr(space, key, [next(rest) for _ in value] if isinstance(value, list) else next(rest))
        return space

    def kernel(*refs):
        body(named((near_in, far_in, near_out, far_out, scratch), refs))

    vmem, anywhere = pl.BlockSpec(memory_space=pltpu.VMEM), pl.BlockSpec(memory_space=pl.ANY)
    outs = pl.pallas_call(
        kernel,
        out_shape=[jax.ShapeDtypeStruct(*shape) for shape in flat(near_out) + flat(far_out)],
        in_specs=[vmem] * len(flat(near_in)) + [anywhere] * len(flat(far_in)),
        out_specs=[vmem] * len(flat(near_out)) + [anywhere] * len(flat(far_out)),
        scratch_shapes=flat(scratch),
        compiler_params=talk(ident),
        cost_estimate=pl.CostEstimate(flops=flops, bytes_accessed=40_000_000, transcendentals=0),
        name=name,
    )(*flat(near_in), *flat(far_in))
    return named((near_out, far_out), outs)


def hold_pack(layer, r):
    mine = lax.axis_index("pipe") == layer
    for k in range(9):
        r.pack[k : k + 1, :] = jnp.where(mine, r.own_vectors[0][k], r.got_vectors[0][k])
    at = BIAS
    for own, got in zip(r.own_vectors[1:], r.got_vectors[1:]):
        r.pack[at : at + own.shape[0], :] = jnp.where(mine, own[...], got[...])
        at += own.shape[0]


def forward_kernel(layer, groups, copies, r):
    trade = layer == 0
    saved, weights = r.held, r.weights
    first, qkv, probs, mixed, second, hidden, slope, conv, depth = saved
    wq, wo, wu, wd, wc, gate_in, gate_out = weights
    own_w, got_w = r.own_weights, r.got_weights
    own, value, slots, pack, turn = r.own, r.value, r.slots, r.pack, r.turn

    size, width = own.shape
    half = width // 2
    tokens, share, ff = first.shape[0], mixed.shape[1], hidden.shape[1]
    spot = place()
    me, xn, yn, dn = spot
    core = lax.axis_index("pipe")
    mine = core == layer

    def rows(i):
        return pl.ds(pl.multiple_of(i * size, 16), size)

    loads = Loads(layer, own_w, got_w, weights, r.load_sem)
    saves = Copies(
        list(zip(saved, r.saved)) + [(turn, r.turn_out)], r.save_sem
    )
    peers = [{"mp": xn}, {"mp": yn}, {"mp": dn}] + others("dp", copies)
    if trade:

        @pl.when(mine)
        def _():
            for i in (CONV, QKV, OUT, GATE_IN, GATE_OUT):
                pltpu.make_async_copy(own_w[i], weights[i], r.load_sem.at[i]).start()

        other = {"pipe": 1 - core}
        ahead = r.flag[...] > 0.0
        r.x[...] = jnp.where(ahead, r.images[0], r.images[1])
        r.cot[...] = jnp.where(ahead, r.cotangents[0], r.cotangents[1])
        channels = r.pooled.shape[1]
        r.part_other[...] = jnp.where(ahead[:, :channels], r.parts[1], r.parts[0])
        greet(peers + [other])
        part_copy = push(r.part_other, r.part_land, r.core_send, r.core_recv, 7, other)
        trades = {
            i: push(own_w[i], got_w[i], r.core_send, r.core_recv, i, other)
            for i in (CONV, QKV, OUT, GATE_IN, GATE_OUT, UP, DOWN)
        }

        def arrive(*which):
            @pl.when(jnp.logical_not(mine))
            def _():
                for i in which:
                    trades[i].wait_recv()
                    pltpu.make_async_copy(got_w[i], weights[i], r.load_sem.at[i]).start()

    else:
        loads.start(CONV, QKV, OUT, GATE_IN, GATE_OUT)

        def arrive(*which):
            pass

        greet(peers)
    hold_pack(layer, r)

    x = r.x[...].astype(F32)
    first[rows(me), :] = norm_rows(x, row_of(pack, GAIN_ONE), row_of(pack, SHIFT_ONE)).astype(BF16)
    gather = Gather(first, r.ag_send.at[0], r.ag_recv.at[0], spot, rows)

    if trade:
        part_copy.wait_recv()
        part = jnp.where(ahead[:, :channels], r.parts[0], r.parts[1])
        r.pooled[...] = (part.astype(F32) + r.part_land[...].astype(F32)).astype(BF16)
    arrive(CONV)
    loads.wait(CONV)
    mapped = mm(r.pooled[...], wc[...])
    for t in range(width // TILE):
        lanes = slice(t * TILE, (t + 1) * TILE)
        conv[:, lanes] = mapped[:, lanes].astype(BF16)
        filtered = depthwise(mapped[:, lanes], [pack[k : k + 1, lanes] for k in range(9)])
        depth[:, lanes] = filtered.astype(BF16)
        value[0, :, lanes] = jnp.sum(filtered, axis=0, keepdims=True)
    sum_one = Sum(value.at[0], slots.at[0], r.sum_send.at[0], r.sum_recv.at[0], "mp", groups)
    saves.start(7, 8)

    def project(i):
        for k in range(3):
            qkv[rows(i), k * share : (k + 1) * share] = mm(first[rows(i), :], wq[k]).astype(BF16)

    arrive(QKV)
    loads.wait(QKV)
    project(me)
    gather.forward()
    if trade:
        arrive(OUT, GATE_IN, GATE_OUT, UP, DOWN)

        @pl.when(mine)
        def _():
            for i in (UP, DOWN):
                pltpu.make_async_copy(own_w[i], weights[i], r.load_sem.at[i]).start()

    else:
        loads.start(UP, DOWN)
    value[1] = sum_one.finish()
    sum_two = Sum(value.at[1], slots.at[1], r.sum_send.at[1], r.sum_recv.at[1], "dp", copies)
    project(xn)
    project(yn)
    turn[rows(me), :] = r.cot[:, layer * half : (layer + 1) * half]
    gather.finish()
    turn_gather = Gather(turn, r.ag_send.at[2], r.ag_recv.at[2], spot, rows)
    project(dn)
    saves.start(0, 1)

    halves = lane_halves()
    for pair in range(share // (2 * HEAD)):
        at_query, at_key, at_value = pair_slices(pair, share)
        query = qkv[:, at_query] * jnp.asarray(HEAD**-0.5, BF16)
        parts = []
        for h in range(2):
            scores = mm(jnp.where(halves[h], query, jnp.zeros_like(query)), qkv[:, at_key], 1, 1)
            raised = jnp.exp(scores - jnp.max(scores, axis=-1, keepdims=True))
            chances = (raised * (1.0 / jnp.sum(raised, axis=-1, keepdims=True))).astype(BF16)
            probs[2 * pair + h] = chances
            parts.append(mm(chances, qkv[:, at_value]))
        mixed[:, at_query] = jnp.where(halves[0], parts[0], parts[1]).astype(BF16)

    loads.wait(OUT, GATE_IN, GATE_OUT)
    turn_gather.forward()
    scatter = Scatter(r.bufs_one, r.rs_send.at[0], r.rs_recv.at[0], spot)

    def out_part(i):
        return mm(mixed[rows(i), :], wo[...])

    scatter.pd[...] = out_part(dn).astype(BF16)
    scatter.far()
    scatter.px[...] = out_part(xn).astype(BF16)
    scatter.near_x()
    scatter.py[...] = out_part(yn).astype(BF16)
    scatter.near_y()
    own[...] = out_part(me)
    saves.start(2, 3)
    mean = sum_two.finish() * (1.0 / (copies * tokens)) + row_of(pack, BIAS)
    level = gelu_parts(jnp.sum(gate_in[...].astype(F32) * mean, axis=1, keepdims=True))[0]
    value[2] = jnp.sum(level * gate_out[...].astype(F32), axis=0, keepdims=True)
    sum_three = Sum(value.at[2], slots.at[2], r.sum_send.at[2], r.sum_recv.at[2], "mp", groups)
    scatter.relay()
    after = x + scatter.total(own[...])
    r.after[...] = after
    second[rows(me), :] = norm_rows(after, row_of(pack, GAIN_TWO), row_of(pack, SHIFT_TWO)).astype(BF16)
    gather.drain()
    gather = Gather(second, r.ag_send.at[1], r.ag_recv.at[1], spot, rows)
    scatter.drain()
    turn_gather.finish()
    saves.start(9)
    gate = jnp.tanh(sum_three.finish())
    r.gate[...] = jnp.concatenate([gate, mean, jnp.zeros((6, width), F32)], axis=0)
    loads.wait(UP, DOWN)

    def feed(i):
        for t in range(ff // TILE):
            lanes = slice(t * TILE, (t + 1) * TILE)
            level, grad = gelu_parts(mm(second[rows(i), :], wu[:, lanes]))
            hidden[rows(i), lanes] = level.astype(BF16)
            slope[rows(i), lanes] = grad.astype(BF16)
        return mm(hidden[rows(i), :], wd[...]) + gate * depth[rows(i), :].astype(F32)

    scatter = Scatter(r.bufs_two, r.rs_send.at[1], r.rs_recv.at[1], spot)
    own[...] = feed(me)
    gather.forward()
    scatter.px[...] = feed(xn).astype(BF16)
    scatter.near_x()
    scatter.py[...] = feed(yn).astype(BF16)
    scatter.near_y()
    gather.finish()
    scatter.pd[...] = feed(dn).astype(BF16)
    scatter.far()
    saves.start(4, 5, 6)
    scatter.relay()
    r.out[...] = (r.after[...] + scatter.total(own[...]) + gate * row_of(pack, BIAS)).astype(BF16)
    gather.drain()
    turn_gather.drain()
    scatter.drain()
    for one in (sum_one, sum_two, sum_three):
        one.drain()
    if trade:

        @pl.when(mine)
        def _():
            for copy in trades.values():
                copy.wait_recv()

        for copy in (part_copy, *trades.values()):
            copy.wait_send()
    saves.finish()


def forward_layer(layer, ident, groups, copies, feed, vectors, own):
    trade = layer == 0
    own_vectors, got_vectors = vectors
    size, width = feed.images.shape[1:] if trade else feed.x.shape
    tokens, channels = feed.parts.shape[1:] if trade else feed.pooled.shape
    share, ff = own[OUT].shape[0], own[UP].shape[1]
    heads = share // HEAD
    saved = [
        ((tokens, width), BF16),
        ((tokens, 3 * share), BF16),
        ((heads, tokens, tokens), BF16),
        ((tokens, share), BF16),
        ((tokens, width), BF16),
        ((tokens, ff), BF16),
        ((tokens, ff), BF16),
        ((tokens, width), BF16),
        ((tokens, width), BF16),
    ]
    turned = ((tokens, width // 2), BF16)
    near_in = dict(own_vectors=own_vectors, got_vectors=got_vectors)
    far_in = dict(own_weights=own)
    near_out = dict(out=((size, width), BF16), after=((size, width), F32), gate=((8, width), F32))
    far_out = dict(saved=saved, turn_out=turned)
    scratch = dict(
        held=[pltpu.VMEM(*shape) for shape in saved],
        weights=[pltpu.VMEM(w.shape, BF16) for w in own],
        bufs_one=scatter_scratch(size, width),
        bufs_two=scatter_scratch(size, width),
        turn=pltpu.VMEM(*turned),
        own=pltpu.VMEM((size, width), F32),
        pack=pltpu.VMEM((16, width), F32),
        load_sem=pltpu.SemaphoreType.DMA((7,)),
        save_sem=pltpu.SemaphoreType.DMA((10,)),
        ag_send=pltpu.SemaphoreType.DMA((3, 6)),
        ag_recv=pltpu.SemaphoreType.DMA((3, 6)),
        rs_send=pltpu.SemaphoreType.DMA((2, 6)),
        rs_recv=pltpu.SemaphoreType.DMA((2, 6)),
        **sum_scratch(groups, copies, width),
    )
    if trade:
        near_in |= dict(flag=feed.flag, images=feed.images, cotangents=feed.cotangents, parts=feed.parts)
        near_out |= dict(x=((size, width), BF16), cot=((size, width), BF16), pooled=((tokens, channels), BF16))
        far_out |= dict(got_weights=[(w.shape, BF16) for w in own])
        scratch |= dict(
            part_other=pltpu.VMEM((tokens, channels), BF16),
            part_land=pltpu.VMEM((tokens, channels), BF16),
            core_send=pltpu.SemaphoreType.DMA((8,)),
            core_recv=pltpu.SemaphoreType.DMA((8,)),
        )
    else:
        near_in |= dict(x=feed.x, cot=feed.cot, pooled=feed.pooled)
        far_in |= dict(got_weights=feed.got_weights)
    return launch(
        functools.partial(forward_kernel, layer, groups, copies),
        "layer_forward",
        ident,
        near_in,
        far_in,
        near_out,
        far_out,
        scratch,
        20_000_000_000,
    )


def backward_kernel(layer, groups, copies, scatters, carried, gathered, r):
    dy_ref, x_ref, after_ref, pack, pooled, gate_ref = r.dy, r.x, r.after, r.pack, r.pooled, r.gate
    dx_ref, small_ref, grad_in, grad_out = r.dx, r.small, r.grad_in, r.grad_out
    held, weights, bufs = r.held, r.weights, r.bufs
    first, qkv, probs, mixed, second, hidden, slope, conv, depth = held
    dhp = slope
    wq, wo, wu, wd, gate_in, gate_out = weights
    own, dyf, daf, dmixed, dqkv, dafter, grads = r.own, r.dyf, r.daf, r.dmixed, r.dqkv, r.dafter, r.grads
    value, slots, sum_send, sum_recv = r.value, r.slots, r.sum_send, r.sum_recv
    ag_send, ag_recv, rs_send, rs_recv = r.ag_send, r.ag_recv, r.rs_send, r.rs_recv

    size, width = dy_ref.shape
    tokens, share, ff = first.shape[0], mixed.shape[1], hidden.shape[1]
    channels = pooled.shape[1]
    shards = grads.shape[0]
    cols = width // shards
    spot = place()
    me, xn, yn, dn = spot
    base_out = 3 * share
    base_conv = base_out + share
    base_up = base_conv + channels
    base_down = base_up + ff

    def rows(i):
        return pl.ds(pl.multiple_of(i * size, 16), size)

    def by_rows(base, grad, s):
        for t in range(grad.shape[1] // cols):
            grads[s, base + t * cols : base + (t + 1) * cols, :] = grad[:, t * cols : (t + 1) * cols].astype(BF16)

    def by_cols(base, grad):
        for s in range(shards):
            grads[s, base : base + grad.shape[0], :] = grad[:, s * cols : (s + 1) * cols].astype(BF16)

    loads = Loads(layer, r.own_weights, r.got_weights, weights, r.load_sem)
    saved = Copies(list(zip(r.saved, held)), r.saved_sem)
    saved.start(6)
    if gathered:
        half = width // 2
        turns = Copies([(r.turns[0], dyf.at[:, :half]), (r.turns[1], dyf.at[:, half:])], r.turn_sem)
        turns.start(0, 1)
        saved.start(5)
    loads.start(3, 2)
    peers = [{"mp": xn}, {"mp": yn}, {"mp": dn}] + others("dp", copies)
    if scatters:
        saves = Copies([] if carried else [(grads.at[:, :base_conv, :], r.late_out)], r.save_sem)
        peers.append({"pipe": 1 - lax.axis_index("pipe")})
        down = GradScatter(r.down, r.down_sem, layer, grads.at[:, base_down : base_down + ff, :])
        up = GradScatter(r.up, r.up_sem, layer, grads.at[:, base_up:base_down, :])
        mid = GradScatter(r.mid, r.mid_sem, layer, grads.at[:, base_conv:base_up, :])
        if carried:
            lates = late_parts(r.late, r.late_sems, 1 - layer, r.late_held)
            rests = late_parts(r.late, r.rest_sems, layer, grads.at[:, :base_conv, :])
            core = lax.axis_index("pipe")
            mine = core == layer
            other = {"pipe": 1 - core}
            other_loads = [
                pltpu.make_async_copy(r.down_in, down.res, r.late_sem.at[1]),
                pltpu.make_async_copy(r.up_in, up.res, r.late_sem.at[2]),
                pltpu.make_async_copy(r.mid_in, mid.res, r.late_sem.at[3]),
            ]

            @pl.when(jnp.logical_not(mine))
            def _():
                for load in other_loads:
                    load.start()

            late_load = pltpu.make_async_copy(r.late_in, r.late_held, r.late_sem.at[0])
            late_load.start()
    else:
        saves = Copies([(grads, r.grads_out)], r.save_sem)
    greet(peers)

    hold_pack(layer, r)
    if not gathered:
        dyf[rows(me), :] = dy_ref[...]
        gather = Gather(dyf, ag_send.at[0], ag_recv.at[0], spot, rows)
    scatter = Scatter(bufs, rs_send.at[0], rs_recv.at[0], spot)
    dy = dy_ref[...].astype(F32)
    dy_bias = jnp.sum(dy, axis=0, keepdims=True) * row_of(pack, BIAS)
    small_ref[...] = jnp.zeros_like(small_ref)
    def down_back():
        saved.wait(5)
        by_cols(base_down, mm(hidden[...], dyf[...], 0, 0))
        if scatters:
            down.begin()

    if gathered:
        turns.wait(0, 1)
        down_back()
    saved.wait(6)
    loads.wait(3, 2)

    def feed_back(i):
        for t in range(ff // TILE):
            lanes = slice(t * TILE, (t + 1) * TILE)
            back = mm(dyf[rows(i), :], wd[lanes, :], 1, 1)
            dhp[rows(i), lanes] = (back * slope[rows(i), lanes].astype(F32)).astype(BF16)
        return mm(dhp[rows(i), :], wu[...], 1, 1)

    if carried:
        late_load.wait()
        for late in lates:
            late.begin()
    if gathered:
        scatter.pd[...] = feed_back(dn).astype(BF16)
        scatter.far()
        saved.start(8, 4)
        scatter.px[...] = feed_back(xn).astype(BF16)
        scatter.near_x()
        if scatters:
            down.step(0)
        scatter.py[...] = feed_back(yn).astype(BF16)
        scatter.near_y()
        loads.start(1, 0, 4, 5)
        saved.start(1, 2, 3, 0, 7)
        own[...] = feed_back(me)
    else:
        own[...] = feed_back(me)
        saved.start(5, 8, 4)
        if carried:
            for late in lates:
                late.step(0)
        gather.forward()
        scatter.px[...] = feed_back(xn).astype(BF16)
        scatter.near_x()
        scatter.py[...] = feed_back(yn).astype(BF16)
        scatter.near_y()
        loads.start(1, 0, 4, 5)
        if carried:
            for late in lates:
                late.step(1)
        saved.start(1, 2, 3, 0, 7)
        gather.finish()
        scatter.pd[...] = feed_back(dn).astype(BF16)
        scatter.far()
    saved.wait(8)
    value[0] = dy_bias + jnp.sum(dyf[...].astype(F32) * depth[...].astype(F32), axis=0, keepdims=True)
    sum_one = Sum(value.at[0], slots.at[0], sum_send.at[0], sum_recv.at[0], "mp", groups)
    if not gathered:
        down_back()
    if carried:
        for late in lates:
            late.step(2)
    scatter.relay()
    value[1] = sum_one.finish()
    sum_two = Sum(value.at[1], slots.at[1], sum_send.at[1], sum_recv.at[1], "dp", copies)
    saved.wait(4)
    for s in range(shards):
        by_rows(base_up, mm(second[:, s * cols : (s + 1) * cols], dhp[...], 0, 0), s)
    if scatters:
        up.begin()
        down.step(1 if gathered else 0)
    back, gain_grad, bias_grad = norm_back(after_ref[...], row_of(pack, GAIN_TWO), scatter.total(own[...]))
    small_ref[1:2, :] = gain_grad
    small_ref[3:4, :] = bias_grad
    dafter[...] = dy + back
    daf[rows(me), :] = dafter[...].astype(BF16)
    if not gathered:
        gather.drain()
    gather = Gather(daf, ag_send.at[1], ag_recv.at[1], spot, rows)
    scatter.drain()
    scatter = Scatter(bufs, rs_send.at[1], rs_recv.at[1], spot)

    loads.wait(4, 5, 1)
    gate, mean = gate_ref[0:1, :], gate_ref[1:2, :]
    pre = sum_two.finish() * (1.0 - gate * gate)
    level, steep = gelu_parts(jnp.sum(gate_in[...].astype(F32) * mean, axis=1, keepdims=True))
    inner = jnp.sum(gate_out[...].astype(F32) * pre, axis=1, keepdims=True) * steep
    grad_out[...] = level * pre
    grad_in[...] = inner * mean
    value[2] = jnp.sum(gate_in[...].astype(F32) * inner, axis=0, keepdims=True)
    sum_three = Sum(value.at[2], slots.at[2], sum_send.at[2], sum_recv.at[2], "mp", groups)

    def mix_back(i):
        dmixed[rows(i), :] = mm(daf[rows(i), :], wo[...], 1, 1).astype(BF16)

    mix_back(me)
    if gathered and scatters:
        down.step(2)
    if scatters:
        up.step(0)
    gather.forward()
    mix_back(xn)
    mix_back(yn)
    if scatters and not gathered:
        down.step(1)
    mean_grad = sum_three.finish() * (1.0 / (copies * tokens))
    saved.wait(7)
    for t in range(shards):
        lanes = slice(t * cols, (t + 1) * cols)
        grad = gate[:, lanes] * dyf[:, lanes].astype(F32) + mean_grad[:, lanes]
        shifted = beside(conv[:, lanes].astype(F32))
        for i in range(3):
            for j in range(3):
                if i == 0:
                    terms = shifted[j][: tokens - GRID] * grad[GRID:]
                elif i == 1:
                    terms = shifted[j] * grad
                else:
                    terms = shifted[j][GRID:] * grad[: tokens - GRID]
                small_ref[4 + 3 * i + j : 5 + 3 * i + j, lanes] = jnp.sum(terms, axis=0, keepdims=True)
        small_ref[13:14, lanes] = jnp.sum(grad, axis=0, keepdims=True) * (1.0 / groups)
        back = depthwise(grad, [pack[8 - k : 9 - k, lanes] for k in range(9)])
        grads[t, base_conv : base_conv + channels, :] = mm(pooled[...], back.astype(BF16), 0, 0).astype(BF16)
    if scatters:
        mid.begin()
    if gathered and scatters:
        up.step(1)
        down.close()
    gather.finish()
    mix_back(dn)
    if gathered and scatters:
        mid.step(0)
    elif scatters:
        up.step(1)
        down.step(2)
        mid.step(0)

    saved.wait(1, 2)
    halves = lane_halves()
    scale = HEAD**-0.5
    for pair in range(share // (2 * HEAD)):
        at_query, at_key, at_value = pair_slices(pair, share)
        upper = dmixed[:, at_query]
        parts, key_grads, value_grads = [], [], []
        for h in range(2):
            low = probs[2 * pair + h]
            exact = low.astype(F32)
            grad_probs = mm(jnp.where(halves[h], upper, jnp.zeros_like(upper)), qkv[:, at_value], 1, 1)
            delta = jnp.sum(exact * grad_probs, axis=-1, keepdims=True)
            grad_scores = (exact * (grad_probs - delta)).astype(BF16)
            parts.append(mm(grad_scores, qkv[:, at_key]))
            key_grads.append(mm(grad_scores, qkv[:, at_query], 0, 0))
            value_grads.append(mm(low, upper, 0, 0))
        dqkv[:, at_query] = (jnp.where(halves[0], parts[0], parts[1]) * scale).astype(BF16)
        dqkv[:, at_key] = (jnp.where(halves[0], key_grads[0], key_grads[1]) * scale).astype(BF16)
        dqkv[:, at_value] = jnp.where(halves[0], value_grads[0], value_grads[1]).astype(BF16)
    loads.wait(0)
    if gathered and scatters:
        up.step(2)
        mid.step(1)

    def first_back(i):
        return sum(mm(dqkv[rows(i), k * share : (k + 1) * share], wq[k], 1, 1) for k in range(3))

    scatter.pd[...] = first_back(dn).astype(BF16)
    scatter.far()
    scatter.px[...] = first_back(xn).astype(BF16)
    scatter.near_x()
    scatter.py[...] = first_back(yn).astype(BF16)
    scatter.near_y()
    own[...] = first_back(me)
    saved.wait(3)
    by_cols(base_out, mm(mixed[...], daf[...], 0, 0))
    if carried:
        for late in lates:
            late.close()
        down.close()
        up.step(2)
    elif scatters:
        mid.step(2)
    scatter.relay()
    saved.wait(0)
    for s in range(shards):
        by_rows(0, mm(first[:, s * cols : (s + 1) * cols], dqkv[...], 0, 0), s)
    if carried:
        for rest in rests:
            rest.begin()
        mid.step(1)
    else:
        saves.start(0)
    back, gain_grad, bias_grad = norm_back(
        x_ref[...].astype(F32), row_of(pack, GAIN_ONE), scatter.total(own[...])
    )
    small_ref[0:1, :] = gain_grad
    small_ref[2:3, :] = bias_grad
    dx_ref[...] = (dafter[...] + back).astype(BF16)
    if scatters:
        up.close()
    if carried:
        for rest in rests:
            rest.step(0)
        mid.step(2)
        units = grad_in.shape[0]
        dafter[2 * units :, :] = jnp.where(mine, r.small_in[...], small_ref[...])
        small_copy = push(dafter.at[2 * units :, :], r.small_got, r.core_send, r.core_recv, 0, other)
        dafter[:units, :] = jnp.where(mine, r.grad_in_in[...], grad_in[...])
        dafter[units : 2 * units, :] = jnp.where(mine, r.grad_out_in[...], grad_out[...])
        gate_copy = push(dafter.at[: 2 * units, :], r.gate_got, r.core_send, r.core_recv, 1, other)
        r.trade_stage[0] = jnp.where(mine, r.outs[1][...], r.outs[0][...])
        r.trade_stage[1] = jnp.where(mine, dy_ref[...], dx_ref[...])
        trade = push(r.trade_stage, r.trade_land, r.core_send, r.core_recv, 2, other)
    elif scatters:
        mid.close()
    if carried:
        small_copy.wait_recv()
        r.total[...] = jnp.where(mine, small_ref[...], r.small_in[...]) + r.small_got[...]
        peers = [lax.rem(me + j, groups) for j in range(1, groups)]
        spread = [
            push(r.total.at[:, tile_of(peer, cols)], r.slot_a.at[j], r.last_send.at[0], r.last_recv.at[0], j, {"mp": peer})
            for j, peer in enumerate(peers)
        ]
        for rest in rests:
            rest.step(1)
        mid.close()
        down.finish()
        up.finish()
        mid.finish()

        @pl.when(jnp.logical_not(mine))
        def _():
            for load in other_loads:
                load.wait()

        results = Copies(
            [(down.res, r.down_sum), (up.res, r.up_sum), (mid.res, r.mid_sum)]
            + [(rests[i].res, r.late_sum.at[i]) for i in range(2)],
            r.done_sem,
        )
        results.start(0, 1, 2)
        gate_copy.wait_recv()
        r.gate_sum[:units, :] = jnp.where(mine, grad_in[...], r.grad_in_in[...]) + r.gate_got[:units, :]
        r.gate_sum[units:, :] = jnp.where(mine, grad_out[...], r.grad_out_in[...]) + r.gate_got[units:, :]
        for copy in spread:
            copy.wait_recv()
        r.share[...] = r.total[:, tile_of(me, cols)] + sum(r.slot_a[j] for j in range(groups - 1))
        over_copies = Sum(r.share, r.slot_b, r.last_send.at[1], r.last_recv.at[1], "dp", copies)
        for rest in rests:
            rest.step(2)
        at_me = r.whole.at[:, tile_of(me, cols)]
        at_me[...] = over_copies.finish()
        joined = [
            push(at_me, at_me, r.last_send.at[2], r.last_recv.at[2], j, {"mp": peer}) for j, peer in enumerate(peers)
        ]
        for rest in rests:
            rest.close()
        for piece in rests + lates:
            piece.finish()
        results.start(3, 4)
        for copy in joined:
            copy.wait_recv()
        r.vector_sum[...] = r.whole[...]
        trade.wait_recv()
        r.traded[...] = r.trade_land[...]
        results.finish()
        trade.wait_send()
        small_copy.wait_send()
        gate_copy.wait_send()
        over_copies.drain()
        for copy in spread + joined:
            copy.wait_send()
    gather.drain()
    scatter.drain()
    for one in (sum_one, sum_two, sum_three):
        one.drain()
    saves.finish()
    if scatters and not carried:
        for i, (piece, out) in enumerate([(down, r.down_out), (up, r.up_out), (mid, r.mid_out)]):
            piece.finish()

            @pl.when(lax.axis_index("pipe") == layer)
            def _():
                copy = pltpu.make_async_copy(piece.res, out, r.done_sem.at[i])
                copy.start()
                copy.wait()


def late_parts(bufs, signals, layer, src):
    half = src.shape[1] // 2
    return [
        GradScatter(bufs[3 * i : 3 * i + 3], signals[2 * i : 2 * i + 2], layer, src.at[:, i * half : (i + 1) * half, :])
        for i in range(2)
    ]


BACK_WEIGHTS = (QKV, OUT, UP, DOWN, GATE_IN, GATE_OUT)


def backward_layer(layer, ident, groups, copies, scatters, dy, x, fore, vectors, pooled, own, got, later=None, outs=(), turns=()):
    size, width = dy.shape
    tokens, channels = pooled.shape
    share, ff = own[OUT].shape[0], own[UP].shape[1]
    hidden = own[GATE_IN].shape[0]
    shards = width // TILE
    late_rows = 4 * share
    grads_shape = (shards, late_rows + channels + 2 * ff, TILE)
    late_shape = (shards, late_rows, TILE)
    carried, gathered = later is not None, len(turns) > 0
    own, got = ([w[i] for i in BACK_WEIGHTS] for w in (own, got))
    near_in = dict(
        dy=dy, x=x, after=fore.after, own_vectors=vectors[0], got_vectors=vectors[1], pooled=pooled, gate=fore.gate
    )
    far_in = dict(saved=fore.saved, own_weights=own, got_weights=got)
    near_out = dict(dx=((size, width), BF16))
    far_out = {}
    rows = dict(small=((16, width), F32), grad_in=((hidden, width), F32), grad_out=((hidden, width), F32))
    signals = [pltpu.SemaphoreType.DMA((8,)) for _ in range(2)]
    halves, mids = ((2, ff // 2, TILE), BF16), ((2, channels // 2, TILE), BF16)
    scratch = dict(
        held=[pltpu.VMEM(s.shape, s.dtype) for s in fore.saved],
        weights=[pltpu.VMEM(w.shape, BF16) for w in own],
        bufs=scatter_scratch(size, width),
        own=pltpu.VMEM((size, width), F32),
        pack=pltpu.VMEM((16, width), F32),
        dyf=pltpu.VMEM((tokens, width), BF16),
        daf=pltpu.VMEM((tokens, width), BF16),
        dmixed=pltpu.VMEM((tokens, share), BF16),
        dqkv=pltpu.VMEM((tokens, 3 * share), BF16),
        dafter=pltpu.VMEM((size, width), F32),
        grads=pltpu.VMEM(grads_shape, BF16),
        load_sem=pltpu.SemaphoreType.DMA((6,)),
        saved_sem=pltpu.SemaphoreType.DMA((9,)),
        save_sem=pltpu.SemaphoreType.DMA((1,)),
        ag_send=pltpu.SemaphoreType.DMA((2, 6)),
        ag_recv=pltpu.SemaphoreType.DMA((2, 6)),
        rs_send=pltpu.SemaphoreType.DMA((2, 6)),
        rs_recv=pltpu.SemaphoreType.DMA((2, 6)),
        **sum_scratch(groups, copies, width),
    )
    if scatters:
        scratch |= dict(
            down=grad_scratch(shards, ff, TILE),
            down_sem=signals,
            up=grad_scratch(shards, ff, TILE),
            up_sem=signals,
            mid=grad_scratch(shards, channels, TILE),
            mid_sem=signals,
        )
    if carried:
        near_in |= dict(small_in=later.small, grad_in_in=later.grad_in, grad_out_in=later.grad_out, outs=outs)
        far_in |= dict(late_in=later.late_out, down_in=later.down_out, up_in=later.up_out, mid_in=later.mid_out)
        near_out |= dict(
            vector_sum=((16, width), F32), gate_sum=((2 * hidden, width), F32), traded=((2, size, width), BF16)
        )
        far_out |= dict(down_sum=halves, up_sum=halves, mid_sum=mids, late_sum=((2, 2, late_rows // 4, TILE), BF16))
        scratch |= {name: pltpu.VMEM(*shape) for name, shape in rows.items()}
        most = max(groups, copies) - 1
        scratch |= dict(
            late=grad_scratch(shards, late_rows // 2, TILE) + grad_scratch(shards, late_rows // 2, TILE),
            late_sems=signals + signals,
            rest_sems=signals + signals,
            late_held=pltpu.VMEM(late_shape, BF16),
            late_sem=pltpu.SemaphoreType.DMA((4,)),
            done_sem=pltpu.SemaphoreType.DMA((5,)),
            small_got=pltpu.VMEM((16, width), F32),
            gate_got=pltpu.VMEM((2 * hidden, width), F32),
            trade_stage=pltpu.VMEM((2, size, width), BF16),
            trade_land=pltpu.VMEM((2, size, width), BF16),
            total=pltpu.VMEM((16, width), F32),
            share=pltpu.VMEM((16, TILE), F32),
            whole=pltpu.VMEM((16, width), F32),
            slot_a=pltpu.VMEM((groups - 1, 16, TILE), F32),
            slot_b=pltpu.VMEM((copies - 1, 16, TILE), F32),
            core_send=pltpu.SemaphoreType.DMA((3,)),
            core_recv=pltpu.SemaphoreType.DMA((3,)),
            last_send=pltpu.SemaphoreType.DMA((3, most)),
            last_recv=pltpu.SemaphoreType.DMA((3, most)),
        )
    else:
        near_out |= rows
        if scatters:
            far_out |= dict(late_out=(late_shape, BF16), down_out=halves, up_out=halves, mid_out=mids)
            scratch |= dict(done_sem=pltpu.SemaphoreType.DMA((3,)))
        else:
            far_out |= dict(grads_out=(grads_shape, BF16))
    if gathered:
        far_in |= dict(turns=turns)
        scratch |= dict(turn_sem=pltpu.SemaphoreType.DMA((2,)))
    return launch(
        functools.partial(backward_kernel, layer, groups, copies, scatters, carried, gathered),
        "layer_backward",
        ident,
        near_in,
        far_in,
        near_out,
        far_out,
        scratch,
        40_000_000_000,
    )


def results_kernel(share, r):
    core = lax.axis_index("pipe")
    ahead = r.flag[...] > 0.0
    for result, mine, got in ((r.layer_out, r.outs, r.traded[0]), (r.input_grad, r.grads, r.traded[1])):
        kept = jnp.where(core == 0, mine[0][...], mine[1][...])
        result[0] = jnp.where(ahead, kept, got)
        result[1] = jnp.where(ahead, got, kept)
    sums = r.vector_sum
    r.gain_grad[...] = sums[0:2, :]
    r.shift_grad[...] = sums[2:4, :]
    for k in range(9):
        r.depth_grad[k] = sums[4 + k : 5 + k, :]
    r.bias_grad[...] = sums[13:14, :]
    units = r.gate_in_grad.shape[0]
    r.gate_in_grad[...] = r.gate_sum[:units, :]
    r.gate_out_grad[...] = r.gate_sum[units:, :]
    half, cols = r.down_sum.shape[1:]
    for k in range(2):
        r.down_grad[k * half : (k + 1) * half, :] = r.down_sum[k].astype(F32)
        for t in range(half // cols):
            lanes = slice((k * (half // cols) + t) * cols, (k * (half // cols) + t + 1) * cols)
            r.up_grad[:, lanes] = r.up_sum[k, t * cols : (t + 1) * cols, :].astype(F32)
    part = r.late_sum.shape[2]

    def put(base, count, store):
        at = base
        while at < base + count:
            stop = min(base + count, (at // part + 1) * part)
            line = at % part
            rows = r.late_sum[at // (2 * part), at // part % 2, line : line + stop - at, :]
            store(slice(at - base, stop - base), rows.astype(F32))
            at = stop

    def store_qkv(k, lines, rows):
        r.qkv_grad[k, lines, :] = rows

    def store_out(lines, rows):
        r.out_grad[lines, :] = rows

    for k in range(3):
        put(k * cols, cols, functools.partial(store_qkv, k))
    put(3 * share, share, store_out)
    half = r.mid_sum.shape[1]
    for k in range(2):
        r.conv_grad[k * half : (k + 1) * half, :] = r.mid_sum[k].astype(F32)


def results(flag, outs, grads, last, share, channels):
    size, width = outs[0].shape
    cols = last.down_sum.shape[2]
    ff = 2 * last.down_sum.shape[1]
    hidden = last.gate_sum.shape[0] // 2
    return launch(
        functools.partial(results_kernel, share),
        "results",
        None,
        dict(
            flag=flag,
            outs=outs,
            grads=grads,
            traded=last.traded,
            vector_sum=last.vector_sum,
            gate_sum=last.gate_sum,
            down_sum=last.down_sum,
            up_sum=last.up_sum,
            mid_sum=last.mid_sum,
            late_sum=last.late_sum,
        ),
        {},
        dict(
            layer_out=((2, size, width), BF16),
            input_grad=((2, size, width), BF16),
            gain_grad=((2, width), F32),
            shift_grad=((2, width), F32),
            qkv_grad=((3, cols, share), F32),
            out_grad=((share, cols), F32),
            up_grad=((cols, ff), F32),
            down_grad=((ff, cols), F32),
            conv_grad=((channels, cols), F32),
            depth_grad=((9, 1, width), F32),
            bias_grad=((1, width), F32),
            gate_in_grad=((hidden, width), F32),
            gate_out_grad=((hidden, width), F32),
        ),
        {},
        {},
        1_000_000,
    )


def pool_weights(side, count, offset):
    rows_index = jnp.arange(GRID, dtype=jnp.int32)[:, None]
    cols_index = jnp.arange(count, dtype=jnp.int32)[None, :] + offset
    lower = rows_index * side // GRID
    upper = ((rows_index + 1) * side + GRID - 1) // GRID
    inside = (cols_index >= lower) & (cols_index < upper)
    return jnp.where(inside, 1.0 / (upper - lower).astype(F32), 0.0)


def pool_partial(feature, pixels, row_start):
    side = pixels * GRID // 768
    row_matrix = pool_weights(side, feature.shape[0], row_start)
    col_matrix = pool_weights(side, feature.shape[1], 0)
    first = jnp.einsum("ia,abc->ibc", row_matrix.astype(BF16), feature, preferred_element_type=F32)
    high = lax.reduce_precision(first, 8, 7)
    both = [part.astype(BF16) for part in (high, first - high)]
    col_low = col_matrix.astype(BF16)
    second = sum(jnp.einsum("jb,ibc->ijc", col_low, part, preferred_element_type=F32) for part in both)
    return second.reshape(GRID * GRID, feature.shape[2])


def per_device(
    inputs, cotangent, highres, resolution, assign, norm_gain, norm_bias, qkv_weight, out_weight, up_weight,
    down_weight, conv_weight, depth_weight, depth_bias, gate_in, gate_out,
):
    section = lax.axis_index("pipe")
    groups, copies = lax.axis_size("mp"), lax.axis_size("dp")
    first_half = section == 0
    order = assign[0]
    slot = order[section]

    def swap(block):
        return lax.ppermute(block, "pipe", SWAP)

    width = inputs.shape[2]
    share, channels, ff = out_weight.shape[1], conv_weight.shape[1], up_weight.shape[2]
    own_vectors = [depth_weight.transpose(1, 0, 2), depth_bias, norm_gain[0], norm_bias[0]]
    vectors = (own_vectors, [swap(v) for v in own_vectors])
    own = [
        qkv_weight[0].transpose(1, 0, 2), out_weight[0], up_weight[0], down_weight[0], conv_weight[0],
        gate_in[0], gate_out[0],
    ]
    row_start = section * highres.shape[1]
    parts = jax.vmap(pool_partial, in_axes=(0, 0, None))(highres, resolution, row_start).astype(BF16)
    flag = jnp.broadcast_to(jnp.where(slot == 0, 1.0, 0.0).astype(F32), (1, width))

    feed = types.SimpleNamespace(flag=flag, images=inputs, cotangents=cotangent, parts=parts)
    fore0 = forward_layer(0, 0, groups, copies, feed, vectors, own)
    pooled, got = fore0.pooled, fore0.got_weights
    feed = types.SimpleNamespace(x=fore0.out, cot=fore0.cot, pooled=pooled, got_weights=got)
    fore1 = forward_layer(1, 1, groups, copies, feed, vectors, own)
    scatters = copies == groups == 4 and width // TILE == copies and inputs.shape[1] == 2 * gate_in.shape[1] + 16
    outs = [fore0.out, fore1.out]
    back1 = backward_layer(
        1, 2, groups, copies, scatters, fore0.cot, fore0.out, fore1, vectors, pooled, own, got,
        turns=[fore0.turn_out, fore1.turn_out],
    )
    back0 = backward_layer(
        0, 3, groups, copies, scatters, back1.dx, fore0.x, fore0, vectors, pooled, own, got,
        back1 if scatters else None, outs,
    )
    if scatters:
        last = results(flag, outs, [back0.dx, back1.dx], back0, share, channels)
        return (
            last.layer_out[None],
            last.input_grad[None],
            last.gain_grad[None],
            last.shift_grad[None],
            last.qkv_grad.transpose(1, 0, 2)[None],
            last.out_grad[None],
            last.up_grad[None],
            last.down_grad[None],
            last.conv_grad[None],
            last.depth_grad.transpose(1, 0, 2),
            last.bias_grad,
            last.gate_in_grad[None],
            last.gate_out_grad[None],
        )

    def owned(first, second):
        kept = jnp.where(first_half, first, second)
        return kept, swap(jnp.where(first_half, second, first))

    def by_image(first, second):
        kept, received = owned(first, second)
        return jnp.where(slot == 0, jnp.stack([kept, received]), jnp.stack([received, kept]))[None]

    layer_out, input_grad = by_image(*outs), by_image(back0.dx, back1.dx)
    cols, blocks = width // copies, width // TILE
    ends = [3 * share, 4 * share, 4 * share + channels, 4 * share + channels + ff]

    def cores_sum(first, second, kind):
        kept, received = owned(first, second)
        return (kept.astype(F32) + received.astype(F32)).astype(kind)

    def scattered(blocked, dim):
        return lax.psum_scatter(blocked, "dp", scatter_dimension=dim, tiled=True).astype(F32)

    def by_rows(block):
        tiles = block.reshape(blocks, block.shape[1] // TILE, TILE, TILE)
        return scattered(tiles.transpose(0, 2, 1, 3).reshape(width, block.shape[1]), 0)

    def by_cols(block):
        return scattered(block.transpose(1, 0, 2).reshape(block.shape[1], width), 1)

    whole = cores_sum(back0.grads_out, back1.grads_out, BF16)
    small = lax.psum(cores_sum(back0.small, back1.small, F32), ("dp", "mp"))
    return (
        layer_out,
        input_grad,
        small[0:2][None],
        small[2:4][None],
        by_rows(whole[:, : ends[0]]).reshape(cols, 3, share)[None],
        by_cols(whole[:, ends[0] : ends[1]])[None],
        by_rows(whole[:, ends[2] : ends[3]])[None],
        by_cols(whole[:, ends[3] :])[None],
        by_cols(whole[:, ends[1] : ends[2]])[None],
        small[4:13][None],
        small[13][None],
        cores_sum(back0.grad_in, back1.grad_in, F32)[None],
        cores_sum(back0.grad_out, back1.grad_out, F32)[None],
    )


def solution(mesh):
    return jax.shard_map(
        per_device,
        mesh=mesh,
        in_specs=(
            P("dp", "mp", None),
            P("dp", "mp", None),
            P("dp", "pipe", None, "mp"),
            P("dp"),
            P("dp", None),
            P("pipe", None, None),
            P("pipe", None, None),
            P("pipe", None, None, "mp"),
            P("pipe", "mp", None),
            P("pipe", None, "mp"),
            P("pipe", "mp", None),
            P("pipe", "mp", None),
            P("pipe", None, None),
            P("pipe", None),
            P("pipe", "mp", None),
            P("pipe", "mp", None),
        ),
        out_specs=(
            P("pipe", "dp", "mp", None),
            P("pipe", "dp", "mp", None),
            P("pipe", None, None),
            P("pipe", None, None),
            P("pipe", "dp", None, "mp"),
            P("pipe", "mp", "dp"),
            P("pipe", "dp", "mp"),
            P("pipe", "mp", "dp"),
            P("pipe", "mp", "dp"),
            P("pipe", None, None),
            P("pipe", None),
            P("pipe", "mp", None),
            P("pipe", "mp", None),
        ),
        check_vma=False,
    )
```
